32 devices in a mesh: seq: 4 (over y, x), head: 4 (over z), dp: 2 (over core).
Axes of the slice: x: 2, y: 2, z: 4, core: 2. Of those that a mesh axis runs over, the one named last changes fastest.
Arguments:
- query_heads: bfloat16 [2, 1024, 4096], P('dp', 'seq', 'head'), may hold values from -100 to 100
- key_heads: bfloat16 [2, 1024, 4096], P('dp', 'seq', 'head'), may hold values from -100 to 100
- value_heads: bfloat16 [2, 1024, 4096], P('dp', 'seq', 'head'), may hold values from -6 to 6
- query_gain: float32 [4096], P('head'), may hold values from 0.5 to 1.5
- key_gain: float32 [4096], P('head'), may hold values from 0.5 to 1.5
- key_squeeze: bfloat16 [32, 512, 128], P('head'), may hold values from -0.25 to 0.25
- value_squeeze: bfloat16 [32, 512, 128], P('head'), may hold values from -0.25 to 0.25
- grad_out: bfloat16 [2, 1024, 4096], P('dp', 'seq', 'head'), may hold values from -6 to 6
Outputs:
- grad_query: bfloat16 [2, 1024, 4096], P('dp', 'seq', 'head')
- grad_key: bfloat16 [2, 1024, 4096], P('dp', 'seq', 'head')
- grad_value: bfloat16 [2, 1024, 4096], P('dp', 'seq', 'head')
- grad_query_gain: float32 [4096], P('head')
- grad_key_gain: float32 [4096], P('head')
- grad_key_squeeze: float32 [32, 512, 128], P('head')
- grad_value_squeeze: float32 [32, 512, 128], P('head')
The draws below stay inside these ranges and needn't reach their ends.
All inputs are finite; a program needn't handle non-finite values.
Results may differ from the reference program's by a relative error of at most 0.025.
Values may be sent and summed in bfloat16 or wider, within the bound.
No kernel may reach another device: no remote copies, remote signals or barrier semaphores. Data moves between devices by JAX's collectives and lax.ppermute only.
A program may use at most 64 MiB of HBM per device.

```python
import jax
import jax.numpy as jnp
from jax import lax

H = 32
HD = 128
KS = 4
S_DEV = 256
HH = 4096
L = 1024
BATCH = 2
SLOTS = 64
NMEM = 256
N_SEQ = 4


def drawn_pair(key):
    base = jax.random.fold_in(key, 811)
    streams = jax.random.split(base, 12)
    columns = jnp.arange(HH)
    rise = 3.0
    tilt = rise ** (columns / (HH - 1.0)) / jnp.sqrt(rise)

    def scaled(first, second, third):
        noise = jax.random.truncated_normal(streams[first], -3.0, 3.0, (BATCH, L, HH), jnp.float32)
        row_scale = jnp.exp(jax.random.uniform(streams[second], (BATCH, L, 1), jnp.float32, jnp.log(0.3), jnp.log(3.0)))
        col_scale = jnp.exp(jax.random.uniform(streams[third], (HH,), jnp.float32, jnp.log(0.3), jnp.log(3.0)))
        return (noise, noise * row_scale * col_scale * tilt)
    noise_q, queries = scaled(0, 1, 2)
    noise_k, keyset = scaled(3, 4, 5)
    return (queries, keyset)


def draw_query_heads(key, part):
    return drawn_pair(key)[0].astype(jnp.bfloat16)


def draw_key_heads(key, part):
    return drawn_pair(key)[1].astype(jnp.bfloat16)


def shard_levels(rng, shape, cuts, low, largest):
    level = 1.0
    for dim, shards_of in cuts:
        heights = jax.random.uniform(jax.random.fold_in(jax.random.fold_in(rng, 6), dim), (shards_of,), jnp.float32, low / len(cuts), largest / len(cuts))
        level = level * jnp.repeat(jnp.exp(heights), shape[dim] // shards_of).reshape((-1,) + (1,) * (len(shape) - 1 - dim))
    return level


def scatter_about(own_key, dims, spread, limit, cuts=(), kind=jnp.bfloat16):
    result = jax.random.normal(own_key, dims, jnp.float32) * spread
    if len(cuts) > 0:
        result = shard_levels(own_key, dims, cuts, -0.22, 0.18) * result
    return jnp.clip(result, min=-limit, max=limit).astype(kind)


def setup_inputs(seed: int = 0) -> dict:
    key_list = jax.random.split(jax.random.key(seed), 9)
    return {
        "query_heads": draw_query_heads(jax.random.fold_in(key_list[8], 71), 0),
        "key_heads": draw_key_heads(jax.random.fold_in(key_list[8], 71), 0),
        "value_heads": scatter_about(key_list[2], (BATCH, L, HH), 1.0, 6.0, ((0, 2), (1, 4), (2, 4))),
        "query_gain": jnp.clip(1.0 + 0.1 * jax.random.normal(key_list[3], (HH,), jnp.float32), 0.5, 1.5),
        "key_gain": jnp.clip(1.0 + 0.1 * jax.random.normal(key_list[4], (HH,), jnp.float32), 0.5, 1.5),
        "key_squeeze": scatter_about(key_list[5], (H, KS * HD, HD), (KS * HD) ** -0.5, 0.25, ((0, 4),)),
        "value_squeeze": scatter_about(key_list[6], (H, KS * HD, HD), (KS * HD) ** -0.5, 0.25, ((0, 4),)),
        "grad_out": scatter_about(key_list[7], (BATCH, L, HH), 1.0, 6.0, ((0, 2), (1, 4), (2, 4))),
    }


EPSILON = 1e-06

def to_half(source):
    return lax.optimization_barrier(source.astype(jnp.bfloat16)).astype(jnp.float32)

def normalize(source, gain):
    full = source.astype(jnp.float32)
    inverse = lax.rsqrt(lax.optimization_barrier(jnp.sum(full * full, -1, keepdims=True)) / HH + EPSILON)
    return (full, inverse, (full * inverse * gain).astype(jnp.bfloat16))

def unfold_slots(source):
    return source.reshape(BATCH, NMEM, KS, H, HD).transpose(0, 1, 3, 2, 4).reshape(BATCH, NMEM, H, KS * HD)

def fold_slots(source):
    return source.reshape(BATCH, NMEM, H, KS, HD).transpose(0, 1, 3, 2, 4).reshape(BATCH, L, HH)

def compress(unfolded, weight):
    return jnp.einsum('bmhc,hcd->bmhd', unfolded.astype(jnp.float32), weight.astype(jnp.float32)).astype(jnp.bfloat16)

def sequence_grads(queries, key_rows, value_rows, cotangent, mem_keys, mem_values):
    score_scale = HD ** (-0.5)
    positions = jnp.arange(S_DEV, dtype=jnp.int32)
    causal = positions[:, None] >= positions[None, :]
    slot_ids = jnp.arange(NMEM, dtype=jnp.int32)
    keys_mem = mem_keys.astype(jnp.float32)
    values_mem = mem_values.astype(jnp.float32)

    def shard_step(carry, index):
        first_row = index * S_DEV
        query_blk = lax.dynamic_slice_in_dim(queries, first_row, S_DEV, 0).astype(jnp.float32)
        key_blk = lax.dynamic_slice_in_dim(key_rows, first_row, S_DEV, 0).astype(jnp.float32)
        value_blk = lax.dynamic_slice_in_dim(value_rows, first_row, S_DEV, 0).astype(jnp.float32)
        grad_blk = lax.dynamic_slice_in_dim(cotangent, first_row, S_DEV, 0).astype(jnp.float32)
        keys_all = jnp.concatenate([key_blk, keys_mem], 0)
        values_all = jnp.concatenate([value_blk, values_mem], 0)
        scores = jnp.einsum('thd,uhd->htu', query_blk, keys_all) * score_scale
        earlier = jnp.broadcast_to(slot_ids[None, :] < index * SLOTS, (S_DEV, NMEM))
        allowed = jnp.concatenate([causal, earlier], 1)
        scores = jnp.where(allowed[None], scores, -jnp.inf)
        peak = lax.optimization_barrier(jnp.max(scores, -1, keepdims=True))
        log_mass = peak + jnp.log(lax.optimization_barrier(jnp.sum(jnp.exp(scores - peak), -1, keepdims=True)))
        attend = jnp.exp(scores - log_mass)
        grads = jnp.einsum('thd,uhd->htu', grad_blk, values_all)
        row_delta = lax.optimization_barrier(jnp.sum(attend * grads, -1, keepdims=True))
        d_scores = to_half(attend * (grads - row_delta))
        grad_q = score_scale * jnp.einsum('htu,uhd->thd', d_scores, keys_all)
        grad_keys = score_scale * jnp.einsum('htu,thd->uhd', d_scores, query_blk)
        grad_values = jnp.einsum('htu,thd->uhd', to_half(attend), grad_blk)
        sum_k, sum_v = carry
        carry = (sum_k + to_half(grad_keys[S_DEV:]), sum_v + to_half(grad_values[S_DEV:]))
        return (carry, (grad_q, grad_keys[:S_DEV], grad_values[:S_DEV]))
    zeros = jnp.zeros((NMEM, H, HD), jnp.float32)
    sums, per_shard = lax.scan(shard_step, (zeros, zeros), jnp.arange(N_SEQ, dtype=jnp.int32))
    flat = tuple((stacked.reshape(L, HH) for stacked in per_shard))
    return (sums, flat)

def reference(query_heads, key_heads, value_heads, query_gain, key_gain, key_squeeze, value_squeeze, grad_out):
    q_full, inv_q, q_norm = normalize(query_heads, query_gain)
    k_full, inv_k, k_norm = normalize(key_heads, key_gain)
    k_unf = unfold_slots(k_norm)
    v_unf = unfold_slots(value_heads)
    mem_k = compress(k_unf, key_squeeze)
    mem_v = compress(v_unf, value_squeeze)
    results = []
    for member in range(BATCH):
        results.append(sequence_grads(q_norm[member].reshape(L, H, HD), k_norm[member].reshape(L, H, HD), value_heads[member].reshape(L, H, HD), grad_out[member].reshape(L, H, HD), mem_k[member], mem_v[member]))
    grad_mem_k = jnp.stack([item[0][0] for item in results]).astype(jnp.bfloat16)
    grad_mem_v = jnp.stack([item[0][1] for item in results]).astype(jnp.bfloat16)
    grad_qn = jnp.stack([item[1][0] for item in results])
    grad_kn_local = jnp.stack([item[1][1] for item in results])
    grad_v_local = jnp.stack([item[1][2] for item in results])
    grad_key_squeeze = jnp.einsum('bmhc,bmhd->hcd', k_unf.astype(jnp.float32), grad_mem_k.astype(jnp.float32))
    grad_value_squeeze = jnp.einsum('bmhc,bmhd->hcd', v_unf.astype(jnp.float32), grad_mem_v.astype(jnp.float32))
    back_k = fold_slots(jnp.einsum('bmhd,hcd->bmhc', grad_mem_k.astype(jnp.float32), key_squeeze.astype(jnp.float32)))
    back_v = fold_slots(jnp.einsum('bmhd,hcd->bmhc', grad_mem_v.astype(jnp.float32), value_squeeze.astype(jnp.float32)))
    grad_kn = grad_kn_local + back_k
    grad_value = (grad_v_local + back_v).astype(jnp.bfloat16)
    grad_query_gain = lax.optimization_barrier(jnp.sum(grad_qn * q_full * inv_q, (0, 1)))
    grad_key_gain = lax.optimization_barrier(jnp.sum(grad_kn * k_full * inv_k, (0, 1)))
    dot_q = lax.optimization_barrier(jnp.sum(query_gain * grad_qn * q_full, -1, keepdims=True))
    dot_k = lax.optimization_barrier(jnp.sum(key_gain * grad_kn * k_full, -1, keepdims=True))
    grad_query = (inv_q * query_gain * grad_qn - q_full * inv_q ** 3 * dot_q / HH).astype(jnp.bfloat16)
    grad_key = (inv_k * key_gain * grad_kn - k_full * inv_k ** 3 * dot_k / HH).astype(jnp.bfloat16)
    return (grad_query, grad_key, grad_value, grad_query_gain, grad_key_gain, grad_key_squeeze, grad_value_squeeze)
```

```python
import jax
import jax.numpy as jnp
from jax import lax
from jax.experimental import pallas as pl
from jax.experimental.pallas import tpu as pltpu
from jax.sharding import PartitionSpec as P

HD = 128
KS = 4
HH = 4096


epsilon = 1e-06


def unfold_slots(source, head_count):
    batch_size, row_count, widths = source.shape
    return (
        source.reshape(batch_size, row_count // KS, KS, head_count, HD)
        .transpose(0, 1, 3, 2, 4)
        .reshape(batch_size, row_count // KS, head_count, KS * HD)
    )


def fold_slots(source):
    batch_size, slot_count, head_count, spans = source.shape
    return (
        source.reshape(batch_size, slot_count, head_count, KS, HD)
        .transpose(0, 1, 3, 2, 4)
        .reshape(batch_size, slot_count * KS, head_count * HD)
    )


def on_device_any(
    query_heads, key_heads, value_heads, query_gain, key_gain, key_squeeze, value_squeeze, grad_out
):
    batch_size, row_count, widths = query_heads.shape
    head_count = widths // HD
    slot_count = row_count // KS
    score_scale = HD ** (-0.5)
    own_limit = lax.axis_index("seq") * slot_count
    q_full = query_heads.astype(jnp.float32)
    k_full = key_heads.astype(jnp.float32)
    sum_q, sum_k = lax.psum((jnp.sum(q_full * q_full, -1), jnp.sum(k_full * k_full, -1)), "head")
    inv_q = lax.rsqrt(sum_q / HH + epsilon)[..., None]
    inv_k = lax.rsqrt(sum_k / HH + epsilon)[..., None]
    q_norm = (q_full * inv_q * query_gain).astype(jnp.bfloat16)
    k_norm = (k_full * inv_k * key_gain).astype(jnp.bfloat16)
    k_unf = unfold_slots(k_norm, head_count)
    v_unf = unfold_slots(value_heads, head_count)
    mem_k = (
        jnp.einsum("bmhc,hcd->bmhd", k_unf, key_squeeze, preferred_element_type=jnp.float32)
        .astype(jnp.bfloat16)
        .reshape(batch_size, slot_count, widths)
    )
    mem_v = (
        jnp.einsum("bmhc,hcd->bmhd", v_unf, value_squeeze, preferred_element_type=jnp.float32)
        .astype(jnp.bfloat16)
        .reshape(batch_size, slot_count, widths)
    )
    queries = q_norm.reshape(batch_size, row_count, head_count, HD)
    key_loc = k_norm.reshape(batch_size, row_count, head_count, HD)
    value_loc = value_heads.reshape(batch_size, row_count, head_count, HD)
    cotangent = grad_out.reshape(batch_size, row_count, head_count, HD)
    positions = jnp.arange(row_count)
    causal = positions[:, None] >= positions[None, :]
    scores_loc = jnp.where(
        causal,
        jnp.einsum("bthd,buhd->bhtu", queries, key_loc, preferred_element_type=jnp.float32)
        * score_scale,
        -jnp.inf,
    )
    grads_loc = jnp.einsum(
        "bthd,buhd->bhtu", cotangent, value_loc, preferred_element_type=jnp.float32
    )
    all_k, all_v = (
        lax.all_gather(mem_k, "seq", axis=1, tiled=True),
        lax.all_gather(mem_v, "seq", axis=1, tiled=True),
    )
    piece_rows = all_k.shape[1]
    key_rows = all_k.reshape(batch_size, piece_rows, head_count, HD)
    value_rows = all_v.reshape(batch_size, piece_rows, head_count, HD)
    allowed = jnp.arange(piece_rows) < own_limit
    scores = jnp.where(
        allowed,
        jnp.einsum("bthd,buhd->bhtu", queries, key_rows, preferred_element_type=jnp.float32)
        * score_scale,
        -jnp.inf,
    )
    gradients = jnp.einsum(
        "bthd,buhd->bhtu", cotangent, value_rows, preferred_element_type=jnp.float32
    )
    key_rows, scores_mem, grads_mem = (key_rows, scores, gradients)
    peak = jnp.maximum(jnp.max(scores_loc, -1), jnp.max(scores_mem, -1))
    summed = jnp.sum(jnp.exp(scores_loc - peak[..., None]), -1) + jnp.sum(
        jnp.exp(scores_mem - peak[..., None]), -1
    )
    log_mass = peak + jnp.log(summed)
    row_delta = jnp.sum(jnp.exp(scores_loc - log_mass[..., None]) * grads_loc, -1) + jnp.sum(
        jnp.exp(scores_mem - log_mass[..., None]) * grads_mem, -1
    )
    piece_rows = key_rows.shape[1]
    attend = jnp.exp(scores_mem - log_mass[..., None])
    d_scores = (attend * (grads_mem - row_delta[..., None])).astype(jnp.bfloat16)
    grad_q = score_scale * jnp.einsum(
        "bhtu,buhd->bthd", d_scores, key_rows, preferred_element_type=jnp.float32
    )
    grad_k = score_scale * jnp.einsum(
        "bhtu,bthd->buhd", d_scores, queries, preferred_element_type=jnp.float32
    )
    grad_v = jnp.einsum(
        "bhtu,bthd->buhd",
        attend.astype(jnp.bfloat16),
        cotangent,
        preferred_element_type=jnp.float32,
    )
    stacked = jnp.stack(
        (
            grad_k.reshape(batch_size, piece_rows, widths),
            grad_v.reshape(batch_size, piece_rows, widths),
        )
    )
    attend_loc = jnp.exp(scores_loc - log_mass[..., None])
    d_loc = (attend_loc * (grads_loc - row_delta[..., None])).astype(jnp.bfloat16)
    grad_qn = (
        score_scale
        * jnp.einsum("bhtu,buhd->bthd", d_loc, key_loc, preferred_element_type=jnp.float32)
        + grad_q
    ).reshape(batch_size, row_count, widths)
    grad_kn_local = score_scale * jnp.einsum(
        "bhtu,bthd->buhd", d_loc, queries, preferred_element_type=jnp.float32
    )
    grad_v_local = jnp.einsum(
        "bhtu,bthd->buhd",
        attend_loc.astype(jnp.bfloat16),
        cotangent,
        preferred_element_type=jnp.float32,
    )
    mine = lax.psum_scatter(stacked.astype(jnp.bfloat16), "seq", scatter_dimension=2, tiled=True)
    grad_mem_k = mine[0].reshape(batch_size, slot_count, head_count, HD)
    grad_mem_v = mine[1].reshape(batch_size, slot_count, head_count, HD)
    squeeze_k_part = jnp.einsum(
        "bmhc,bmhd->hcd", k_unf, grad_mem_k, preferred_element_type=jnp.float32
    )
    squeeze_v_part = jnp.einsum(
        "bmhc,bmhd->hcd", v_unf, grad_mem_v, preferred_element_type=jnp.float32
    )
    back_k = fold_slots(
        jnp.einsum("bmhd,hcd->bmhc", grad_mem_k, key_squeeze, preferred_element_type=jnp.float32)
    )
    back_v = fold_slots(
        jnp.einsum("bmhd,hcd->bmhc", grad_mem_v, value_squeeze, preferred_element_type=jnp.float32)
    )
    grad_kn = grad_kn_local.reshape(batch_size, row_count, widths) + back_k
    grad_value = (grad_v_local.reshape(batch_size, row_count, widths) + back_v).astype(jnp.bfloat16)
    dot_q, dot_k = lax.psum(
        (jnp.sum(query_gain * grad_qn * q_full, -1), jnp.sum(key_gain * grad_kn * k_full, -1)),
        "head",
    )
    grad_query = (
        inv_q * query_gain * grad_qn - q_full * inv_q**3 * dot_q[..., None] / HH
    ).astype(jnp.bfloat16)
    grad_key = (inv_k * key_gain * grad_kn - k_full * inv_k**3 * dot_k[..., None] / HH).astype(
        jnp.bfloat16
    )
    gain_q_part = jnp.sum(grad_qn * q_full * inv_q, (0, 1))
    gain_k_part = jnp.sum(grad_kn * k_full * inv_k, (0, 1))
    grad_query_gain, grad_key_gain, grad_key_squeeze, grad_value_squeeze = (
        lax.psum(gain_q_part.astype(jnp.bfloat16), ("seq", "dp")).astype(jnp.float32),
        lax.psum(gain_k_part.astype(jnp.bfloat16), ("seq", "dp")).astype(jnp.float32),
        lax.psum(squeeze_k_part.astype(jnp.bfloat16), ("seq", "dp")).astype(jnp.float32),
        lax.psum(squeeze_v_part.astype(jnp.bfloat16), ("seq", "dp")).astype(jnp.float32),
    )
    return (
        grad_query,
        grad_key,
        grad_value,
        grad_query_gain,
        grad_key_gain,
        grad_key_squeeze,
        grad_value_squeeze,
    )


F32 = jnp.float32
BF16 = jnp.bfloat16
NN = (((1,), (0,)), ((), ()))
NT = (((1,), (1,)), ((), ()))
TN = (((0,), (0,)), ((), ()))


def dot(a, b, dims=NN):
    return lax.dot_general(a, b, dims, preferred_element_type=F32)


def sds(shape, dtype):
    return jax.ShapeDtypeStruct(shape, dtype)


def whole_call(body, outs, *ins, cost=1_000_000):
    return pl.pallas_call(
        body,
        out_shape=outs,
        compiler_params=pltpu.CompilerParams(vmem_limit_bytes=40 * 2**20),
        cost_estimate=pl.CostEstimate(flops=cost, bytes_accessed=cost, transcendentals=0),
    )(*ins)


def grid_call(body, steps, outs, in_specs, out_specs, scratch, ids, *ins, cost=1_000_000):
    return pl.pallas_call(
        body,
        out_shape=outs,
        grid_spec=pltpu.PrefetchScalarGridSpec(
            num_scalar_prefetch=1,
            grid=(steps,),
            in_specs=in_specs,
            out_specs=out_specs,
            scratch_shapes=scratch,
        ),
        compiler_params=pltpu.CompilerParams(
            vmem_limit_bytes=40 * 2**20, dimension_semantics=("arbitrary",)
        ),
        cost_estimate=pl.CostEstimate(flops=cost, bytes_accessed=cost, transcendentals=0),
    )(ids, *ins)


def row_order(rows):
    slots = rows // KS
    r = lax.broadcasted_iota(jnp.int32, (rows, rows), 0)
    c = lax.broadcasted_iota(jnp.int32, (rows, rows), 1)
    return jnp.where(c == KS * (r % slots) + r // slots, 1.0, 0.0).astype(BF16)


def row_order_back(rows):
    slots = rows // KS
    r = lax.broadcasted_iota(jnp.int32, (rows, rows), 0)
    c = lax.broadcasted_iota(jnp.int32, (rows, rows), 1)
    return jnp.where(r == KS * (c % slots) + c // slots, 1.0, 0.0).astype(BF16)


def causal_t(rows):
    slots = rows // KS
    u = lax.broadcasted_iota(jnp.int32, (rows, rows), 0)
    t = lax.broadcasted_iota(jnp.int32, (rows, rows), 1)
    return KS * (u % slots) + u // slots <= t


def fold_lanes(x):
    total = x[:, :HD]
    for i in range(1, x.shape[1] // HD):
        total = total + x[:, i * HD : (i + 1) * HD]
    return total


def lane_sum_row(x):
    return jnp.sum(x.T, axis=0, keepdims=True)


def as_columns(rows):
    pad = jnp.zeros((8 - rows.shape[0], rows.shape[1]), F32)
    return jnp.concatenate([rows, pad], axis=0).T


def on_device(
    query_heads, key_heads, value_heads, query_gain, key_gain, key_squeeze, value_squeeze, grad_out
):
    n_seq, n_head = lax.axis_size("seq"), lax.axis_size("head")
    batch_size, rows, cols = query_heads.shape
    heads = cols // HD
    if batch_size != 1 or n_seq & (n_seq - 1) or heads % n_seq or lax.axis_size("dp") != 2:
        return on_device_any(
            query_heads,
            key_heads,
            value_heads,
            query_gain,
            key_gain,
            key_squeeze,
            value_squeeze,
            grad_out,
        )
    slots = rows // KS
    hp = heads // n_seq
    wide = hp * HD
    mem_rows = n_seq * slots
    peers = range(1, n_seq)
    n_mem = (n_seq - 1) * slots
    scale = HD ** (-0.5)
    full_width = cols * n_head
    me = lax.axis_index("seq")
    core = lax.axis_index("dp")
    ids = jnp.stack([me, core]).astype(jnp.int32)

    def to_peers(axis, arrays):
        n = lax.axis_size(axis)
        return [
            lax.ppermute(a, axis, [(i, i ^ k) for i in range(n)])
            for k, a in zip(range(1, n), arrays)
        ]

    def to_core(a):
        return lax.ppermute(a, "dp", [(0, 1), (1, 0)])

    q = query_heads[0]
    k = key_heads[0]
    v = value_heads[0]
    do = grad_out[0]
    qg = query_gain.reshape(1, cols)
    kg = key_gain.reshape(1, cols)
    full = lambda a: pl.BlockSpec(a.shape, lambda i, ids: (0,) * len(a.shape))
    own_cols = pl.BlockSpec((rows, wide), lambda i, ids: (0, i))
    rel_cols = pl.BlockSpec((rows, wide), lambda i, ids: (0, ids[0] ^ i))
    rel_mem = pl.BlockSpec((slots, wide), lambda i, ids: (rows // slots + (ids[0] ^ i), 0))
    own_mem = pl.BlockSpec((slots, wide), lambda i, ids: (rows // slots + i, 0))

    def squares_body(q_ref, k_ref, ss_ref, kp_ref):
        kp = dot(row_order(rows), k_ref[...])
        kp_ref[...] = kp.astype(BF16)
        qf = q_ref[...].astype(F32)
        ss_ref[0:1, :] = lane_sum_row(fold_lanes(qf * qf))
        ss_ref[1:2, :] = lane_sum_row(fold_lanes(kp * kp))

    ss, kp = whole_call(squares_body, (sds((2, rows), F32), sds((rows, cols), BF16)), q, k)
    ss_peers = to_peers("head", [ss] * (n_head - 1))

    def pack_sends(ids_ref, rows_ref, mem_scr, sends):
        for r, send in zip(peers, sends):
            dest = ids_ref[0] ^ r
            send[:rows, :] = rows_ref[:, pl.ds(pl.multiple_of(dest * wide, wide), wide)]
            send[rows:, :] = mem_scr[...]

    def compress(source, w_ref, mem_scr):
        for h in range(heads):
            total = None
            for j in range(KS):
                part = dot(
                    source[j * slots : (j + 1) * slots, h * HD : (h + 1) * HD],
                    w_ref[h, j * HD : (j + 1) * HD, :],
                )
                total = part if total is None else total + part
            block = h // hp
            mem_scr[
                block * slots : (block + 1) * slots, (h % hp) * HD : (h % hp + 1) * HD
            ] = total.astype(BF16)

    def values_body(ids_ref, v_ref, w_ref, vp_ref, *rest):
        sends, mem_scr = rest[:-1], rest[-1]
        vp_ref[...] = dot(row_order(rows), v_ref[...]).astype(BF16)
        compress(vp_ref, w_ref, mem_scr)
        pack_sends(ids_ref, vp_ref, mem_scr, sends)

    packet = sds((rows + mem_rows, wide), BF16)
    smem = pl.BlockSpec(memory_space=pltpu.SMEM)

    def packet_call(body, extra, scalars, *ins):
        outs = extra + (packet,) * (n_seq - 1)
        return pl.pallas_call(
            body,
            out_shape=outs,
            in_specs=[smem] + [pl.BlockSpec(memory_space=pltpu.VMEM)] * len(ins),
            out_specs=tuple(pl.BlockSpec(memory_space=pltpu.VMEM) for _ in outs),
            scratch_shapes=[pltpu.VMEM((mem_rows, wide), BF16)],
            compiler_params=pltpu.CompilerParams(vmem_limit_bytes=40 * 2**20),
            cost_estimate=pl.CostEstimate(
                flops=1_000_000, bytes_accessed=1_000_000, transcendentals=0
            ),
        )(scalars, *ins)

    vp, *v_sends = packet_call(values_body, (sds((rows, cols), BF16),), ids, v, value_squeeze)
    v_recv = to_peers("seq", v_sends)

    def keys_body(ids_ref, q_ref, kp_ref, qg_ref, kg_ref, w_ref, *rest):
        ss_refs = rest[:n_head]
        inv_ref, qn_ref, kn_ref = rest[n_head : n_head + 3]
        sends, mem_scr = rest[n_head + 3 : -1], rest[-1]
        total = ss_refs[0][...]
        for other in ss_refs[1:]:
            total = total + other[...]
        inv = lax.rsqrt(total / full_width + epsilon)
        inv_ref[...] = inv
        inv_c = as_columns(inv)
        qn_ref[...] = (q_ref[...].astype(F32) * inv_c[:, 0:1] * qg_ref[...]).astype(BF16)
        kn_ref[...] = (kp_ref[...].astype(F32) * inv_c[:, 1:2] * kg_ref[...]).astype(BF16)
        compress(kn_ref, w_ref, mem_scr)
        pack_sends(ids_ref, kn_ref, mem_scr, sends)

    inv, qn, kn, *k_sends = packet_call(
        keys_body,
        (sds((2, rows), F32), sds((rows, cols), BF16), sds((rows, cols), BF16)),
        ids, q, kp, qg, kg, key_squeeze, ss, *ss_peers,
    )
    k_recv = to_peers("seq", k_sends)

    def local_body(ids_ref, qn_ref, kn_ref, vp_ref, do_ref, st_ref):
        allowed = causal_t(rows)
        for i in range(hp):
            at = slice(i * HD, (i + 1) * HD)
            s = jnp.where(allowed, dot(kn_ref[:, at], qn_ref[:, at], NT) * scale, -jnp.inf)
            g = dot(vp_ref[:, at], do_ref[:, at], NT)
            m = jnp.max(s, axis=0, keepdims=True)
            p = jnp.exp(s - m)
            st_ref[i, 0:1, :] = m
            st_ref[i, 1:2, :] = jnp.sum(p, axis=0, keepdims=True)
            st_ref[i, 2:3, :] = jnp.sum(p * g, axis=0, keepdims=True)

    (stats,) = grid_call(
        local_body,
        n_seq,
        (sds((heads, 8, rows), F32),),
        [own_cols] * 4,
        (pl.BlockSpec((hp, 8, rows), lambda i, ids: (i, 0, 0)),),
        [],
        ids, qn, kn, vp, do,
    )

    def memory_body(ids_ref, qn_ref, do_ref, st_ref, *rest):
        mk_refs = rest[: n_seq - 1]
        mv_refs = rest[n_seq - 1 : 2 * n_seq - 2]
        st2_ref, ds_ref = rest[2 * n_seq - 2 : 2 * n_seq]
        parts = rest[2 * n_seq :]
        step = pl.program_id(0)
        mine = ids_ref[0]
        for i in range(hp):
            at = slice(i * HD, (i + 1) * HD)
            qn_h = qn_ref[:, at]
            do_h = do_ref[:, at]
            mk = jnp.concatenate([ref[:, at] for ref in mk_refs], axis=0)
            mv = jnp.concatenate([ref[:, at] for ref in mv_refs], axis=0)
            raw = dot(mk, qn_h, NT) * scale
            s = jnp.concatenate(
                [
                    jnp.where((mine ^ r) < mine, raw[(r - 1) * slots : r * slots], -jnp.inf)
                    for r in peers
                ],
                axis=0,
            )
            g = dot(mv, do_h, NT)
            m_loc, l_loc, d_loc = st_ref[i, 0:1, :], st_ref[i, 1:2, :], st_ref[i, 2:3, :]
            m = jnp.maximum(m_loc, jnp.max(s, axis=0, keepdims=True))
            p = jnp.exp(s - m)
            shrink = jnp.exp(m_loc - m)
            mass = l_loc * shrink + jnp.sum(p, axis=0, keepdims=True)
            inv_mass = 1.0 / mass
            delta = (d_loc * shrink + jnp.sum(p * g, axis=0, keepdims=True)) * inv_mass
            st2_ref[i, 0:1, :] = m
            st2_ref[i, 1:2, :] = inv_mass
            st2_ref[i, 2:3, :] = delta
            attend = p * inv_mass
            ds = (attend * (g - delta)).astype(BF16)
            ds_ref[i] = ds
            gk = (dot(ds, qn_h) * scale).astype(BF16)
            gv = dot(attend.astype(BF16), do_h).astype(BF16)
            for r in range(n_seq):
                @pl.when(step == r)
                def _(r=r):
                    parts[r][0, :, at] = gk
                    parts[r][1, :, at] = gv

    part = sds((2, n_mem, wide), BF16)
    rel_stat = pl.BlockSpec((hp, 8, rows), lambda i, ids: (ids[0] ^ i, 0, 0))
    stats2, ds_mem, *parts = grid_call(
        memory_body,
        n_seq,
        (sds((heads, 8, rows), F32), sds((heads, n_mem, rows), BF16)) + (part,) * n_seq,
        [rel_cols, rel_cols, rel_stat] + [rel_mem] * (2 * n_seq - 2),
        (
            rel_stat,
            pl.BlockSpec((hp, n_mem, rows), lambda i, ids: (ids[0] ^ i, 0, 0)),
        )
        + (full(part),) * n_seq,
        [],
        ids, qn, do, stats, *k_recv, *v_recv,
    )
    parts_recv = to_peers("seq", parts[1:])

    def grads_body(ids_ref, q_ref, kp_ref, qn_ref, kn_ref, vp_ref, do_ref, st_ref, ds_ref, *rest):
        mk_refs = rest[: n_seq - 1]
        inv_ref, qg_ref, gq_ref, gk_ref, gv_ref, dq_ref, gain_q_ref, gain_k_ref, acc = rest[
            n_seq - 1 :
        ]
        step = pl.program_id(0)
        allowed = causal_t(rows)
        inv_c = as_columns(inv_ref[...])

        @pl.when(step == 0)
        def _():
            acc[...] = jnp.zeros_like(acc)

        total = acc[...]
        for i in range(hp):
            at = slice(i * HD, (i + 1) * HD)
            qn_h, kn_h, do_h = qn_ref[:, at], kn_ref[:, at], do_ref[:, at]
            s = jnp.where(allowed, dot(kn_h, qn_h, NT) * scale, -jnp.inf)
            g = dot(vp_ref[:, at], do_h, NT)
            m, inv_mass, delta = st_ref[i, 0:1, :], st_ref[i, 1:2, :], st_ref[i, 2:3, :]
            attend = jnp.exp(s - m) * inv_mass
            ds = (attend * (g - delta)).astype(BF16)
            mk = jnp.concatenate([ref[:, at] for ref in mk_refs], axis=0)
            gq = scale * (dot(ds, kn_h, TN) + dot(ds_ref[i], mk, TN))
            gk = scale * dot(ds, qn_h)
            gq_ref[:, at] = gq
            gk_ref[:, at] = gk
            gv_ref[:, at] = dot(attend.astype(BF16), do_h)
            q_h = q_ref[:, at].astype(F32)
            k_h = kp_ref[:, at].astype(F32)
            gq_q = gq * q_h
            total = total + gq_q * qg_ref[:, at]
            gain_q_ref[0, i : i + 1, :] = jnp.sum(gq_q * inv_c[:, 0:1], axis=0, keepdims=True)
            gain_k_ref[0, i : i + 1, :] = jnp.sum(
                gk * k_h * inv_c[:, 1:2], axis=0, keepdims=True
            )
        acc[...] = total

        @pl.when(step == n_seq - 1)
        def _():
            dq_ref[...] = lane_sum_row(acc[...])

    gain_rows = sds((n_seq, hp, HD), F32)
    gain_spec = pl.BlockSpec((1, hp, HD), lambda i, ids: (i, 0, 0))
    wide_f32 = sds((rows, cols), F32)
    dot_row = sds((1, rows), F32)
    gq, gk_local, gv_local, dot_q, gain_q, gain_k = grid_call(
        grads_body,
        n_seq,
        (wide_f32, wide_f32, wide_f32, dot_row, gain_rows, gain_rows),
        [own_cols] * 6
        + [
            pl.BlockSpec((hp, 8, rows), lambda i, ids: (i, 0, 0)),
            pl.BlockSpec((hp, n_mem, rows), lambda i, ids: (i, 0, 0)),
        ]
        + [own_mem] * (n_seq - 1)
        + [full(inv), pl.BlockSpec((1, wide), lambda i, ids: (0, i))],
        (own_cols, own_cols, own_cols, full(dot_row), gain_spec, gain_spec),
        [pltpu.VMEM((rows, HD), F32)],
        ids, q, kp, qn, kn, vp, do, stats2, ds_mem, *k_recv, inv, qg,
    )

    def slots_body(*refs):
        ins, outs = refs[:n_seq], refs[n_seq:]
        for r in range(n_seq):
            for tensor in range(2):
                total = None
                for src in range(n_seq):
                    if src == r:
                        continue
                    block = (src ^ r) - 1
                    term = ins[src][tensor, block * slots : (block + 1) * slots, :].astype(F32)
                    total = term if total is None else total + term
                outs[r][tensor] = total.astype(BF16)

    slot_grad = sds((2, slots, wide), BF16)
    slot_grads = whole_call(slots_body, (slot_grad,) * n_seq, parts[0], *parts_recv)
    slots_recv = to_peers("seq", slot_grads[1:])

    def weights_body(ids_ref, kn_ref, vp_ref, *rest):
        gm = rest[:n_seq]
        k_refs = rest[n_seq : 2 * n_seq - 1]
        v_refs = rest[2 * n_seq - 1 : 3 * n_seq - 2]
        same_ref, other_ref = rest[3 * n_seq - 2 :]
        here = pl.ds(pl.multiple_of(ids_ref[0] * wide, wide), wide)
        own = (kn_ref[:, here], vp_ref[:, here])
        core_id = ids_ref[1]
        for i in range(hp):
            at = slice(i * HD, (i + 1) * HD)
            for j in range(KS):
                span = slice(j * slots, (j + 1) * slots)
                found = []
                for tensor, refs in ((0, k_refs), (1, v_refs)):
                    lhs = jnp.concatenate(
                        [own[tensor][span, at]] + [ref[span, at] for ref in refs], axis=0
                    )
                    rhs = jnp.concatenate([ref[tensor, :, at] for ref in gm], axis=0)
                    found.append(dot(lhs, rhs, TN))
                to = slice((i * KS + j) * HD, (i * KS + j + 1) * HD)
                first = core_id == 0
                same_ref[to, :] = jnp.where(first, found[0], found[1])
                other_ref[to, :] = jnp.where(first, found[1], found[0]).astype(BF16)

    span_rows = hp * KS * HD
    packet_rows = sds((rows, wide), BF16)
    head_rows = pl.BlockSpec((rows, wide), lambda i, ids: (0, 0))
    w_same, w_other = grid_call(
        weights_body,
        1,
        (sds((span_rows, HD), F32), sds((span_rows, HD), BF16)),
        [full(kn), full(vp)] + [full(slot_grad)] * n_seq + [head_rows] * (2 * n_seq - 2),
        (full(sds((span_rows, HD), F32)), full(sds((span_rows, HD), BF16))),
        [],
        ids, kn, vp, *slot_grads, *k_recv, *v_recv,
    )
    w_recv = to_core(w_other)

    def chunk_body(a_ref, b_ref, gq_ref, gk_ref, out_ref):
        out_ref[:span_rows, :] = (a_ref[...] + b_ref[...].astype(F32)).astype(BF16)
        rows_q = [gq_ref[i] for i in range(n_seq)]
        rows_k = [gk_ref[i] for i in range(n_seq)]
        out_ref[span_rows:, :] = jnp.concatenate(rows_q + rows_k, axis=0).astype(BF16)

    chunk_shape = sds((span_rows + 2 * heads, HD), BF16)
    chunk = whole_call(chunk_body, chunk_shape, w_same, w_recv, gain_q, gain_k)
    chunks = [chunk] + to_peers("seq", [chunk] * (n_seq - 1))
    others = [to_core(c) for c in chunks]

    def back_body(ids_ref, gk_ref, gv_ref, kp_ref, wk_ref, wv_ref, kg_ref, dq_ref, *rest):
        gm = rest[:n_seq]
        value_ref, gkn_ref, dots_ref, acc = rest[n_seq:]
        step = pl.program_id(0)
        unorder = row_order_back(rows)

        @pl.when(step == 0)
        def _():
            acc[...] = jnp.zeros_like(acc)

        total = acc[...]
        mine = gm[0][...]
        for r in peers:
            mine = jnp.where(step == r, gm[r][...], mine)
        for i in range(hp):
            at = slice(i * HD, (i + 1) * HD)
            sides = []
            for tensor, w_ref in ((0, wk_ref), (1, wv_ref)):
                spread = dot(mine[tensor][:, at], w_ref[i], NT)
                sides.append(
                    jnp.concatenate(
                        [spread[:, j * HD : (j + 1) * HD] for j in range(KS)], axis=0
                    )
                )
            gkn = gk_ref[:, at] + sides[0]
            gkn_ref[:, at] = gkn
            total = total + gkn * kp_ref[:, at].astype(F32) * kg_ref[:, at]
            value = (gv_ref[:, at] + sides[1]).astype(BF16)
            value_ref[:, at] = dot(unorder, value).astype(BF16)
        acc[...] = total

        @pl.when(step == n_seq - 1)
        def _():
            dots_ref[0:1, :] = dq_ref[...]
            dots_ref[1:2, :] = lane_sum_row(acc[...])

    rel_w = pl.BlockSpec((hp, KS * HD, HD), lambda i, ids: (ids[0] ^ i, 0, 0))
    two_rows = sds((2, rows), F32)
    grad_value, gkn, dots = grid_call(
        back_body,
        n_seq,
        (sds((rows, cols), BF16), wide_f32, two_rows),
        [rel_cols, rel_cols, rel_cols, rel_w, rel_w]
        + [pl.BlockSpec((1, wide), lambda i, ids: (0, ids[0] ^ i)), full(dot_q)]
        + [full(slot_grad)] * n_seq,
        (rel_cols, rel_cols, full(two_rows)),
        [pltpu.VMEM((rows, HD), F32)],
        ids, gk_local, gv_local, kp, key_squeeze, value_squeeze, kg, dot_q,
        slot_grads[0], *slots_recv,
    )
    dots_peers = to_peers("head", [dots] * (n_head - 1))

    def norms_body(ids_ref, q_ref, kp_ref, gq_ref, gkn_ref, qg_ref, kg_ref, inv_ref, *rest):
        dot_refs = rest[:n_head]
        out_q, out_k = rest[n_head:]
        total = dot_refs[0][...]
        for other in dot_refs[1:]:
            total = total + other[...]
        inv_rows = inv_ref[...]
        inv_c = as_columns(inv_rows)
        pull = as_columns(inv_rows * inv_rows * inv_rows * total / full_width)
        out_q[...] = (
            inv_c[:, 0:1] * qg_ref[...] * gq_ref[...] - q_ref[...].astype(F32) * pull[:, 0:1]
        ).astype(BF16)
        grad_k = (
            inv_c[:, 1:2] * kg_ref[...] * gkn_ref[...] - kp_ref[...].astype(F32) * pull[:, 1:2]
        ).astype(BF16)
        out_k[...] = dot(row_order_back(rows), grad_k).astype(BF16)

    gain_cols = pl.BlockSpec((1, wide), lambda i, ids: (0, i))
    grad_query, grad_key = grid_call(
        norms_body,
        n_seq,
        (sds((rows, cols), BF16), sds((rows, cols), BF16)),
        [own_cols] * 4 + [gain_cols] * 2 + [full(inv)] + [full(dots)] * n_head,
        (own_cols, own_cols),
        [],
        ids, q, kp, gq, gkn, qg, kg, inv, dots, *dots_peers,
    )

    def finish_body(ids_ref, kg_ref, wk_ref, *rest):
        same, other = rest[:n_seq], rest[n_seq : 2 * n_seq]
        gks_ref, gvs_ref, gain_ref = rest[2 * n_seq :]
        step = pl.program_id(0)
        first = ids_ref[1] == 0

        @pl.when(step == 0)
        def _():
            total = None
            for ref in rest[: 2 * n_seq]:
                term = ref[span_rows:, :].astype(F32)
                total = term if total is None else total + term
            gain_ref[...] = total

        for r in range(n_seq):
            @pl.when(step == r)
            def _(r=r):
                for i in range(hp):
                    span = slice(i * KS * HD, (i + 1) * KS * HD)
                    a = same[r][span, :].astype(F32)
                    b = other[r][span, :].astype(F32)
                    gks_ref[i] = jnp.where(first, a, b)
                    gvs_ref[i] = jnp.where(first, b, a)

        for i in range(hp):
            prod = gks_ref[i] * wk_ref[i].astype(F32)
            total = prod[:HD]
            for j in range(1, KS):
                total = total + prod[j * HD : (j + 1) * HD]
            row = lane_sum_row(total)
            head = (ids_ref[0] ^ step) * hp + i
            at = pl.ds(heads + head, 1)
            gain_ref[at, :] = gain_ref[at, :] + row / kg_ref[:, i * HD : (i + 1) * HD]

    kernel_out = sds((heads, KS * HD, HD), F32)
    gains_shape = sds((2 * heads, HD), F32)
    gks, gvs, gains = grid_call(
        finish_body,
        n_seq,
        (kernel_out, kernel_out, gains_shape),
        [pl.BlockSpec((1, wide), lambda i, ids: (0, ids[0] ^ i)), rel_w]
        + [full(chunk_shape)] * (2 * n_seq),
        (rel_w, rel_w, full(gains_shape)),
        [],
        ids, kg, key_squeeze, *chunks, *others,
    )
    return (
        grad_query[None],
        grad_key[None],
        grad_value[None],
        gains[:heads].reshape(cols),
        gains[heads:].reshape(cols),
        gks,
        gvs,
    )


def solution(mesh):
    placed = (
        P("dp", "seq", "head"),
        P("dp", "seq", "head"),
        P("dp", "seq", "head"),
        P("head"),
        P("head"),
        P("head", None, None),
        P("head", None, None),
        P("dp", "seq", "head"),
    )
    return jax.shard_map(
        on_device,
        mesh=mesh,
        in_specs=placed,
        out_specs=(
            P("dp", "seq", "head"),
            P("dp", "seq", "head"),
            P("dp", "seq", "head"),
            P("head"),
            P("head"),
            P("head", None, None),
            P("head", None, None),
        ),
        check_vma=False,
    )
```

```python
import jax
import jax.numpy as jnp
from jax import lax
from jax.experimental import pallas as pl
from jax.experimental.pallas import tpu as pltpu
from jax.sharding import PartitionSpec as P

HD = 128
KS = 4
HH = 4096


epsilon = 1e-06


def unfold_slots(source, head_count):
    batch_size, row_count, widths = source.shape
    return (
        source.reshape(batch_size, row_count // KS, KS, head_count, HD)
        .transpose(0, 1, 3, 2, 4)
        .reshape(batch_size, row_count // KS, head_count, KS * HD)
    )


def fold_slots(source):
    batch_size, slot_count, head_count, spans = source.shape
    return (
        source.reshape(batch_size, slot_count, head_count, KS, HD)
        .transpose(0, 1, 3, 2, 4)
        .reshape(batch_size, slot_count * KS, head_count * HD)
    )


def on_device_any(
    query_heads, key_heads, value_heads, query_gain, key_gain, key_squeeze, value_squeeze, grad_out
):
    batch_size, row_count, widths = query_heads.shape
    head_count = widths // HD
    slot_count = row_count // KS
    score_scale = HD ** (-0.5)
    own_limit = lax.axis_index("seq") * slot_count
    q_full = query_heads.astype(jnp.float32)
    k_full = key_heads.astype(jnp.float32)
    sum_q, sum_k = lax.psum((jnp.sum(q_full * q_full, -1), jnp.sum(k_full * k_full, -1)), "head")
    inv_q = lax.rsqrt(sum_q / HH + epsilon)[..., None]
    inv_k = lax.rsqrt(sum_k / HH + epsilon)[..., None]
    q_norm = (q_full * inv_q * query_gain).astype(jnp.bfloat16)
    k_norm = (k_full * inv_k * key_gain).astype(jnp.bfloat16)
    k_unf = unfold_slots(k_norm, head_count)
    v_unf = unfold_slots(value_heads, head_count)
    mem_k = (
        jnp.einsum("bmhc,hcd->bmhd", k_unf, key_squeeze, preferred_element_type=jnp.float32)
        .astype(jnp.bfloat16)
        .reshape(batch_size, slot_count, widths)
    )
    mem_v = (
        jnp.einsum("bmhc,hcd->bmhd", v_unf, value_squeeze, preferred_element_type=jnp.float32)
        .astype(jnp.bfloat16)
        .reshape(batch_size, slot_count, widths)
    )
    queries = q_norm.reshape(batch_size, row_count, head_count, HD)
    key_loc = k_norm.reshape(batch_size, row_count, head_count, HD)
    value_loc = value_heads.reshape(batch_size, row_count, head_count, HD)
    cotangent = grad_out.reshape(batch_size, row_count, head_count, HD)
    positions = jnp.arange(row_count)
    causal = positions[:, None] >= positions[None, :]
    scores_loc = jnp.where(
        causal,
        jnp.einsum("bthd,buhd->bhtu", queries, key_loc, preferred_element_type=jnp.float32)
        * score_scale,
        -jnp.inf,
    )
    grads_loc = jnp.einsum(
        "bthd,buhd->bhtu", cotangent, value_loc, preferred_element_type=jnp.float32
    )
    all_k, all_v = (
        lax.all_gather(mem_k, "seq", axis=1, tiled=True),
        lax.all_gather(mem_v, "seq", axis=1, tiled=True),
    )
    piece_rows = all_k.shape[1]
    key_rows = all_k.reshape(batch_size, piece_rows, head_count, HD)
    value_rows = all_v.reshape(batch_size, piece_rows, head_count, HD)
    allowed = jnp.arange(piece_rows) < own_limit
    scores = jnp.where(
        allowed,
        jnp.einsum("bthd,buhd->bhtu", queries, key_rows, preferred_element_type=jnp.float32)
        * score_scale,
        -jnp.inf,
    )
    gradients = jnp.einsum(
        "bthd,buhd->bhtu", cotangent, value_rows, preferred_element_type=jnp.float32
    )
    key_rows, scores_mem, grads_mem = (key_rows, scores, gradients)
    peak = jnp.maximum(jnp.max(scores_loc, -1), jnp.max(scores_mem, -1))
    summed = jnp.sum(jnp.exp(scores_loc - peak[..., None]), -1) + jnp.sum(
        jnp.exp(scores_mem - peak[..., None]), -1
    )
    log_mass = peak + jnp.log(summed)
    row_delta = jnp.sum(jnp.exp(scores_loc - log_mass[..., None]) * grads_loc, -1) + jnp.sum(
        jnp.exp(scores_mem - log_mass[..., None]) * grads_mem, -1
    )
    piece_rows = key_rows.shape[1]
    attend = jnp.exp(scores_mem - log_mass[..., None])
    d_scores = (attend * (grads_mem - row_delta[..., None])).astype(jnp.bfloat16)
    grad_q = score_scale * jnp.einsum(
        "bhtu,buhd->bthd", d_scores, key_rows, preferred_element_type=jnp.float32
    )
    grad_k = score_scale * jnp.einsum(
        "bhtu,bthd->buhd", d_scores, queries, preferred_element_type=jnp.float32
    )
    grad_v = jnp.einsum(
        "bhtu,bthd->buhd",
        attend.astype(jnp.bfloat16),
        cotangent,
        preferred_element_type=jnp.float32,
    )
    stacked = jnp.stack(
        (
            grad_k.reshape(batch_size, piece_rows, widths),
            grad_v.reshape(batch_size, piece_rows, widths),
        )
    )
    attend_loc = jnp.exp(scores_loc - log_mass[..., None])
    d_loc = (attend_loc * (grads_loc - row_delta[..., None])).astype(jnp.bfloat16)
    grad_qn = (
        score_scale
        * jnp.einsum("bhtu,buhd->bthd", d_loc, key_loc, preferred_element_type=jnp.float32)
        + grad_q
    ).reshape(batch_size, row_count, widths)
    grad_kn_local = score_scale * jnp.einsum(
        "bhtu,bthd->buhd", d_loc, queries, preferred_element_type=jnp.float32
    )
    grad_v_local = jnp.einsum(
        "bhtu,bthd->buhd",
        attend_loc.astype(jnp.bfloat16),
        cotangent,
        preferred_element_type=jnp.float32,
    )
    mine = lax.psum_scatter(stacked.astype(jnp.bfloat16), "seq", scatter_dimension=2, tiled=True)
    grad_mem_k = mine[0].reshape(batch_size, slot_count, head_count, HD)
    grad_mem_v = mine[1].reshape(batch_size, slot_count, head_count, HD)
    squeeze_k_part = jnp.einsum(
        "bmhc,bmhd->hcd", k_unf, grad_mem_k, preferred_element_type=jnp.float32
    )
    squeeze_v_part = jnp.einsum(
        "bmhc,bmhd->hcd", v_unf, grad_mem_v, preferred_element_type=jnp.float32
    )
    back_k = fold_slots(
        jnp.einsum("bmhd,hcd->bmhc", grad_mem_k, key_squeeze, preferred_element_type=jnp.float32)
    )
    back_v = fold_slots(
        jnp.einsum("bmhd,hcd->bmhc", grad_mem_v, value_squeeze, preferred_element_type=jnp.float32)
    )
    grad_kn = grad_kn_local.reshape(batch_size, row_count, widths) + back_k
    grad_value = (grad_v_local.reshape(batch_size, row_count, widths) + back_v).astype(jnp.bfloat16)
    dot_q, dot_k = lax.psum(
        (jnp.sum(query_gain * grad_qn * q_full, -1), jnp.sum(key_gain * grad_kn * k_full, -1)),
        "head",
    )
    grad_query = (
        inv_q * query_gain * grad_qn - q_full * inv_q**3 * dot_q[..., None] / HH
    ).astype(jnp.bfloat16)
    grad_key = (inv_k * key_gain * grad_kn - k_full * inv_k**3 * dot_k[..., None] / HH).astype(
        jnp.bfloat16
    )
    gain_q_part = jnp.sum(grad_qn * q_full * inv_q, (0, 1))
    gain_k_part = jnp.sum(grad_kn * k_full * inv_k, (0, 1))
    grad_query_gain, grad_key_gain, grad_key_squeeze, grad_value_squeeze = (
        lax.psum(gain_q_part.astype(jnp.bfloat16), ("seq", "dp")).astype(jnp.float32),
        lax.psum(gain_k_part.astype(jnp.bfloat16), ("seq", "dp")).astype(jnp.float32),
        lax.psum(squeeze_k_part.astype(jnp.bfloat16), ("seq", "dp")).astype(jnp.float32),
        lax.psum(squeeze_v_part.astype(jnp.bfloat16), ("seq", "dp")).astype(jnp.float32),
    )
    return (
        grad_query,
        grad_key,
        grad_value,
        grad_query_gain,
        grad_key_gain,
        grad_key_squeeze,
        grad_value_squeeze,
    )


F32 = jnp.float32
BF16 = jnp.bfloat16
NN = (((1,), (0,)), ((), ()))
NT = (((1,), (1,)), ((), ()))
TN = (((0,), (0,)), ((), ()))


def dot(a, b, dims=NN):
    return lax.dot_general(a, b, dims, preferred_element_type=F32)


def sds(shape, dtype):
    return jax.ShapeDtypeStruct(shape, dtype)


def cost_of(micros):
    return pl.CostEstimate(
        flops=int(micros * 1e9), bytes_accessed=int(micros * 3.6e6), transcendentals=0
    )


def whole_call(body, outs, *ins, micros=1.0, after=(), scratch=(), vmem=40):
    n_out = len(jax.tree.leaves(outs))
    skip = len(after)
    space = pl.BlockSpec(memory_space=pltpu.VMEM)
    return pl.pallas_call(
        lambda *refs: body(*refs[: len(ins)], *refs[len(ins) + skip :]),
        out_shape=outs,
        in_specs=[
            pl.BlockSpec(memory_space=pltpu.SMEM) if a.dtype == jnp.int32 else space for a in ins
        ]
        + [pl.BlockSpec(memory_space=pl.ANY)] * skip,
        out_specs=jax.tree.map(lambda _: space, outs),
        scratch_shapes=list(scratch),
        compiler_params=pltpu.CompilerParams(vmem_limit_bytes=vmem * 2**20),
        cost_estimate=cost_of(micros),
    )(*ins, *after)


def grid_call(body, steps, outs, in_specs, out_specs, scratch, ids, *ins, micros=1.0, after=()):
    skip = len(after)
    return pl.pallas_call(
        lambda ids_ref, *refs: body(ids_ref, *refs[skip:]),
        out_shape=outs,
        grid_spec=pltpu.PrefetchScalarGridSpec(
            num_scalar_prefetch=1,
            grid=(steps,),
            in_specs=[pl.BlockSpec(memory_space=pl.ANY)] * skip + list(in_specs),
            out_specs=out_specs,
            scratch_shapes=scratch,
        ),
        compiler_params=pltpu.CompilerParams(
            vmem_limit_bytes=40 * 2**20, dimension_semantics=("arbitrary",)
        ),
        cost_estimate=cost_of(micros),
    )(ids, *after, *ins)


def row_order(rows):
    slots = rows // KS
    r = lax.broadcasted_iota(jnp.int32, (rows, rows), 0)
    c = lax.broadcasted_iota(jnp.int32, (rows, rows), 1)
    return jnp.where(c == KS * (r % slots) + r // slots, 1.0, 0.0).astype(BF16)


def row_order_back(rows):
    slots = rows // KS
    r = lax.broadcasted_iota(jnp.int32, (rows, rows), 0)
    c = lax.broadcasted_iota(jnp.int32, (rows, rows), 1)
    return jnp.where(r == KS * (c % slots) + c // slots, 1.0, 0.0).astype(BF16)


def causal_t(rows):
    slots = rows // KS
    u = lax.broadcasted_iota(jnp.int32, (rows, rows), 0)
    t = lax.broadcasted_iota(jnp.int32, (rows, rows), 1)
    return KS * (u % slots) + u // slots <= t


def fold_lanes(x):
    total = x[:, :HD]
    for i in range(1, x.shape[1] // HD):
        total = total + x[:, i * HD : (i + 1) * HD]
    return total


def lane_sum_row(x):
    return jnp.sum(x.T, axis=0, keepdims=True)


def as_columns(rows):
    pad = jnp.zeros((8 - rows.shape[0], rows.shape[1]), F32)
    return jnp.concatenate([rows, pad], axis=0).T


def on_device(
    query_heads, key_heads, value_heads, query_gain, key_gain, key_squeeze, value_squeeze, grad_out
):
    n_seq, n_head = lax.axis_size("seq"), lax.axis_size("head")
    batch_size, rows, cols = query_heads.shape
    heads = cols // HD
    if batch_size != 1 or n_seq & (n_seq - 1) or heads % n_seq or lax.axis_size("dp") != 2:
        return on_device_any(
            query_heads,
            key_heads,
            value_heads,
            query_gain,
            key_gain,
            key_squeeze,
            value_squeeze,
            grad_out,
        )
    slots = rows // KS
    hp = heads // n_seq
    wide = hp * HD
    mem_rows = n_seq * slots
    peers = range(1, n_seq)
    n_mem = (n_seq - 1) * slots
    scale = HD ** (-0.5)
    full_width = cols * n_head
    me = lax.axis_index("seq")
    core = lax.axis_index("dp")
    ids = jnp.stack([me, core]).astype(jnp.int32)

    def to_peers(axis, arrays):
        n = lax.axis_size(axis)
        return [
            lax.ppermute(a, axis, [(i, i ^ k) for i in range(n)])
            for k, a in zip(range(1, n), arrays)
        ]

    def to_core(a):
        return lax.ppermute(a, "dp", [(0, 1), (1, 0)])

    q = query_heads[0]
    k = key_heads[0]
    v = value_heads[0]
    do = grad_out[0]
    qg = query_gain.reshape(1, cols)
    kg = key_gain.reshape(1, cols)
    full = lambda a: pl.BlockSpec(a.shape, lambda i, ids: (0,) * len(a.shape))
    own_cols = pl.BlockSpec((rows, wide), lambda i, ids: (0, i))
    rel_cols = pl.BlockSpec((rows, wide), lambda i, ids: (0, ids[0] ^ i))
    rel_mem = pl.BlockSpec((slots, wide), lambda i, ids: (ids[0] ^ i, 0))
    own_mem = pl.BlockSpec((slots, wide), lambda i, ids: (i, 0))

    def squares_body(q_ref, k_ref, ss_ref, kp_ref):
        kp = dot(row_order(rows), k_ref[...])
        kp_ref[...] = kp.astype(BF16)
        qf = q_ref[...].astype(F32)
        ss_ref[0:1, :] = lane_sum_row(fold_lanes(qf * qf))
        ss_ref[1:2, :] = lane_sum_row(fold_lanes(kp * kp))

    ss, kp = whole_call(
        squares_body, (sds((2, rows), F32), sds((rows, cols), BF16)), q, k, micros=1.2, vmem=62
    )
    ss_peers = to_peers("head", [ss] * (n_head - 1))

    def compress(source, w_ref, out_ref):
        for h in range(heads):
            total = None
            for j in range(KS):
                part = dot(
                    source[j * slots : (j + 1) * slots, h * HD : (h + 1) * HD],
                    w_ref[h, j * HD : (j + 1) * HD, :],
                )
                total = part if total is None else total + part
            block = h // hp
            out_ref[
                block * slots : (block + 1) * slots, (h % hp) * HD : (h % hp + 1) * HD
            ] = total.astype(BF16)

    def values_body(v_ref, w_ref, vp_ref, mem_ref):
        vp_ref[...] = dot(row_order(rows), v_ref[...]).astype(BF16)
        compress(vp_ref, w_ref, mem_ref)

    rows_shape = sds((rows, cols), BF16)
    mem_shape = sds((mem_rows, wide), BF16)
    vp, mem_v = whole_call(
        values_body, (rows_shape, mem_shape), v, value_squeeze, after=(ss_peers[0],), micros=0.6
    )
    mv_recv = to_peers("seq", [mem_v] * (n_seq - 1))

    def keys_body(q_ref, kp_ref, qg_ref, kg_ref, w_ref, *rest):
        ss_refs = rest[:n_head]
        inv_ref, qn_ref, kn_ref, mem_ref = rest[n_head:]
        total = ss_refs[0][...]
        for other in ss_refs[1:]:
            total = total + other[...]
        inv = lax.rsqrt(total / full_width + epsilon)
        inv_ref[...] = inv
        inv_c = as_columns(inv)
        kn_ref[...] = (kp_ref[...].astype(F32) * inv_c[:, 1:2] * kg_ref[...]).astype(BF16)
        compress(kn_ref, w_ref, mem_ref)
        qn_ref[...] = (q_ref[...].astype(F32) * inv_c[:, 0:1] * qg_ref[...]).astype(BF16)

    inv, qn, kn, mem_k = whole_call(
        keys_body,
        (sds((2, rows), F32), rows_shape, rows_shape, mem_shape),
        q, kp, qg, kg, key_squeeze, ss, *ss_peers,
        micros=1.5,
    )
    mk_recv = to_peers("seq", [mem_k] * (n_seq - 1))

    def local_body(ids_ref, qn_ref, kn_ref, vp_ref, do_ref, st_ref):
        allowed = causal_t(rows)
        for i in range(hp):
            at = slice(i * HD, (i + 1) * HD)
            s = jnp.where(allowed, dot(kn_ref[:, at], qn_ref[:, at], NT) * scale, -jnp.inf)
            g = dot(vp_ref[:, at], do_ref[:, at], NT)
            m = jnp.max(s, axis=0, keepdims=True)
            p = jnp.exp(s - m)
            st_ref[i, 0:1, :] = m
            st_ref[i, 1:2, :] = jnp.sum(p, axis=0, keepdims=True)
            st_ref[i, 2:3, :] = jnp.sum(p * g, axis=0, keepdims=True)

    (stats,) = grid_call(
        local_body,
        n_seq,
        (sds((heads, 8, rows), F32),),
        [own_cols] * 4,
        (pl.BlockSpec((hp, 8, rows), lambda i, ids: (i, 0, 0)),),
        [],
        ids, qn, kn, vp, do,
        micros=2.6,
    )

    def rows_body(ids_ref, kn_ref, vp_ref, *sends):
        for r, send in zip(peers, sends):
            dest = ids_ref[0] ^ r
            at = pl.ds(pl.multiple_of(dest * wide, wide), wide)
            send[0] = kn_ref[:, at]
            send[1] = vp_ref[:, at]

    row_pair = sds((2, rows, wide), BF16)
    row_sends = whole_call(
        rows_body, (row_pair,) * (n_seq - 1), ids, kn, vp, after=(stats,), micros=0.7
    )
    rows_recv = to_peers("seq", row_sends)

    def memory_body(ids_ref, qn_ref, do_ref, st_ref, *rest):
        mk_refs = rest[: n_seq - 1]
        mv_refs = rest[n_seq - 1 : 2 * n_seq - 2]
        st2_ref, ds_ref = rest[2 * n_seq - 2 : 2 * n_seq]
        parts = rest[2 * n_seq :]
        step = pl.program_id(0)
        mine = ids_ref[0]
        for i in range(hp):
            at = slice(i * HD, (i + 1) * HD)
            qn_h = qn_ref[:, at]
            do_h = do_ref[:, at]
            mk = jnp.concatenate([ref[:, at] for ref in mk_refs], axis=0)
            mv = jnp.concatenate([ref[:, at] for ref in mv_refs], axis=0)
            raw = dot(mk, qn_h, NT) * scale
            s = jnp.concatenate(
                [
                    jnp.where((mine ^ r) < mine, raw[(r - 1) * slots : r * slots], -jnp.inf)
                    for r in peers
                ],
                axis=0,
            )
            g = dot(mv, do_h, NT)
            m_loc, l_loc, d_loc = st_ref[i, 0:1, :], st_ref[i, 1:2, :], st_ref[i, 2:3, :]
            m = jnp.maximum(m_loc, jnp.max(s, axis=0, keepdims=True))
            p = jnp.exp(s - m)
            shrink = jnp.exp(m_loc - m)
            mass = l_loc * shrink + jnp.sum(p, axis=0, keepdims=True)
            inv_mass = 1.0 / mass
            delta = (d_loc * shrink + jnp.sum(p * g, axis=0, keepdims=True)) * inv_mass
            st2_ref[i, 0:1, :] = m
            st2_ref[i, 1:2, :] = inv_mass
            st2_ref[i, 2:3, :] = delta
            attend = p * inv_mass
            ds = (attend * (g - delta)).astype(BF16)
            ds_ref[i] = ds
            gk = (dot(ds, qn_h) * scale).astype(BF16)
            gv = dot(attend.astype(BF16), do_h).astype(BF16)
            for r in range(n_seq):
                @pl.when(step == r)
                def _(r=r):
                    parts[r][0, :, at] = gk
                    parts[r][1, :, at] = gv

    part = sds((2, n_mem, wide), BF16)
    rel_stat = pl.BlockSpec((hp, 8, rows), lambda i, ids: (ids[0] ^ i, 0, 0))
    stats2, ds_mem, *parts = grid_call(
        memory_body,
        n_seq,
        (sds((heads, 8, rows), F32), sds((heads, n_mem, rows), BF16)) + (part,) * n_seq,
        [rel_cols, rel_cols, rel_stat] + [rel_mem] * (2 * n_seq - 2),
        (
            rel_stat,
            pl.BlockSpec((hp, n_mem, rows), lambda i, ids: (ids[0] ^ i, 0, 0)),
        )
        + (full(part),) * n_seq,
        [],
        ids, qn, do, stats, *mk_recv, *mv_recv,
        micros=4.8,
    )
    parts_recv = to_peers("seq", parts[1:])

    def grads_body(ids_ref, q_ref, kp_ref, qn_ref, kn_ref, vp_ref, do_ref, st_ref, ds_ref, *rest):
        mk_refs = rest[: n_seq - 1]
        inv_ref, qg_ref, gq_ref, gk_ref, gv_ref, dq_ref, gain_q_ref, gain_k_ref, acc = rest[
            n_seq - 1 :
        ]
        step = pl.program_id(0)
        allowed = causal_t(rows)
        inv_c = as_columns(inv_ref[...])

        @pl.when(step == 0)
        def _():
            acc[...] = jnp.zeros_like(acc)

        total = acc[...]
        for i in range(hp):
            at = slice(i * HD, (i + 1) * HD)
            qn_h, kn_h, do_h = qn_ref[:, at], kn_ref[:, at], do_ref[:, at]
            s = jnp.where(allowed, dot(kn_h, qn_h, NT) * scale, -jnp.inf)
            g = dot(vp_ref[:, at], do_h, NT)
            m, inv_mass, delta = st_ref[i, 0:1, :], st_ref[i, 1:2, :], st_ref[i, 2:3, :]
            attend = jnp.exp(s - m) * inv_mass
            ds = (attend * (g - delta)).astype(BF16)
            mk = jnp.concatenate([ref[:, at] for ref in mk_refs], axis=0)
            gq = scale * (dot(ds, kn_h, TN) + dot(ds_ref[i], mk, TN))
            gk = scale * dot(ds, qn_h)
            gq_ref[:, at] = gq
            gk_ref[:, at] = gk
            gv_ref[:, at] = dot(attend.astype(BF16), do_h)
            q_h = q_ref[:, at].astype(F32)
            k_h = kp_ref[:, at].astype(F32)
            gq_q = gq * q_h
            total = total + gq_q * qg_ref[:, at]
            gain_q_ref[0, i : i + 1, :] = jnp.sum(gq_q * inv_c[:, 0:1], axis=0, keepdims=True)
            gain_k_ref[0, i : i + 1, :] = jnp.sum(
                gk * k_h * inv_c[:, 1:2], axis=0, keepdims=True
            )
        acc[...] = total

        @pl.when(step == n_seq - 1)
        def _():
            dq_ref[...] = lane_sum_row(acc[...])

    gain_rows = sds((n_seq, hp, HD), F32)
    gain_spec = pl.BlockSpec((1, hp, HD), lambda i, ids: (i, 0, 0))
    wide_f32 = sds((rows, cols), F32)
    dot_row = sds((1, rows), F32)
    gq, gk_local, gv_local, dot_q, gain_q, gain_k = grid_call(
        grads_body,
        n_seq,
        (wide_f32, wide_f32, wide_f32, dot_row, gain_rows, gain_rows),
        [own_cols] * 6
        + [
            pl.BlockSpec((hp, 8, rows), lambda i, ids: (i, 0, 0)),
            pl.BlockSpec((hp, n_mem, rows), lambda i, ids: (i, 0, 0)),
        ]
        + [own_mem] * (n_seq - 1)
        + [full(inv), pl.BlockSpec((1, wide), lambda i, ids: (0, i))],
        (own_cols, own_cols, own_cols, full(dot_row), gain_spec, gain_spec),
        [pltpu.VMEM((rows, HD), F32)],
        ids, q, kp, qn, kn, vp, do, stats2, ds_mem, *mk_recv, inv, qg,
        micros=5.8,
    )

    def slots_body(*refs):
        ins, outs = refs[:n_seq], refs[n_seq:]
        for r in range(n_seq):
            for tensor in range(2):
                total = None
                for src in range(n_seq):
                    if src == r:
                        continue
                    block = (src ^ r) - 1
                    term = ins[src][tensor, block * slots : (block + 1) * slots, :].astype(F32)
                    total = term if total is None else total + term
                outs[r][tensor] = total.astype(BF16)

    slot_grad = sds((2, slots, wide), BF16)
    slot_grads = whole_call(
        slots_body, (slot_grad,) * n_seq, parts[0], *parts_recv, after=(gain_q,), micros=0.3
    )
    slots_recv = to_peers("seq", slot_grads[1:])

    def weights_body(ids_ref, kn_ref, vp_ref, *rest):
        gm = rest[:n_seq]
        row_refs = rest[n_seq : 2 * n_seq - 1]
        same_ref, other_ref = rest[2 * n_seq - 1 :]
        here = pl.ds(pl.multiple_of(ids_ref[0] * wide, wide), wide)
        own = (kn_ref[:, here], vp_ref[:, here])
        first = ids_ref[1] == 0
        for i in range(hp):
            at = slice(i * HD, (i + 1) * HD)
            for j in range(KS):
                span = slice(j * slots, (j + 1) * slots)
                found = []
                for tensor in range(2):
                    lhs = jnp.concatenate(
                        [own[tensor][span, at]] + [ref[tensor, span, at] for ref in row_refs],
                        axis=0,
                    )
                    rhs = jnp.concatenate([ref[tensor, :, at] for ref in gm], axis=0)
                    found.append(dot(lhs, rhs, TN))
                to = slice((i * KS + j) * HD, (i * KS + j + 1) * HD)
                same_ref[to, :] = jnp.where(first, found[0], found[1])
                other_ref[to, :] = jnp.where(first, found[1], found[0]).astype(BF16)

    span_rows = hp * KS * HD
    w_same, w_other = whole_call(
        weights_body,
        (sds((span_rows, HD), F32), sds((span_rows, HD), BF16)),
        ids, kn, vp, *slot_grads, *rows_recv,
        micros=1.1,
    )
    w_recv = to_core(w_other)

    def chunk_body(a_ref, b_ref, gq_ref, gk_ref, out_ref):
        out_ref[:span_rows, :] = (a_ref[...] + b_ref[...].astype(F32)).astype(BF16)
        rows_q = [gq_ref[i] for i in range(n_seq)]
        rows_k = [gk_ref[i] for i in range(n_seq)]
        out_ref[span_rows:, :] = jnp.concatenate(rows_q + rows_k, axis=0).astype(BF16)

    chunk_shape = sds((span_rows + 2 * heads, HD), BF16)
    chunk = whole_call(chunk_body, chunk_shape, w_same, w_recv, gain_q, gain_k, micros=0.3)
    chunks = [chunk] + to_peers("seq", [chunk] * (n_seq - 1))

    def back_body(ids_ref, gk_ref, gv_ref, kp_ref, wk_ref, wv_ref, kg_ref, dq_ref, *rest):
        gm = rest[:n_seq]
        value_ref, gkn_ref, dots_ref, acc = rest[n_seq:]
        step = pl.program_id(0)
        unorder = row_order_back(rows)

        @pl.when(step == 0)
        def _():
            acc[...] = jnp.zeros_like(acc)

        total = acc[...]
        mine = gm[0][...]
        for r in peers:
            mine = jnp.where(step == r, gm[r][...], mine)
        for i in range(hp):
            at = slice(i * HD, (i + 1) * HD)
            sides = []
            for tensor, w_ref in ((0, wk_ref), (1, wv_ref)):
                spread = dot(mine[tensor][:, at], w_ref[i], NT)
                sides.append(
                    jnp.concatenate(
                        [spread[:, j * HD : (j + 1) * HD] for j in range(KS)], axis=0
                    )
                )
            gkn = gk_ref[:, at] + sides[0]
            gkn_ref[:, at] = gkn
            total = total + gkn * kp_ref[:, at].astype(F32) * kg_ref[:, at]
            value = (gv_ref[:, at] + sides[1]).astype(BF16)
            value_ref[:, at] = dot(unorder, value).astype(BF16)
        acc[...] = total

        @pl.when(step == n_seq - 1)
        def _():
            dots_ref[0:1, :] = dq_ref[...]
            dots_ref[1:2, :] = lane_sum_row(acc[...])

    rel_w = pl.BlockSpec((hp, KS * HD, HD), lambda i, ids: (ids[0] ^ i, 0, 0))
    two_rows = sds((2, rows), F32)
    grad_value, gkn, dots = grid_call(
        back_body,
        n_seq,
        (sds((rows, cols), BF16), wide_f32, two_rows),
        [rel_cols, rel_cols, rel_cols, rel_w, rel_w]
        + [pl.BlockSpec((1, wide), lambda i, ids: (0, ids[0] ^ i)), full(dot_q)]
        + [full(slot_grad)] * n_seq,
        (rel_cols, rel_cols, full(two_rows)),
        [pltpu.VMEM((rows, HD), F32)],
        ids, gk_local, gv_local, kp, key_squeeze, value_squeeze, kg, dot_q,
        slot_grads[0], *slots_recv,
        after=(chunk,),
        micros=4.5,
    )
    dots_peers = to_peers("head", [dots] * (n_head - 1))

    def pack_body(*refs):
        for r in range(n_seq):
            refs[n_seq][r] = refs[r][...]

    packed_shape = sds((n_seq,) + chunk_shape.shape, BF16)
    packed = whole_call(pack_body, packed_shape, *chunks, after=tuple(dots_peers), micros=1.0)
    packed_other = to_core(packed)

    def norms_body(ids_ref, q_ref, kp_ref, gq_ref, gkn_ref, qg_ref, kg_ref, inv_ref, *rest):
        dot_refs = rest[:n_head]
        out_q, out_k = rest[n_head:]
        total = dot_refs[0][...]
        for other in dot_refs[1:]:
            total = total + other[...]
        inv_rows = inv_ref[...]
        inv_c = as_columns(inv_rows)
        pull = as_columns(inv_rows * inv_rows * inv_rows * total / full_width)
        out_q[...] = (
            inv_c[:, 0:1] * qg_ref[...] * gq_ref[...] - q_ref[...].astype(F32) * pull[:, 0:1]
        ).astype(BF16)
        grad_k = (
            inv_c[:, 1:2] * kg_ref[...] * gkn_ref[...] - kp_ref[...].astype(F32) * pull[:, 1:2]
        ).astype(BF16)
        out_k[...] = dot(row_order_back(rows), grad_k).astype(BF16)

    gain_cols = pl.BlockSpec((1, wide), lambda i, ids: (0, i))
    grad_query, grad_key = grid_call(
        norms_body,
        n_seq,
        (sds((rows, cols), BF16), sds((rows, cols), BF16)),
        [own_cols] * 4 + [gain_cols] * 2 + [full(inv)] + [full(dots)] * n_head,
        (own_cols, own_cols),
        [],
        ids, q, kp, gq, gkn, qg, kg, inv, dots, *dots_peers,
        micros=3.5,
    )

    def finish_body(ids_ref, kg_ref, wk_ref, same, other, gks_ref, gvs_ref, gain_ref):
        step = pl.program_id(0)
        first = ids_ref[1] == 0

        @pl.when(step == 0)
        def _():
            gain_ref[...] = jnp.zeros_like(gain_ref)

        gain_ref[...] += same[0, span_rows:, :].astype(F32) + other[0, span_rows:, :].astype(F32)
        for i in range(hp):
            span = slice(i * KS * HD, (i + 1) * KS * HD)
            a = same[0, span, :].astype(F32)
            b = other[0, span, :].astype(F32)
            gks_ref[i] = jnp.where(first, a, b)
            gvs_ref[i] = jnp.where(first, b, a)
            prod = gks_ref[i] * wk_ref[i].astype(F32)
            total = prod[:HD]
            for j in range(1, KS):
                total = total + prod[j * HD : (j + 1) * HD]
            row = lane_sum_row(total)
            head = (ids_ref[0] ^ step) * hp + i
            at = pl.ds(heads + head, 1)
            gain_ref[at, :] = gain_ref[at, :] + row / kg_ref[:, i * HD : (i + 1) * HD]

    kernel_out = sds((heads, KS * HD, HD), F32)
    gains_shape = sds((2 * heads, HD), F32)
    step_chunk = pl.BlockSpec((1,) + chunk_shape.shape, lambda i, ids: (i, 0, 0))
    gks, gvs, gains = grid_call(
        finish_body,
        n_seq,
        (kernel_out, kernel_out, gains_shape),
        [pl.BlockSpec((1, wide), lambda i, ids: (0, ids[0] ^ i)), rel_w, step_chunk, step_chunk],
        (rel_w, rel_w, full(gains_shape)),
        [],
        ids, kg, key_squeeze, packed, packed_other,
        micros=3.2,
    )
    return (
        grad_query[None],
        grad_key[None],
        grad_value[None],
        gains[:heads].reshape(cols),
        gains[heads:].reshape(cols),
        gks,
        gvs,
    )


def solution(mesh):
    placed = (
        P("dp", "seq", "head"),
        P("dp", "seq", "head"),
        P("dp", "seq", "head"),
        P("head"),
        P("head"),
        P("head", None, None),
        P("head", None, None),
        P("dp", "seq", "head"),
    )
    return jax.shard_map(
        on_device,
        mesh=mesh,
        in_specs=placed,
        out_specs=(
            P("dp", "seq", "head"),
            P("dp", "seq", "head"),
            P("dp", "seq", "head"),
            P("head"),
            P("head"),
            P("head", None, None),
            P("head", None, None),
        ),
        check_vma=False,
    )
```

```python
import jax
import jax.numpy as jnp
from jax import lax
from jax.experimental import pallas as pl
from jax.experimental.pallas import tpu as pltpu
from jax.sharding import PartitionSpec as P

HD = 128
KS = 4
HH = 4096


epsilon = 1e-06


def unfold_slots(source, head_count):
    batch_size, row_count, widths = source.shape
    return (
        source.reshape(batch_size, row_count // KS, KS, head_count, HD)
        .transpose(0, 1, 3, 2, 4)
        .reshape(batch_size, row_count // KS, head_count, KS * HD)
    )


def fold_slots(source):
    batch_size, slot_count, head_count, spans = source.shape
    return (
        source.reshape(batch_size, slot_count, head_count, KS, HD)
        .transpose(0, 1, 3, 2, 4)
        .reshape(batch_size, slot_count * KS, head_count * HD)
    )


def on_device_any(
    query_heads, key_heads, value_heads, query_gain, key_gain, key_squeeze, value_squeeze, grad_out
):
    batch_size, row_count, widths = query_heads.shape
    head_count = widths // HD
    slot_count = row_count // KS
    score_scale = HD ** (-0.5)
    own_limit = lax.axis_index("seq") * slot_count
    q_full = query_heads.astype(jnp.float32)
    k_full = key_heads.astype(jnp.float32)
    sum_q, sum_k = lax.psum((jnp.sum(q_full * q_full, -1), jnp.sum(k_full * k_full, -1)), "head")
    inv_q = lax.rsqrt(sum_q / HH + epsilon)[..., None]
    inv_k = lax.rsqrt(sum_k / HH + epsilon)[..., None]
    q_norm = (q_full * inv_q * query_gain).astype(jnp.bfloat16)
    k_norm = (k_full * inv_k * key_gain).astype(jnp.bfloat16)
    k_unf = unfold_slots(k_norm, head_count)
    v_unf = unfold_slots(value_heads, head_count)
    mem_k = (
        jnp.einsum("bmhc,hcd->bmhd", k_unf, key_squeeze, preferred_element_type=jnp.float32)
        .astype(jnp.bfloat16)
        .reshape(batch_size, slot_count, widths)
    )
    mem_v = (
        jnp.einsum("bmhc,hcd->bmhd", v_unf, value_squeeze, preferred_element_type=jnp.float32)
        .astype(jnp.bfloat16)
        .reshape(batch_size, slot_count, widths)
    )
    queries = q_norm.reshape(batch_size, row_count, head_count, HD)
    key_loc = k_norm.reshape(batch_size, row_count, head_count, HD)
    value_loc = value_heads.reshape(batch_size, row_count, head_count, HD)
    cotangent = grad_out.reshape(batch_size, row_count, head_count, HD)
    positions = jnp.arange(row_count)
    causal = positions[:, None] >= positions[None, :]
    scores_loc = jnp.where(
        causal,
        jnp.einsum("bthd,buhd->bhtu", queries, key_loc, preferred_element_type=jnp.float32)
        * score_scale,
        -jnp.inf,
    )
    grads_loc = jnp.einsum(
        "bthd,buhd->bhtu", cotangent, value_loc, preferred_element_type=jnp.float32
    )
    all_k, all_v = (
        lax.all_gather(mem_k, "seq", axis=1, tiled=True),
        lax.all_gather(mem_v, "seq", axis=1, tiled=True),
    )
    piece_rows = all_k.shape[1]
    key_rows = all_k.reshape(batch_size, piece_rows, head_count, HD)
    value_rows = all_v.reshape(batch_size, piece_rows, head_count, HD)
    allowed = jnp.arange(piece_rows) < own_limit
    scores = jnp.where(
        allowed,
        jnp.einsum("bthd,buhd->bhtu", queries, key_rows, preferred_element_type=jnp.float32)
        * score_scale,
        -jnp.inf,
    )
    gradients = jnp.einsum(
        "bthd,buhd->bhtu", cotangent, value_rows, preferred_element_type=jnp.float32
    )
    key_rows, scores_mem, grads_mem = (key_rows, scores, gradients)
    peak = jnp.maximum(jnp.max(scores_loc, -1), jnp.max(scores_mem, -1))
    summed = jnp.sum(jnp.exp(scores_loc - peak[..., None]), -1) + jnp.sum(
        jnp.exp(scores_mem - peak[..., None]), -1
    )
    log_mass = peak + jnp.log(summed)
    row_delta = jnp.sum(jnp.exp(scores_loc - log_mass[..., None]) * grads_loc, -1) + jnp.sum(
        jnp.exp(scores_mem - log_mass[..., None]) * grads_mem, -1
    )
    piece_rows = key_rows.shape[1]
    attend = jnp.exp(scores_mem - log_mass[..., None])
    d_scores = (attend * (grads_mem - row_delta[..., None])).astype(jnp.bfloat16)
    grad_q = score_scale * jnp.einsum(
        "bhtu,buhd->bthd", d_scores, key_rows, preferred_element_type=jnp.float32
    )
    grad_k = score_scale * jnp.einsum(
        "bhtu,bthd->buhd", d_scores, queries, preferred_element_type=jnp.float32
    )
    grad_v = jnp.einsum(
        "bhtu,bthd->buhd",
        attend.astype(jnp.bfloat16),
        cotangent,
        preferred_element_type=jnp.float32,
    )
    stacked = jnp.stack(
        (
            grad_k.reshape(batch_size, piece_rows, widths),
            grad_v.reshape(batch_size, piece_rows, widths),
        )
    )
    attend_loc = jnp.exp(scores_loc - log_mass[..., None])
    d_loc = (attend_loc * (grads_loc - row_delta[..., None])).astype(jnp.bfloat16)
    grad_qn = (
        score_scale
        * jnp.einsum("bhtu,buhd->bthd", d_loc, key_loc, preferred_element_type=jnp.float32)
        + grad_q
    ).reshape(batch_size, row_count, widths)
    grad_kn_local = score_scale * jnp.einsum(
        "bhtu,bthd->buhd", d_loc, queries, preferred_element_type=jnp.float32
    )
    grad_v_local = jnp.einsum(
        "bhtu,bthd->buhd",
        attend_loc.astype(jnp.bfloat16),
        cotangent,
        preferred_element_type=jnp.float32,
    )
    mine = lax.psum_scatter(stacked.astype(jnp.bfloat16), "seq", scatter_dimension=2, tiled=True)
    grad_mem_k = mine[0].reshape(batch_size, slot_count, head_count, HD)
    grad_mem_v = mine[1].reshape(batch_size, slot_count, head_count, HD)
    squeeze_k_part = jnp.einsum(
        "bmhc,bmhd->hcd", k_unf, grad_mem_k, preferred_element_type=jnp.float32
    )
    squeeze_v_part = jnp.einsum(
        "bmhc,bmhd->hcd", v_unf, grad_mem_v, preferred_element_type=jnp.float32
    )
    back_k = fold_slots(
        jnp.einsum("bmhd,hcd->bmhc", grad_mem_k, key_squeeze, preferred_element_type=jnp.float32)
    )
    back_v = fold_slots(
        jnp.einsum("bmhd,hcd->bmhc", grad_mem_v, value_squeeze, preferred_element_type=jnp.float32)
    )
    grad_kn = grad_kn_local.reshape(batch_size, row_count, widths) + back_k
    grad_value = (grad_v_local.reshape(batch_size, row_count, widths) + back_v).astype(jnp.bfloat16)
    dot_q, dot_k = lax.psum(
        (jnp.sum(query_gain * grad_qn * q_full, -1), jnp.sum(key_gain * grad_kn * k_full, -1)),
        "head",
    )
    grad_query = (
        inv_q * query_gain * grad_qn - q_full * inv_q**3 * dot_q[..., None] / HH
    ).astype(jnp.bfloat16)
    grad_key = (inv_k * key_gain * grad_kn - k_full * inv_k**3 * dot_k[..., None] / HH).astype(
        jnp.bfloat16
    )
    gain_q_part = jnp.sum(grad_qn * q_full * inv_q, (0, 1))
    gain_k_part = jnp.sum(grad_kn * k_full * inv_k, (0, 1))
    grad_query_gain, grad_key_gain, grad_key_squeeze, grad_value_squeeze = (
        lax.psum(gain_q_part.astype(jnp.bfloat16), ("seq", "dp")).astype(jnp.float32),
        lax.psum(gain_k_part.astype(jnp.bfloat16), ("seq", "dp")).astype(jnp.float32),
        lax.psum(squeeze_k_part.astype(jnp.bfloat16), ("seq", "dp")).astype(jnp.float32),
        lax.psum(squeeze_v_part.astype(jnp.bfloat16), ("seq", "dp")).astype(jnp.float32),
    )
    return (
        grad_query,
        grad_key,
        grad_value,
        grad_query_gain,
        grad_key_gain,
        grad_key_squeeze,
        grad_value_squeeze,
    )


F32 = jnp.float32
BF16 = jnp.bfloat16
NN = (((1,), (0,)), ((), ()))
NT = (((1,), (1,)), ((), ()))
TN = (((0,), (0,)), ((), ()))


def dot(a, b, dims=NN):
    return lax.dot_general(a, b, dims, preferred_element_type=F32)


def sds(shape, dtype):
    return jax.ShapeDtypeStruct(shape, dtype)


def cost_of(micros):
    return pl.CostEstimate(
        flops=int(micros * 1e9), bytes_accessed=int(micros * 3.6e6), transcendentals=0
    )


def whole_call(body, outs, *ins, micros=1.0, after=(), scratch=(), vmem=40):
    n_out = len(jax.tree.leaves(outs))
    skip = len(after)
    space = pl.BlockSpec(memory_space=pltpu.VMEM)
    return pl.pallas_call(
        lambda *refs: body(*refs[: len(ins)], *refs[len(ins) + skip :]),
        out_shape=outs,
        in_specs=[
            pl.BlockSpec(memory_space=pltpu.SMEM) if a.dtype == jnp.int32 else space for a in ins
        ]
        + [pl.BlockSpec(memory_space=pl.ANY)] * skip,
        out_specs=jax.tree.map(lambda _: space, outs),
        scratch_shapes=list(scratch),
        compiler_params=pltpu.CompilerParams(vmem_limit_bytes=vmem * 2**20),
        cost_estimate=cost_of(micros),
    )(*ins, *after)


def row_order(rows):
    slots = rows // KS
    r = lax.broadcasted_iota(jnp.int32, (rows, rows), 0)
    c = lax.broadcasted_iota(jnp.int32, (rows, rows), 1)
    return jnp.where(c == KS * (r % slots) + r // slots, 1.0, 0.0).astype(BF16)


def row_order_back(rows):
    slots = rows // KS
    r = lax.broadcasted_iota(jnp.int32, (rows, rows), 0)
    c = lax.broadcasted_iota(jnp.int32, (rows, rows), 1)
    return jnp.where(r == KS * (c % slots) + c // slots, 1.0, 0.0).astype(BF16)


def causal_t(rows):
    slots = rows // KS
    u = lax.broadcasted_iota(jnp.int32, (rows, rows), 0)
    t = lax.broadcasted_iota(jnp.int32, (rows, rows), 1)
    return KS * (u % slots) + u // slots <= t


def fold_lanes(x):
    total = x[:, :HD]
    for i in range(1, x.shape[1] // HD):
        total = total + x[:, i * HD : (i + 1) * HD]
    return total


def lane_sum_row(x):
    return jnp.sum(x.T, axis=0, keepdims=True)


def as_columns(rows):
    pad = jnp.zeros((8 - rows.shape[0], rows.shape[1]), F32)
    return jnp.concatenate([rows, pad], axis=0).T


def on_device(
    query_heads, key_heads, value_heads, query_gain, key_gain, key_squeeze, value_squeeze, grad_out
):
    n_seq, n_head = lax.axis_size("seq"), lax.axis_size("head")
    batch_size, rows, cols = query_heads.shape
    heads = cols // HD
    if batch_size != 1 or n_seq & (n_seq - 1) or heads % n_seq or lax.axis_size("dp") != 2:
        return on_device_any(
            query_heads,
            key_heads,
            value_heads,
            query_gain,
            key_gain,
            key_squeeze,
            value_squeeze,
            grad_out,
        )
    slots = rows // KS
    hp = heads // n_seq
    wide = hp * HD
    mem_rows = n_seq * slots
    peers = range(1, n_seq)
    n_mem = (n_seq - 1) * slots
    scale = HD ** (-0.5)
    full_width = cols * n_head
    me = lax.axis_index("seq")
    core = lax.axis_index("dp")
    ids = jnp.stack([me, core]).astype(jnp.int32)

    def to_peers(axis, arrays):
        n = lax.axis_size(axis)
        return [
            lax.ppermute(a, axis, [(i, i ^ k) for i in range(n)])
            for k, a in zip(range(1, n), arrays)
        ]

    def to_core(a):
        return lax.ppermute(a, "dp", [(0, 1), (1, 0)])

    q = query_heads[0]
    k = key_heads[0]
    v = value_heads[0]
    do = grad_out[0]
    qg = query_gain.reshape(1, cols)
    kg = key_gain.reshape(1, cols)

    def squares_body(q_ref, k_ref, ss_ref):
        qf = q_ref[...].astype(F32)
        ss_ref[0:1, :] = lane_sum_row(fold_lanes(qf * qf))
        kf = k_ref[...].astype(F32)
        ss_ref[1:2, :] = lane_sum_row(fold_lanes(kf * kf))

    two_rows = sds((2, rows), F32)
    ss = whole_call(squares_body, two_rows, q, k, micros=1.5, vmem=62)
    ss_peers = to_peers("head", [ss] * (n_head - 1))

    def compress(source, w_ref, out_ref):
        for h in range(heads):
            total = None
            for j in range(KS):
                part = dot(
                    source[j * slots : (j + 1) * slots, h * HD : (h + 1) * HD],
                    w_ref[h, j * HD : (j + 1) * HD, :],
                )
                total = part if total is None else total + part
            block = h // hp
            out_ref[
                block * slots : (block + 1) * slots, (h % hp) * HD : (h % hp + 1) * HD
            ] = total.astype(BF16)

    def values_body(v_ref, k_ref, w_ref, vp_ref, mem_ref, kp_ref):
        order = row_order(rows)
        vp_ref[...] = dot(order, v_ref[...]).astype(BF16)
        compress(vp_ref, w_ref, mem_ref)
        kp_ref[...] = dot(order, k_ref[...]).astype(BF16)

    rows_shape = sds((rows, cols), BF16)
    mem_shape = sds((mem_rows, wide), BF16)
    vp, mem_v, kp = whole_call(
        values_body,
        (rows_shape, mem_shape, rows_shape),
        v, k, value_squeeze,
        micros=0.8,
    )

    def keys_body(q_ref, k_ref, qg_ref, kg_ref, w_ref, mem_v_ref, *rest):
        ss_refs = rest[:n_head]
        inv_ref, qn_ref, kn_ref, mem_ref = rest[n_head:]
        total = ss_refs[0][...]
        for other in ss_refs[1:]:
            total = total + other[...]
        natural = as_columns(lax.rsqrt(total / full_width + epsilon))
        order = row_order(rows)
        high = natural.astype(BF16)
        rest_1 = natural - high.astype(F32)
        middle = rest_1.astype(BF16)
        low = (rest_1 - middle.astype(F32)).astype(BF16)
        ordered = dot(order, high) + dot(order, middle) + dot(order, low)
        inv_c = jnp.concatenate([natural[:, 0:1], ordered[:, 1:2], natural[:, 2:]], axis=1)
        inv_ref[...] = inv_c.T[:2]
        normed = (k_ref[...].astype(F32) * natural[:, 1:2] * kg_ref[...]).astype(BF16)
        kn_ref[...] = dot(order, normed).astype(BF16)
        compress(kn_ref, w_ref, mem_ref.at[0])
        mem_ref[1] = mem_v_ref[...]
        qn_ref[...] = (q_ref[...].astype(F32) * inv_c[:, 0:1] * qg_ref[...]).astype(BF16)

    mem_pair = sds((2, mem_rows, wide), BF16)
    inv, qn, kn, mem = whole_call(
        keys_body,
        (sds((2, rows), F32), rows_shape, rows_shape, mem_pair),
        q, k, qg, kg, key_squeeze, mem_v, ss, *ss_peers,
        micros=1.5,
    )
    mem_recv = to_peers("seq", [mem] * (n_seq - 1))

    def local_body(qn_ref, kn_ref, vp_ref, do_ref, st_ref):
        allowed = causal_t(rows)
        for h in range(heads):
            at = slice(h * HD, (h + 1) * HD)
            s = jnp.where(allowed, dot(kn_ref[:, at], qn_ref[:, at], NT) * scale, -jnp.inf)
            g = dot(vp_ref[:, at], do_ref[:, at], NT)
            m = jnp.max(s, axis=0, keepdims=True)
            p = jnp.exp(s - m)
            st_ref[h, 0:1, :] = m
            st_ref[h, 1:2, :] = jnp.sum(p, axis=0, keepdims=True)
            st_ref[h, 2:3, :] = jnp.sum(p * g, axis=0, keepdims=True)

    stat_shape = sds((heads, 8, rows), F32)
    stats = whole_call(local_body, stat_shape, qn, kn, vp, do, micros=0.5)

    def rows_body(ids_ref, kn_ref, vp_ref, *sends):
        for r, send in zip(peers, sends):
            dest = ids_ref[0] ^ r
            at = pl.ds(pl.multiple_of(dest * wide, wide), wide)
            send[0] = kn_ref[:, at]
            send[1] = vp_ref[:, at]

    row_pair = sds((2, rows, wide), BF16)
    row_sends = whole_call(
        rows_body, (row_pair,) * (n_seq - 1), ids, kn, vp, after=(stats,), micros=0.7
    )
    rows_recv = to_peers("seq", row_sends)

    def memory_body(ids_ref, qn_ref, do_ref, st_ref, *rest):
        mem_refs = rest[: n_seq - 1]
        st2_ref, ds_ref = rest[n_seq - 1 : n_seq + 1]
        parts = rest[n_seq + 1 :]
        mine = ids_ref[0]
        for r in range(n_seq):
            block = mine ^ r
            span = pl.ds(pl.multiple_of(block * slots, slots), slots)
            for i in range(hp):
                at = slice(i * HD, (i + 1) * HD)
                h = block * hp + i
                wide_at = pl.ds(pl.multiple_of(h * HD, HD), HD)
                qn_h = qn_ref[:, wide_at]
                do_h = do_ref[:, wide_at]
                mk = jnp.concatenate([ref[0, span, at] for ref in mem_refs], axis=0)
                mv = jnp.concatenate([ref[1, span, at] for ref in mem_refs], axis=0)
                raw = dot(mk, qn_h, NT) * scale
                s = jnp.concatenate(
                    [
                        jnp.where((mine ^ src) < mine, raw[(src - 1) * slots : src * slots], -jnp.inf)
                        for src in peers
                    ],
                    axis=0,
                )
                g = dot(mv, do_h, NT)
                stat = st_ref[h]
                m_loc, l_loc, d_loc = stat[0:1], stat[1:2], stat[2:3]
                m = jnp.maximum(m_loc, jnp.max(s, axis=0, keepdims=True))
                p = jnp.exp(s - m)
                shrink = jnp.exp(m_loc - m)
                mass = l_loc * shrink + jnp.sum(p, axis=0, keepdims=True)
                inv_mass = 1.0 / mass
                delta = (d_loc * shrink + jnp.sum(p * g, axis=0, keepdims=True)) * inv_mass
                st2_ref[h] = jnp.concatenate([m, inv_mass, delta, stat[3:]], axis=0)
                attend = p * inv_mass
                ds = (attend * (g - delta)).astype(BF16)
                ds_ref[h] = ds
                parts[r][0, :, at] = (dot(ds, qn_h) * scale).astype(BF16)
                parts[r][1, :, at] = dot(attend.astype(BF16), do_h).astype(BF16)

    part = sds((2, n_mem, wide), BF16)
    stats2, ds_mem, *parts = whole_call(
        memory_body,
        (stat_shape, sds((heads, n_mem, rows), BF16)) + (part,) * n_seq,
        ids, qn, do, stats, *mem_recv,
        micros=0.5,
    )
    parts_recv = to_peers("seq", parts[1:])

    def grads_body(q_ref, kp_ref, qn_ref, kn_ref, vp_ref, do_ref, st_ref, ds_ref, *rest):
        mem_refs = rest[: n_seq - 1]
        inv_ref, qg_ref, gq_ref, gk_ref, gv_ref, dq_ref, gain_q_ref, gain_k_ref = rest[n_seq - 1 :]
        allowed = causal_t(rows)
        inv_c = as_columns(inv_ref[...])
        total = jnp.zeros((rows, HD), F32)
        for h in range(heads):
            at = slice(h * HD, (h + 1) * HD)
            narrow = slice((h % hp) * HD, (h % hp + 1) * HD)
            span = slice((h // hp) * slots, (h // hp + 1) * slots)
            qn_h, kn_h, do_h = qn_ref[:, at], kn_ref[:, at], do_ref[:, at]
            s = jnp.where(allowed, dot(kn_h, qn_h, NT) * scale, -jnp.inf)
            g = dot(vp_ref[:, at], do_h, NT)
            m, inv_mass, delta = st_ref[h, 0:1, :], st_ref[h, 1:2, :], st_ref[h, 2:3, :]
            attend = jnp.exp(s - m) * inv_mass
            ds = (attend * (g - delta)).astype(BF16)
            mk = jnp.concatenate([ref[0, span, narrow] for ref in mem_refs], axis=0)
            gq = scale * (dot(ds, kn_h, TN) + dot(ds_ref[h], mk, TN))
            gk = scale * dot(ds, qn_h)
            gq_ref[:, at] = gq
            gk_ref[:, at] = gk
            gv_ref[:, at] = dot(attend.astype(BF16), do_h)
            gq_q = gq * q_ref[:, at].astype(F32)
            gk_k = gk * kp_ref[:, at].astype(F32)
            total = total + gq_q * qg_ref[:, at]
            gain_q_ref[h : h + 1, :] = jnp.sum(gq_q * inv_c[:, 0:1], axis=0, keepdims=True)
            gain_k_ref[h : h + 1, :] = jnp.sum(gk_k * inv_c[:, 1:2], axis=0, keepdims=True)
        dq_ref[...] = lane_sum_row(total)

    gain_rows = sds((heads, HD), F32)
    wide_f32 = sds((rows, cols), F32)
    dot_row = sds((1, rows), F32)
    gq, gk_local, gv_local, dot_q, gain_q, gain_k = whole_call(
        grads_body,
        (wide_f32, wide_f32, wide_f32, dot_row, gain_rows, gain_rows),
        q, kp, qn, kn, vp, do, stats2, ds_mem, *mem_recv, inv, qg,
        micros=0.5,
        after=tuple(rows_recv),
    )

    def slots_body(*refs):
        ins, outs = refs[:n_seq], refs[n_seq:]
        for r in range(n_seq):
            for tensor in range(2):
                total = None
                for src in range(n_seq):
                    if src == r:
                        continue
                    block = (src ^ r) - 1
                    term = ins[src][tensor, block * slots : (block + 1) * slots, :].astype(F32)
                    total = term if total is None else total + term
                outs[r][tensor] = total.astype(BF16)

    slot_grad = sds((2, slots, wide), BF16)
    slot_grads = whole_call(
        slots_body, (slot_grad,) * n_seq, parts[0], *parts_recv, after=(gain_q,), micros=0.3
    )
    slots_recv = to_peers("seq", slot_grads[1:])

    def weights_body(ids_ref, kn_ref, vp_ref, *rest):
        gm = rest[:n_seq]
        row_refs = rest[n_seq : 2 * n_seq - 1]
        same_ref, other_ref = rest[2 * n_seq - 1 :]
        here = pl.ds(pl.multiple_of(ids_ref[0] * wide, wide), wide)
        own = (kn_ref[:, here], vp_ref[:, here])
        first = ids_ref[1] == 0
        for i in range(hp):
            at = slice(i * HD, (i + 1) * HD)
            for j in range(KS):
                span = slice(j * slots, (j + 1) * slots)
                found = []
                for tensor in range(2):
                    lhs = jnp.concatenate(
                        [own[tensor][span, at]] + [ref[tensor, span, at] for ref in row_refs],
                        axis=0,
                    )
                    rhs = jnp.concatenate([ref[tensor, :, at] for ref in gm], axis=0)
                    found.append(dot(lhs, rhs, TN))
                to = slice((i * KS + j) * HD, (i * KS + j + 1) * HD)
                same_ref[to, :] = jnp.where(first, found[0], found[1])
                other_ref[to, :] = jnp.where(first, found[1], found[0]).astype(BF16)

    span_rows = hp * KS * HD
    w_same, w_other = whole_call(
        weights_body,
        (sds((span_rows, HD), F32), sds((span_rows, HD), BF16)),
        ids, kn, vp, *slot_grads, *rows_recv,
        micros=1.1,
    )
    w_recv = to_core(w_other)

    def chunk_body(a_ref, b_ref, gq_ref, gk_ref, out_ref):
        out_ref[:span_rows, :] = (a_ref[...] + b_ref[...].astype(F32)).astype(BF16)
        gains = jnp.concatenate([gq_ref[...], gk_ref[...]], axis=0)
        out_ref[span_rows:, :] = gains.astype(BF16)

    chunk_shape = sds((span_rows + 2 * heads, HD), BF16)
    chunk = whole_call(chunk_body, chunk_shape, w_same, w_recv, gain_q, gain_k, micros=0.3)
    chunks = [chunk] + to_peers("seq", [chunk] * (n_seq - 1))

    def send_out(buffer, target, sems, index, at):
        copy = pltpu.make_async_copy(buffer.at[:, at], target.at[:, at], sems.at[index])
        copy.start()
        return copy

    def column_out(body, outs, n_out, *ins, micros, after=()):
        skip = len(after)
        inside = pl.BlockSpec(memory_space=pltpu.VMEM)
        small = len(outs) - n_out
        return pl.pallas_call(
            lambda *refs: body(*refs[: len(ins)], *refs[len(ins) + skip :]),
            out_shape=outs,
            in_specs=[
                pl.BlockSpec(memory_space=pltpu.SMEM) if a.dtype == jnp.int32 else inside
                for a in ins
            ]
            + [pl.BlockSpec(memory_space=pl.ANY)] * skip,
            out_specs=(inside,) * small + (pl.BlockSpec(memory_space=pl.ANY),) * n_out,
            scratch_shapes=[pltpu.VMEM((rows, cols), BF16)] * n_out
            + [pltpu.SemaphoreType.DMA((n_out, n_seq))],
            compiler_params=pltpu.CompilerParams(vmem_limit_bytes=40 * 2**20),
            cost_estimate=cost_of(micros),
        )(*ins, *after)

    def back_body(ids_ref, gk_ref, gv_ref, kp_ref, wk_ref, wv_ref, kg_ref, dq_ref, *rest):
        gm = rest[:n_seq]
        gkn_ref, dots_ref, value_ref, buffer, sems = rest[n_seq:]
        unorder = row_order_back(rows)
        total = jnp.zeros((rows, HD), F32)
        copies = []
        for r in range(n_seq):
            block = ids_ref[0] ^ r
            for i in range(hp):
                narrow = slice(i * HD, (i + 1) * HD)
                h = block * hp + i
                at = pl.ds(pl.multiple_of(h * HD, HD), HD)
                sides = []
                for tensor, w_ref in ((0, wk_ref), (1, wv_ref)):
                    spread = dot(gm[r][tensor, :, narrow], w_ref[h], NT)
                    sides.append(
                        jnp.concatenate(
                            [spread[:, j * HD : (j + 1) * HD] for j in range(KS)], axis=0
                        )
                    )
                gkn = gk_ref[:, at] + sides[0]
                gkn_ref[:, at] = gkn
                total = total + gkn * kp_ref[:, at].astype(F32) * kg_ref[:, at]
                value = (gv_ref[:, at] + sides[1]).astype(BF16)
                buffer[:, at] = dot(unorder, value).astype(BF16)
            wide_at = pl.ds(pl.multiple_of(block * wide, wide), wide)
            copies.append(send_out(buffer, value_ref, sems.at[0], r, wide_at))
        dots_ref[0:1, :] = dq_ref[...]
        dots_ref[1:2, :] = lane_sum_row(total)
        for copy in copies:
            copy.wait()

    gkn, dots, grad_value = column_out(
        back_body,
        (wide_f32, two_rows, rows_shape),
        1,
        ids, gk_local, gv_local, kp, key_squeeze, value_squeeze, kg, dot_q,
        slot_grads[0], *slots_recv,
        micros=3.0,
        after=(chunk,),
    )
    dots_peers = to_peers("head", [dots] * (n_head - 1))

    def pack_body(*refs):
        for r in range(n_seq):
            refs[n_seq][r] = refs[r][...]

    packed_shape = sds((n_seq,) + chunk_shape.shape, BF16)
    packed = whole_call(pack_body, packed_shape, *chunks, micros=0.1, after=(dots_peers[0],))
    packed_other = to_core(packed)

    def norms_body(q_ref, kp_ref, gq_ref, gkn_ref, qg_ref, kg_ref, inv_ref, *rest):
        dot_refs = rest[:n_head]
        out_q, out_k, buffer_q, buffer_k, sems = rest[n_head:]
        total = dot_refs[0][...]
        for other in dot_refs[1:]:
            total = total + other[...]
        inv_rows = inv_ref[...]
        inv_c = as_columns(inv_rows)
        pull = as_columns(inv_rows * inv_rows * inv_rows * total / full_width)
        unorder = row_order_back(rows)
        copies = []
        for r in range(n_seq):
            at = slice(r * wide, (r + 1) * wide)
            buffer_q[:, at] = (
                inv_c[:, 0:1] * qg_ref[:, at] * gq_ref[:, at]
                - q_ref[:, at].astype(F32) * pull[:, 0:1]
            ).astype(BF16)
            copies.append(send_out(buffer_q, out_q, sems.at[0], r, at))
            grad_k = (
                inv_c[:, 1:2] * kg_ref[:, at] * gkn_ref[:, at]
                - kp_ref[:, at].astype(F32) * pull[:, 1:2]
            ).astype(BF16)
            buffer_k[:, at] = dot(unorder, grad_k).astype(BF16)
            copies.append(send_out(buffer_k, out_k, sems.at[1], r, at))
        for copy in copies:
            copy.wait()

    grad_query, grad_key = column_out(
        norms_body,
        (rows_shape, rows_shape),
        2,
        q, kp, gq, gkn, qg, kg, inv, dots, *dots_peers,
        micros=2.0,
    )

    def finish_body(ids_ref, kg_ref, wk_ref, same, other, *rest):
        gq_ref, gk_ref, gks_ref, gvs_ref, buffer_k, buffer_v, sems = rest
        first = ids_ref[1] == 0
        parts = same[0, span_rows:, :].astype(F32) + other[0, span_rows:, :].astype(F32)
        for r in peers:
            parts += same[r, span_rows:, :].astype(F32) + other[r, span_rows:, :].astype(F32)
        gq_ref[...] = parts[:heads]
        gk_ref[...] = parts[heads:]
        copies = []
        for r in range(n_seq):
            start = (ids_ref[0] ^ r) * hp
            for i in range(hp):
                h = start + i
                span = slice(i * KS * HD, (i + 1) * KS * HD)
                a = same[r, span, :].astype(F32)
                b = other[r, span, :].astype(F32)
                grad_w = jnp.where(first, a, b)
                buffer_k[h] = grad_w
                buffer_v[h] = jnp.where(first, b, a)
                prod = grad_w * wk_ref[h].astype(F32)
                total = prod[:HD]
                for j in range(1, KS):
                    total = total + prod[j * HD : (j + 1) * HD]
                row = lane_sum_row(total)
                at = pl.ds(h, 1)
                gain = kg_ref[:, pl.ds(pl.multiple_of(h * HD, HD), HD)]
                gk_ref[at, :] = gk_ref[at, :] + row / gain
            for tensor, (buffer, target) in enumerate(((buffer_k, gks_ref), (buffer_v, gvs_ref))):
                at = pl.ds(start, hp)
                copy = pltpu.make_async_copy(buffer.at[at], target.at[at], sems.at[tensor, r])
                copy.start()
                copies.append(copy)
        for copy in copies:
            copy.wait()

    kernel_out = sds((heads, KS * HD, HD), F32)
    gains_shape = sds((heads, HD), F32)
    inside = pl.BlockSpec(memory_space=pltpu.VMEM)
    outside = pl.BlockSpec(memory_space=pl.ANY)
    gain_q_all, gain_k_all, gks, gvs = pl.pallas_call(
        finish_body,
        out_shape=(gains_shape, gains_shape, kernel_out, kernel_out),
        in_specs=[pl.BlockSpec(memory_space=pltpu.SMEM)] + [inside] * 4,
        out_specs=(inside, inside, outside, outside),
        scratch_shapes=[pltpu.VMEM(kernel_out.shape, F32)] * 2
        + [pltpu.SemaphoreType.DMA((2, n_seq))],
        compiler_params=pltpu.CompilerParams(vmem_limit_bytes=40 * 2**20),
        cost_estimate=cost_of(3.0),
    )(ids, kg, key_squeeze, packed, packed_other)
    return (
        grad_query[None],
        grad_key[None],
        grad_value[None],
        gain_q_all.reshape(cols),
        gain_k_all.reshape(cols),
        gks,
        gvs,
    )


def solution(mesh):
    placed = (
        P("dp", "seq", "head"),
        P("dp", "seq", "head"),
        P("dp", "seq", "head"),
        P("head"),
        P("head"),
        P("head", None, None),
        P("head", None, None),
        P("dp", "seq", "head"),
    )
    return jax.shard_map(
        on_device,
        mesh=mesh,
        in_specs=placed,
        out_specs=(
            P("dp", "seq", "head"),
            P("dp", "seq", "head"),
            P("dp", "seq", "head"),
            P("head"),
            P("head"),
            P("head", None, None),
            P("head", None, None),
        ),
        check_vma=False,
    )
```

```python
import jax
import jax.numpy as jnp
from jax import lax
from jax.experimental import pallas as pl
from jax.experimental.pallas import tpu as pltpu
from jax.sharding import PartitionSpec as P

HD = 128
KS = 4
HH = 4096


epsilon = 1e-06


def unfold_slots(source, head_count):
    batch_size, row_count, widths = source.shape
    return (
        source.reshape(batch_size, row_count // KS, KS, head_count, HD)
        .transpose(0, 1, 3, 2, 4)
        .reshape(batch_size, row_count // KS, head_count, KS * HD)
    )


def fold_slots(source):
    batch_size, slot_count, head_count, spans = source.shape
    return (
        source.reshape(batch_size, slot_count, head_count, KS, HD)
        .transpose(0, 1, 3, 2, 4)
        .reshape(batch_size, slot_count * KS, head_count * HD)
    )


def on_device_any(
    query_heads, key_heads, value_heads, query_gain, key_gain, key_squeeze, value_squeeze, grad_out
):
    batch_size, row_count, widths = query_heads.shape
    head_count = widths // HD
    slot_count = row_count // KS
    score_scale = HD ** (-0.5)
    own_limit = lax.axis_index("seq") * slot_count
    q_full = query_heads.astype(jnp.float32)
    k_full = key_heads.astype(jnp.float32)
    sum_q, sum_k = lax.psum((jnp.sum(q_full * q_full, -1), jnp.sum(k_full * k_full, -1)), "head")
    inv_q = lax.rsqrt(sum_q / HH + epsilon)[..., None]
    inv_k = lax.rsqrt(sum_k / HH + epsilon)[..., None]
    q_norm = (q_full * inv_q * query_gain).astype(jnp.bfloat16)
    k_norm = (k_full * inv_k * key_gain).astype(jnp.bfloat16)
    k_unf = unfold_slots(k_norm, head_count)
    v_unf = unfold_slots(value_heads, head_count)
    mem_k = (
        jnp.einsum("bmhc,hcd->bmhd", k_unf, key_squeeze, preferred_element_type=jnp.float32)
        .astype(jnp.bfloat16)
        .reshape(batch_size, slot_count, widths)
    )
    mem_v = (
        jnp.einsum("bmhc,hcd->bmhd", v_unf, value_squeeze, preferred_element_type=jnp.float32)
        .astype(jnp.bfloat16)
        .reshape(batch_size, slot_count, widths)
    )
    queries = q_norm.reshape(batch_size, row_count, head_count, HD)
    key_loc = k_norm.reshape(batch_size, row_count, head_count, HD)
    value_loc = value_heads.reshape(batch_size, row_count, head_count, HD)
    cotangent = grad_out.reshape(batch_size, row_count, head_count, HD)
    positions = jnp.arange(row_count)
    causal = positions[:, None] >= positions[None, :]
    scores_loc = jnp.where(
        causal,
        jnp.einsum("bthd,buhd->bhtu", queries, key_loc, preferred_element_type=jnp.float32)
        * score_scale,
        -jnp.inf,
    )
    grads_loc = jnp.einsum(
        "bthd,buhd->bhtu", cotangent, value_loc, preferred_element_type=jnp.float32
    )
    all_k, all_v = (
        lax.all_gather(mem_k, "seq", axis=1, tiled=True),
        lax.all_gather(mem_v, "seq", axis=1, tiled=True),
    )
    piece_rows = all_k.shape[1]
    key_rows = all_k.reshape(batch_size, piece_rows, head_count, HD)
    value_rows = all_v.reshape(batch_size, piece_rows, head_count, HD)
    allowed = jnp.arange(piece_rows) < own_limit
    scores = jnp.where(
        allowed,
        jnp.einsum("bthd,buhd->bhtu", queries, key_rows, preferred_element_type=jnp.float32)
        * score_scale,
        -jnp.inf,
    )
    gradients = jnp.einsum(
        "bthd,buhd->bhtu", cotangent, value_rows, preferred_element_type=jnp.float32
    )
    key_rows, scores_mem, grads_mem = (key_rows, scores, gradients)
    peak = jnp.maximum(jnp.max(scores_loc, -1), jnp.max(scores_mem, -1))
    summed = jnp.sum(jnp.exp(scores_loc - peak[..., None]), -1) + jnp.sum(
        jnp.exp(scores_mem - peak[..., None]), -1
    )
    log_mass = peak + jnp.log(summed)
    row_delta = jnp.sum(jnp.exp(scores_loc - log_mass[..., None]) * grads_loc, -1) + jnp.sum(
        jnp.exp(scores_mem - log_mass[..., None]) * grads_mem, -1
    )
    piece_rows = key_rows.shape[1]
    attend = jnp.exp(scores_mem - log_mass[..., None])
    d_scores = (attend * (grads_mem - row_delta[..., None])).astype(jnp.bfloat16)
    grad_q = score_scale * jnp.einsum(
        "bhtu,buhd->bthd", d_scores, key_rows, preferred_element_type=jnp.float32
    )
    grad_k = score_scale * jnp.einsum(
        "bhtu,bthd->buhd", d_scores, queries, preferred_element_type=jnp.float32
    )
    grad_v = jnp.einsum(
        "bhtu,bthd->buhd",
        attend.astype(jnp.bfloat16),
        cotangent,
        preferred_element_type=jnp.float32,
    )
    stacked = jnp.stack(
        (
            grad_k.reshape(batch_size, piece_rows, widths),
            grad_v.reshape(batch_size, piece_rows, widths),
        )
    )
    attend_loc = jnp.exp(scores_loc - log_mass[..., None])
    d_loc = (attend_loc * (grads_loc - row_delta[..., None])).astype(jnp.bfloat16)
    grad_qn = (
        score_scale
        * jnp.einsum("bhtu,buhd->bthd", d_loc, key_loc, preferred_element_type=jnp.float32)
        + grad_q
    ).reshape(batch_size, row_count, widths)
    grad_kn_local = score_scale * jnp.einsum(
        "bhtu,bthd->buhd", d_loc, queries, preferred_element_type=jnp.float32
    )
    grad_v_local = jnp.einsum(
        "bhtu,bthd->buhd",
        attend_loc.astype(jnp.bfloat16),
        cotangent,
        preferred_element_type=jnp.float32,
    )
    mine = lax.psum_scatter(stacked.astype(jnp.bfloat16), "seq", scatter_dimension=2, tiled=True)
    grad_mem_k = mine[0].reshape(batch_size, slot_count, head_count, HD)
    grad_mem_v = mine[1].reshape(batch_size, slot_count, head_count, HD)
    squeeze_k_part = jnp.einsum(
        "bmhc,bmhd->hcd", k_unf, grad_mem_k, preferred_element_type=jnp.float32
    )
    squeeze_v_part = jnp.einsum(
        "bmhc,bmhd->hcd", v_unf, grad_mem_v, preferred_element_type=jnp.float32
    )
    back_k = fold_slots(
        jnp.einsum("bmhd,hcd->bmhc", grad_mem_k, key_squeeze, preferred_element_type=jnp.float32)
    )
    back_v = fold_slots(
        jnp.einsum("bmhd,hcd->bmhc", grad_mem_v, value_squeeze, preferred_element_type=jnp.float32)
    )
    grad_kn = grad_kn_local.reshape(batch_size, row_count, widths) + back_k
    grad_value = (grad_v_local.reshape(batch_size, row_count, widths) + back_v).astype(jnp.bfloat16)
    dot_q, dot_k = lax.psum(
        (jnp.sum(query_gain * grad_qn * q_full, -1), jnp.sum(key_gain * grad_kn * k_full, -1)),
        "head",
    )
    grad_query = (
        inv_q * query_gain * grad_qn - q_full * inv_q**3 * dot_q[..., None] / HH
    ).astype(jnp.bfloat16)
    grad_key = (inv_k * key_gain * grad_kn - k_full * inv_k**3 * dot_k[..., None] / HH).astype(
        jnp.bfloat16
    )
    gain_q_part = jnp.sum(grad_qn * q_full * inv_q, (0, 1))
    gain_k_part = jnp.sum(grad_kn * k_full * inv_k, (0, 1))
    grad_query_gain, grad_key_gain, grad_key_squeeze, grad_value_squeeze = (
        lax.psum(gain_q_part.astype(jnp.bfloat16), ("seq", "dp")).astype(jnp.float32),
        lax.psum(gain_k_part.astype(jnp.bfloat16), ("seq", "dp")).astype(jnp.float32),
        lax.psum(squeeze_k_part.astype(jnp.bfloat16), ("seq", "dp")).astype(jnp.float32),
        lax.psum(squeeze_v_part.astype(jnp.bfloat16), ("seq", "dp")).astype(jnp.float32),
    )
    return (
        grad_query,
        grad_key,
        grad_value,
        grad_query_gain,
        grad_key_gain,
        grad_key_squeeze,
        grad_value_squeeze,
    )


F32 = jnp.float32
BF16 = jnp.bfloat16
NN = (((1,), (0,)), ((), ()))
NT = (((1,), (1,)), ((), ()))
TN = (((0,), (0,)), ((), ()))


def dot(a, b, dims=NN):
    return lax.dot_general(a, b, dims, preferred_element_type=F32)


def sds(shape, dtype):
    return jax.ShapeDtypeStruct(shape, dtype)


def cost_of(micros):
    return pl.CostEstimate(
        flops=int(micros * 1e9), bytes_accessed=int(micros * 3.6e6), transcendentals=0
    )


def whole_call(body, outs, *ins, micros=1.0, after=(), scratch=(), vmem=40):
    n_out = len(jax.tree.leaves(outs))
    skip = len(after)
    space = pl.BlockSpec(memory_space=pltpu.VMEM)
    return pl.pallas_call(
        lambda *refs: body(*refs[: len(ins)], *refs[len(ins) + skip :]),
        out_shape=outs,
        in_specs=[
            pl.BlockSpec(memory_space=pltpu.SMEM) if a.dtype == jnp.int32 else space for a in ins
        ]
        + [pl.BlockSpec(memory_space=pl.ANY)] * skip,
        out_specs=jax.tree.map(lambda _: space, outs),
        scratch_shapes=list(scratch),
        compiler_params=pltpu.CompilerParams(vmem_limit_bytes=vmem * 2**20),
        cost_estimate=cost_of(micros),
    )(*ins, *after)


def row_order(rows):
    slots = rows // KS
    r = lax.broadcasted_iota(jnp.int32, (rows, rows), 0)
    c = lax.broadcasted_iota(jnp.int32, (rows, rows), 1)
    return jnp.where(c == KS * (r % slots) + r // slots, 1.0, 0.0).astype(BF16)


def row_order_back(rows):
    slots = rows // KS
    r = lax.broadcasted_iota(jnp.int32, (rows, rows), 0)
    c = lax.broadcasted_iota(jnp.int32, (rows, rows), 1)
    return jnp.where(r == KS * (c % slots) + c // slots, 1.0, 0.0).astype(BF16)


def causal_t(rows):
    slots = rows // KS
    u = lax.broadcasted_iota(jnp.int32, (rows, rows), 0)
    t = lax.broadcasted_iota(jnp.int32, (rows, rows), 1)
    return KS * (u % slots) + u // slots <= t


def fold_lanes(x):
    total = x[:, :HD]
    for i in range(1, x.shape[1] // HD):
        total = total + x[:, i * HD : (i + 1) * HD]
    return total


def lane_sum_row(x):
    return jnp.sum(x.T, axis=0, keepdims=True)


def as_columns(rows):
    pad = jnp.zeros((8 - rows.shape[0], rows.shape[1]), F32)
    return jnp.concatenate([rows, pad], axis=0).T


def on_device(
    query_heads, key_heads, value_heads, query_gain, key_gain, key_squeeze, value_squeeze, grad_out
):
    n_seq, n_head = lax.axis_size("seq"), lax.axis_size("head")
    batch_size, rows, cols = query_heads.shape
    heads = cols // HD
    if batch_size != 1 or n_seq & (n_seq - 1) or heads % n_seq or lax.axis_size("dp") != 2:
        return on_device_any(
            query_heads,
            key_heads,
            value_heads,
            query_gain,
            key_gain,
            key_squeeze,
            value_squeeze,
            grad_out,
        )
    slots = rows // KS
    hp = heads // n_seq
    wide = hp * HD
    mem_rows = n_seq * slots
    peers = range(1, n_seq)
    n_mem = (n_seq - 1) * slots
    scale = HD ** (-0.5)
    full_width = cols * n_head
    me = lax.axis_index("seq")
    core = lax.axis_index("dp")
    ids = jnp.stack([me, core]).astype(jnp.int32)

    def to_peers(axis, arrays):
        n = lax.axis_size(axis)
        return [
            lax.ppermute(a, axis, [(i, i ^ k) for i in range(n)])
            for k, a in zip(range(1, n), arrays)
        ]

    def sum_body(a_ref, b_ref, out_ref):
        out_ref[...] = a_ref[...] + b_ref[...]

    def over_heads(a, beside=()):
        step, got = 1, None
        while step < n_head:
            if got is not None:
                a = whole_call(sum_body, sds(a.shape, a.dtype), a, got, micros=0.1, after=beside)
            got = lax.ppermute(a, "head", [(i, i ^ step) for i in range(n_head)])
            step *= 2
        return a, got

    def to_core(a):
        return lax.ppermute(a, "dp", [(0, 1), (1, 0)])

    q = query_heads[0]
    k = key_heads[0]
    v = value_heads[0]
    do = grad_out[0]
    qg = query_gain.reshape(1, cols)
    kg = key_gain.reshape(1, cols)

    def squares_body(q_ref, k_ref, ss_ref):
        qf = q_ref[...].astype(F32)
        ss_ref[0:1, :] = lane_sum_row(fold_lanes(qf * qf))
        kf = k_ref[...].astype(F32)
        ss_ref[1:2, :] = lane_sum_row(fold_lanes(kf * kf))

    two_rows = sds((2, rows), F32)
    ss = whole_call(squares_body, two_rows, q, k, micros=1.5, vmem=62)
    ss_parts = [ss] + to_peers("head", [ss] * (n_head - 1))

    def compress(source, w_ref, out_ref):
        for h in range(heads):
            total = None
            for j in range(KS):
                part = dot(
                    source[j * slots : (j + 1) * slots, h * HD : (h + 1) * HD],
                    w_ref[h, j * HD : (j + 1) * HD, :],
                )
                total = part if total is None else total + part
            block = h // hp
            out_ref[
                block * slots : (block + 1) * slots, (h % hp) * HD : (h % hp + 1) * HD
            ] = total.astype(BF16)

    def values_body(v_ref, w_ref, vp_ref, mem_ref):
        vp_ref[...] = dot(row_order(rows), v_ref[...]).astype(BF16)
        compress(vp_ref, w_ref, mem_ref)

    rows_shape = sds((rows, cols), BF16)
    mem_shape = sds((mem_rows, wide), BF16)
    vp, mem_v = whole_call(
        values_body, (rows_shape, mem_shape), v, value_squeeze, micros=0.8
    )

    def keys_body(k_ref, kg_ref, w_ref, mem_v_ref, *rest):
        ss_refs = rest[:n_head]
        inv_ref, kn_ref, mem_ref = rest[n_head:]
        total = ss_refs[0][...]
        for other in ss_refs[1:]:
            total = total + other[...]
        natural = as_columns(lax.rsqrt(total / full_width + epsilon))
        order = row_order(rows)
        high = natural.astype(BF16)
        rest_1 = natural - high.astype(F32)
        middle = rest_1.astype(BF16)
        low = (rest_1 - middle.astype(F32)).astype(BF16)
        ordered = dot(order, high) + dot(order, middle) + dot(order, low)
        inv_c = jnp.concatenate([natural[:, 0:1], ordered[:, 1:2], natural[:, 2:]], axis=1)
        inv_ref[...] = inv_c.T[:2]
        normed = (k_ref[...].astype(F32) * natural[:, 1:2] * kg_ref[...]).astype(BF16)
        kn_ref[...] = dot(order, normed).astype(BF16)
        compress(kn_ref, w_ref, mem_ref.at[0])
        mem_ref[1] = mem_v_ref[...]

    mem_pair = sds((2, mem_rows, wide), BF16)
    inv, kn, mem = whole_call(
        keys_body,
        (two_rows, rows_shape, mem_pair),
        k, kg, key_squeeze, mem_v, *ss_parts,
        micros=1.5,
    )
    mem_recv = to_peers("seq", [mem] * (n_seq - 1))

    def local_body(q_ref, qg_ref, inv_ref, kn_ref, vp_ref, do_ref, qn_ref, st_ref):
        allowed = causal_t(rows)
        inv_c = as_columns(inv_ref[...])[:, 0:1]
        for h in range(heads):
            at = slice(h * HD, (h + 1) * HD)
            qn_h = (q_ref[:, at].astype(F32) * inv_c * qg_ref[:, at]).astype(BF16)
            qn_ref[:, at] = qn_h
            s = jnp.where(allowed, dot(kn_ref[:, at], qn_h, NT) * scale, -jnp.inf)
            g = dot(vp_ref[:, at], do_ref[:, at], NT)
            m = jnp.max(s, axis=0, keepdims=True)
            p = jnp.exp(s - m)
            st_ref[h, 0:1, :] = m
            st_ref[h, 1:2, :] = jnp.sum(p, axis=0, keepdims=True)
            st_ref[h, 2:3, :] = jnp.sum(p * g, axis=0, keepdims=True)

    stat_shape = sds((heads, 8, rows), F32)
    qn, stats = whole_call(
        local_body, (rows_shape, stat_shape), q, qg, inv, kn, vp, do, micros=0.5
    )

    def rows_body(ids_ref, kn_ref, vp_ref, k_ref, *outs):
        sends, kp_ref = outs[:-1], outs[-1]
        kp_ref[...] = dot(row_order(rows), k_ref[...]).astype(BF16)
        for r, send in zip(peers, sends):
            dest = ids_ref[0] ^ r
            at = pl.ds(pl.multiple_of(dest * wide, wide), wide)
            send[0] = kn_ref[:, at]
            send[1] = vp_ref[:, at]

    row_pair = sds((2, rows, wide), BF16)
    *row_sends, kp = whole_call(
        rows_body,
        (row_pair,) * (n_seq - 1) + (rows_shape,),
        ids, kn, vp, k,
        after=(stats,),
        micros=0.7,
    )
    rows_recv = to_peers("seq", row_sends)

    def memory_body(ids_ref, qn_ref, do_ref, st_ref, *rest):
        mem_refs = rest[: n_seq - 1]
        st2_ref, ds_ref = rest[n_seq - 1 : n_seq + 1]
        parts = rest[n_seq + 1 :]
        mine = ids_ref[0]
        for r in range(n_seq):
            block = mine ^ r
            span = pl.ds(pl.multiple_of(block * slots, slots), slots)
            for i in range(hp):
                at = slice(i * HD, (i + 1) * HD)
                h = block * hp + i
                wide_at = pl.ds(pl.multiple_of(h * HD, HD), HD)
                qn_h = qn_ref[:, wide_at]
                do_h = do_ref[:, wide_at]
                mk = jnp.concatenate([ref[0, span, at] for ref in mem_refs], axis=0)
                mv = jnp.concatenate([ref[1, span, at] for ref in mem_refs], axis=0)
                raw = dot(mk, qn_h, NT) * scale
                s = jnp.concatenate(
                    [
                        jnp.where((mine ^ src) < mine, raw[(src - 1) * slots : src * slots], -jnp.inf)
                        for src in peers
                    ],
                    axis=0,
                )
                g = dot(mv, do_h, NT)
                stat = st_ref[h]
                m_loc, l_loc, d_loc = stat[0:1], stat[1:2], stat[2:3]
                m = jnp.maximum(m_loc, jnp.max(s, axis=0, keepdims=True))
                p = jnp.exp(s - m)
                shrink = jnp.exp(m_loc - m)
                mass = l_loc * shrink + jnp.sum(p, axis=0, keepdims=True)
                inv_mass = 1.0 / mass
                delta = (d_loc * shrink + jnp.sum(p * g, axis=0, keepdims=True)) * inv_mass
                st2_ref[h] = jnp.concatenate([m, inv_mass, delta, stat[3:]], axis=0)
                attend = p * inv_mass
                ds = (attend * (g - delta)).astype(BF16)
                ds_ref[h] = ds
                parts[r][0, :, at] = (dot(ds, qn_h) * scale).astype(BF16)
                parts[r][1, :, at] = dot(attend.astype(BF16), do_h).astype(BF16)

    part = sds((2, n_mem, wide), BF16)
    stats2, ds_mem, *parts = whole_call(
        memory_body,
        (stat_shape, sds((heads, n_mem, rows), BF16)) + (part,) * n_seq,
        ids, qn, do, stats, *mem_recv,
        micros=0.5,
    )
    parts_recv = to_peers("seq", parts[1:])

    def grads_body(q_ref, kp_ref, qn_ref, kn_ref, vp_ref, do_ref, st_ref, ds_ref, *rest):
        mem_refs = rest[: n_seq - 1]
        inv_ref, qg_ref, gq_ref, gk_ref, gv_ref, dq_ref, gain_q_ref, gain_k_ref = rest[n_seq - 1 :]
        allowed = causal_t(rows)
        inv_c = as_columns(inv_ref[...])
        total = jnp.zeros((rows, HD), F32)
        for h in range(heads):
            at = slice(h * HD, (h + 1) * HD)
            narrow = slice((h % hp) * HD, (h % hp + 1) * HD)
            span = slice((h // hp) * slots, (h // hp + 1) * slots)
            qn_h, kn_h, do_h = qn_ref[:, at], kn_ref[:, at], do_ref[:, at]
            s = jnp.where(allowed, dot(kn_h, qn_h, NT) * scale, -jnp.inf)
            g = dot(vp_ref[:, at], do_h, NT)
            m, inv_mass, delta = st_ref[h, 0:1, :], st_ref[h, 1:2, :], st_ref[h, 2:3, :]
            attend = jnp.exp(s - m) * inv_mass
            ds = (attend * (g - delta)).astype(BF16)
            mk = jnp.concatenate([ref[0, span, narrow] for ref in mem_refs], axis=0)
            gq = scale * (dot(ds, kn_h, TN) + dot(ds_ref[h], mk, TN))
            gk = scale * dot(ds, qn_h)
            gq_ref[:, at] = gq
            gk_ref[:, at] = gk
            gv_ref[:, at] = dot(attend.astype(BF16), do_h)
            gq_q = gq * q_ref[:, at].astype(F32)
            gk_k = gk * kp_ref[:, at].astype(F32)
            total = total + gq_q * qg_ref[:, at]
            gain_q_ref[h : h + 1, :] = jnp.sum(gq_q * inv_c[:, 0:1], axis=0, keepdims=True)
            gain_k_ref[h : h + 1, :] = jnp.sum(gk_k * inv_c[:, 1:2], axis=0, keepdims=True)
        dq_ref[...] = lane_sum_row(total)

    gain_rows = sds((heads, HD), F32)
    wide_f32 = sds((rows, cols), F32)
    dot_row = sds((1, rows), F32)
    gq, gk_local, gv_local, dot_q, gain_q, gain_k = whole_call(
        grads_body,
        (wide_f32, wide_f32, wide_f32, dot_row, gain_rows, gain_rows),
        q, kp, qn, kn, vp, do, stats2, ds_mem, *mem_recv, inv, qg,
        micros=0.5,
        after=tuple(rows_recv),
    )

    def slots_body(*refs):
        ins, outs = refs[:n_seq], refs[n_seq:]
        for r in range(n_seq):
            for tensor in range(2):
                total = None
                for src in range(n_seq):
                    if src == r:
                        continue
                    block = (src ^ r) - 1
                    term = ins[src][tensor, block * slots : (block + 1) * slots, :].astype(F32)
                    total = term if total is None else total + term
                outs[r][tensor] = total.astype(BF16)

    slot_grad = sds((2, slots, wide), BF16)
    slot_grads = whole_call(
        slots_body, (slot_grad,) * n_seq, parts[0], *parts_recv, after=(gain_q,), micros=0.3
    )

    slots_recv = to_peers("seq", slot_grads[1:])

    def weights_body(ids_ref, kn_ref, vp_ref, *rest):
        gm = rest[:n_seq]
        row_refs = rest[n_seq : 2 * n_seq - 1]
        same_ref, other_ref = rest[2 * n_seq - 1 :]
        here = pl.ds(pl.multiple_of(ids_ref[0] * wide, wide), wide)
        own = (kn_ref[:, here], vp_ref[:, here])
        first = ids_ref[1] == 0
        for i in range(hp):
            at = slice(i * HD, (i + 1) * HD)
            for j in range(KS):
                span = slice(j * slots, (j + 1) * slots)
                found = []
                for tensor in range(2):
                    lhs = jnp.concatenate(
                        [own[tensor][span, at]] + [ref[tensor, span, at] for ref in row_refs],
                        axis=0,
                    )
                    rhs = jnp.concatenate([ref[tensor, :, at] for ref in gm], axis=0)
                    found.append(dot(lhs, rhs, TN))
                to = slice((i * KS + j) * HD, (i * KS + j + 1) * HD)
                same_ref[to, :] = jnp.where(first, found[0], found[1])
                other_ref[to, :] = jnp.where(first, found[1], found[0]).astype(BF16)

    span_rows = hp * KS * HD
    w_same, w_other = whole_call(
        weights_body,
        (sds((span_rows, HD), F32), sds((span_rows, HD), BF16)),
        ids, kn, vp, *slot_grads, *rows_recv,
        micros=1.1,
    )
    w_recv = to_core(w_other)

    def chunk_body(a_ref, b_ref, gq_ref, gk_ref, out_ref):
        out_ref[:span_rows, :] = (a_ref[...] + b_ref[...].astype(F32)).astype(BF16)
        gains = jnp.concatenate([gq_ref[...], gk_ref[...]], axis=0)
        out_ref[span_rows:, :] = gains.astype(BF16)

    chunk_shape = sds((span_rows + 2 * heads, HD), BF16)
    chunk = whole_call(chunk_body, chunk_shape, w_same, w_recv, gain_q, gain_k, micros=0.3)
    chunks = to_peers("seq", [chunk] * (n_seq - 1))
    chunk_other = to_core(chunk)

    def send_out(buffer, target, sems, index, at):
        copy = pltpu.make_async_copy(buffer.at[:, at], target.at[:, at], sems.at[index])
        copy.start()
        return copy

    def column_out(body, outs, n_out, *ins, micros, after=()):
        skip = len(after)
        inside = pl.BlockSpec(memory_space=pltpu.VMEM)
        small = len(outs) - n_out
        return pl.pallas_call(
            lambda *refs: body(*refs[: len(ins)], *refs[len(ins) + skip :]),
            out_shape=outs,
            in_specs=[
                pl.BlockSpec(memory_space=pltpu.SMEM) if a.dtype == jnp.int32 else inside
                for a in ins
            ]
            + [pl.BlockSpec(memory_space=pl.ANY)] * skip,
            out_specs=(inside,) * small + (pl.BlockSpec(memory_space=pl.ANY),) * n_out,
            scratch_shapes=[pltpu.VMEM((rows, cols), BF16)] * n_out
            + [pltpu.SemaphoreType.DMA((n_out, n_seq))],
            compiler_params=pltpu.CompilerParams(vmem_limit_bytes=40 * 2**20),
            cost_estimate=cost_of(micros),
        )(*ins, *after)

    def spread_back(gm, w):
        wide_rows = dot(gm, w, NT)
        return jnp.concatenate([wide_rows[:, j * HD : (j + 1) * HD] for j in range(KS)], axis=0)

    def head_places(mine):
        for r in range(n_seq):
            for i in range(hp):
                h = (mine ^ r) * hp + i
                narrow = slice(i * HD, (i + 1) * HD)
                yield r, i, h, narrow, pl.ds(pl.multiple_of(h * HD, HD), HD)

    def back_keys_body(ids_ref, gk_ref, kp_ref, wk_ref, kg_ref, dq_ref, *rest):
        gm = rest[:n_seq]
        gkn_ref, dots_ref = rest[n_seq:]
        total = jnp.zeros((rows, HD), F32)
        for r, i, h, narrow, at in head_places(ids_ref[0]):
            gkn = gk_ref[:, at] + spread_back(gm[r][0, :, narrow], wk_ref[h])
            gkn_ref[:, at] = gkn
            total = total + gkn * kp_ref[:, at].astype(F32) * kg_ref[:, at]
        dots_ref[0:1, :] = dq_ref[...]
        dots_ref[1:2, :] = lane_sum_row(total)

    gkn, dots = whole_call(
        back_keys_body,
        (wide_f32, two_rows),
        ids, gk_local, kp, key_squeeze, kg, dot_q, slot_grads[0], *slots_recv,
        micros=2.0,
        after=(chunk,),
    )

    def back_values_body(ids_ref, gv_ref, wv_ref, *rest):
        gm = rest[:n_seq]
        mark_ref, value_ref, buffer, sems = rest[n_seq:]
        mark_ref[...] = jnp.zeros_like(mark_ref)
        unorder = row_order_back(rows)
        copies = []
        for r, i, h, narrow, at in head_places(ids_ref[0]):
            value = gv_ref[:, at] + spread_back(gm[r][1, :, narrow], wv_ref[h])
            buffer[:, at] = dot(unorder, value.astype(BF16)).astype(BF16)
            if i == hp - 1:
                block = ids_ref[0] ^ r
                wide_at = pl.ds(pl.multiple_of(block * wide, wide), wide)
                copies.append(send_out(buffer, value_ref, sems.at[0], r, wide_at))
        for copy in copies:
            copy.wait()

    mark, grad_value = column_out(
        back_values_body,
        (sds((8, HD), F32), rows_shape),
        1,
        ids, gv_local, value_squeeze, slot_grads[0], *slots_recv,
        micros=2.0,
        after=(dots,),
    )
    dots_parts = over_heads(dots, beside=(mark,))

    def norms_body(q_ref, kp_ref, gq_ref, gkn_ref, qg_ref, kg_ref, inv_ref, *rest):
        dots_a, dots_b, out_q, out_k, buffer_q, buffer_k, sems = rest
        total = dots_a[...] + dots_b[...]
        inv_rows = inv_ref[...]
        inv_c = as_columns(inv_rows)
        pull = as_columns(inv_rows * inv_rows * inv_rows * total / full_width)
        unorder = row_order_back(rows)
        copies = []
        for r in range(n_seq):
            at = slice(r * wide, (r + 1) * wide)
            buffer_q[:, at] = (
                inv_c[:, 0:1] * qg_ref[:, at] * gq_ref[:, at]
                - q_ref[:, at].astype(F32) * pull[:, 0:1]
            ).astype(BF16)
            copies.append(send_out(buffer_q, out_q, sems.at[0], r, at))
            grad_k = (
                inv_c[:, 1:2] * kg_ref[:, at] * gkn_ref[:, at]
                - kp_ref[:, at].astype(F32) * pull[:, 1:2]
            ).astype(BF16)
            buffer_k[:, at] = dot(unorder, grad_k).astype(BF16)
            copies.append(send_out(buffer_k, out_k, sems.at[1], r, at))
        for copy in copies:
            copy.wait()

    grad_query, grad_key = column_out(
        norms_body,
        (rows_shape, rows_shape),
        2,
        q, kp, gq, gkn, qg, kg, inv, *dots_parts,
        micros=2.0,
    )

    kernel_out = sds((heads, KS * HD, HD), F32)
    gains_shape = sds((heads, HD), F32)

    def write_chunk(mine, r, read, buffer, sem, target):
        start = (mine ^ r) * hp
        for i in range(hp):
            buffer[start + i] = read(slice(i * KS * HD, (i + 1) * KS * HD)).astype(F32)
        at = pl.ds(start, hp)
        copy = pltpu.make_async_copy(buffer.at[at], target.at[at], sem)
        copy.start()
        return copy

    def own_chunk_body(ids_ref, same, other, *rest):
        mark_ref, gks_ref, gvs_ref, buffer_k, buffer_v, sems = rest
        mark_ref[...] = jnp.zeros_like(mark_ref)
        first = ids_ref[1] == 0
        copies = [
            write_chunk(
                ids_ref[0], 0, lambda at: jnp.where(first, same[at, :], other[at, :]),
                buffer_k, sems.at[0], gks_ref,
            ),
            write_chunk(
                ids_ref[0], 0, lambda at: jnp.where(first, other[at, :], same[at, :]),
                buffer_v, sems.at[1], gvs_ref,
            ),
        ]
        for copy in copies:
            copy.wait()

    smem = pl.BlockSpec(memory_space=pltpu.SMEM)
    inside = pl.BlockSpec(memory_space=pltpu.VMEM)
    outside = pl.BlockSpec(memory_space=pl.ANY)
    buffer = pltpu.VMEM(kernel_out.shape, F32)
    params = pltpu.CompilerParams(vmem_limit_bytes=40 * 2**20)
    own_mark, *part_written = pl.pallas_call(
        own_chunk_body,
        out_shape=(sds((8, HD), F32), kernel_out, kernel_out),
        in_specs=[smem, inside, inside],
        out_specs=(inside, outside, outside),
        scratch_shapes=[buffer, buffer, pltpu.SemaphoreType.DMA((2,))],
        compiler_params=params,
        cost_estimate=cost_of(1.2),
    )(ids, chunk, chunk_other)

    def pack_body(*refs):
        for r in range(n_seq - 1):
            refs[n_seq - 1][r] = refs[r][...]

    packed_shape = sds((n_seq - 1,) + chunk_shape.shape, BF16)
    packed = whole_call(pack_body, packed_shape, *chunks, micros=0.1, after=(dots_parts[1], own_mark))
    packed_other = to_core(packed)

    def this_core_body(ids_ref, same, gks_in, gvs_in, gks_ref, gvs_ref, buffer, sems):
        for tensor, target in enumerate((gks_ref, gvs_ref)):
            @pl.when(ids_ref[1] == tensor)
            def _(target=target):
                copies = [
                    write_chunk(
                        ids_ref[0], r, lambda at, r=r: same[r - 1, at, :],
                        buffer, sems.at[r], target,
                    )
                    for r in peers
                ]
                for copy in copies:
                    copy.wait()

    def other_core_body(ids_ref, same_0, other_0, same, other, kg_ref, wk_ref, *rest):
        gks_ref, gvs_ref, gq_ref, gk_ref, buffer, sems = rest[2:]
        first = ids_ref[1] == 0

        def pair(r, at):
            if r == 0:
                return same_0[at, :], other_0[at, :]
            return same[r - 1, at, :], other[r - 1, at, :]

        def gains():
            total = jnp.zeros((2 * heads, HD), F32)
            for r in range(n_seq):
                a, b = pair(r, slice(span_rows, span_rows + 2 * heads))
                total = total + a.astype(F32) + b.astype(F32)
            gq_ref[...] = total[:heads]
            gk_ref[...] = total[heads:]
            for r in range(n_seq):
                for i in range(hp):
                    h = (ids_ref[0] ^ r) * hp + i
                    total = jnp.zeros((HD, HD), F32)
                    for j in range(KS):
                        a, b = pair(r, slice((i * KS + j) * HD, (i * KS + j + 1) * HD))
                        kernel = wk_ref[h, j * HD : (j + 1) * HD, :]
                        total = total + jnp.where(first, a, b).astype(F32) * kernel.astype(F32)
                    at = pl.ds(h, 1)
                    gain = kg_ref[:, pl.ds(pl.multiple_of(h * HD, HD), HD)]
                    gk_ref[at, :] = gk_ref[at, :] + lane_sum_row(total) / gain

        for tensor, target in enumerate((gvs_ref, gks_ref)):
            @pl.when(ids_ref[1] == tensor)
            def _(target=target):
                copies = [
                    write_chunk(
                        ids_ref[0], r, lambda at, r=r: other[r - 1, at, :],
                        buffer, sems.at[r], target,
                    )
                    for r in peers
                ]
                gains()
                for copy in copies:
                    copy.wait()

    part_written = pl.pallas_call(
        this_core_body,
        out_shape=(kernel_out, kernel_out),
        in_specs=[smem, inside, outside, outside],
        out_specs=(outside, outside),
        input_output_aliases={2: 0, 3: 1},
        scratch_shapes=[buffer, pltpu.SemaphoreType.DMA((n_seq,))],
        compiler_params=params,
        cost_estimate=cost_of(1.6),
    )(ids, packed, *part_written)
    gks, gvs, gain_q_all, gain_k_all = pl.pallas_call(
        other_core_body,
        out_shape=(kernel_out, kernel_out, gains_shape, gains_shape),
        in_specs=[smem] + [inside] * 6 + [outside] * 2,
        out_specs=(outside, outside, inside, inside),
        input_output_aliases={7: 0, 8: 1},
        scratch_shapes=[buffer, pltpu.SemaphoreType.DMA((n_seq,))],
        compiler_params=params,
        cost_estimate=cost_of(2.2),
    )(ids, chunk, chunk_other, packed, packed_other, kg, key_squeeze, *part_written)
    return (
        grad_query[None],
        grad_key[None],
        grad_value[None],
        gain_q_all.reshape(cols),
        gain_k_all.reshape(cols),
        gks,
        gvs,
    )


def solution(mesh):
    placed = (
        P("dp", "seq", "head"),
        P("dp", "seq", "head"),
        P("dp", "seq", "head"),
        P("head"),
        P("head"),
        P("head", None, None),
        P("head", None, None),
        P("dp", "seq", "head"),
    )
    return jax.shard_map(
        on_device,
        mesh=mesh,
        in_specs=placed,
        out_specs=(
            P("dp", "seq", "head"),
            P("dp", "seq", "head"),
            P("dp", "seq", "head"),
            P("head"),
            P("head"),
            P("head", None, None),
            P("head", None, None),
        ),
        check_vma=False,
    )
```

```python
import jax
import jax.numpy as jnp
from jax import lax
from jax.experimental import pallas as pl
from jax.experimental.pallas import tpu as pltpu
from jax.sharding import PartitionSpec as P

HD = 128
KS = 4
HH = 4096


epsilon = 1e-06


def unfold_slots(source, head_count):
    batch_size, row_count, widths = source.shape
    return (
        source.reshape(batch_size, row_count // KS, KS, head_count, HD)
        .transpose(0, 1, 3, 2, 4)
        .reshape(batch_size, row_count // KS, head_count, KS * HD)
    )


def fold_slots(source):
    batch_size, slot_count, head_count, spans = source.shape
    return (
        source.reshape(batch_size, slot_count, head_count, KS, HD)
        .transpose(0, 1, 3, 2, 4)
        .reshape(batch_size, slot_count * KS, head_count * HD)
    )


def on_device_any(
    query_heads, key_heads, value_heads, query_gain, key_gain, key_squeeze, value_squeeze, grad_out
):
    batch_size, row_count, widths = query_heads.shape
    head_count = widths // HD
    slot_count = row_count // KS
    score_scale = HD ** (-0.5)
    own_limit = lax.axis_index("seq") * slot_count
    q_full = query_heads.astype(jnp.float32)
    k_full = key_heads.astype(jnp.float32)
    sum_q, sum_k = lax.psum((jnp.sum(q_full * q_full, -1), jnp.sum(k_full * k_full, -1)), "head")
    inv_q = lax.rsqrt(sum_q / HH + epsilon)[..., None]
    inv_k = lax.rsqrt(sum_k / HH + epsilon)[..., None]
    q_norm = (q_full * inv_q * query_gain).astype(jnp.bfloat16)
    k_norm = (k_full * inv_k * key_gain).astype(jnp.bfloat16)
    k_unf = unfold_slots(k_norm, head_count)
    v_unf = unfold_slots(value_heads, head_count)
    mem_k = (
        jnp.einsum("bmhc,hcd->bmhd", k_unf, key_squeeze, preferred_element_type=jnp.float32)
        .astype(jnp.bfloat16)
        .reshape(batch_size, slot_count, widths)
    )
    mem_v = (
        jnp.einsum("bmhc,hcd->bmhd", v_unf, value_squeeze, preferred_element_type=jnp.float32)
        .astype(jnp.bfloat16)
        .reshape(batch_size, slot_count, widths)
    )
    queries = q_norm.reshape(batch_size, row_count, head_count, HD)
    key_loc = k_norm.reshape(batch_size, row_count, head_count, HD)
    value_loc = value_heads.reshape(batch_size, row_count, head_count, HD)
    cotangent = grad_out.reshape(batch_size, row_count, head_count, HD)
    positions = jnp.arange(row_count)
    causal = positions[:, None] >= positions[None, :]
    scores_loc = jnp.where(
        causal,
        jnp.einsum("bthd,buhd->bhtu", queries, key_loc, preferred_element_type=jnp.float32)
        * score_scale,
        -jnp.inf,
    )
    grads_loc = jnp.einsum(
        "bthd,buhd->bhtu", cotangent, value_loc, preferred_element_type=jnp.float32
    )
    all_k, all_v = (
        lax.all_gather(mem_k, "seq", axis=1, tiled=True),
        lax.all_gather(mem_v, "seq", axis=1, tiled=True),
    )
    piece_rows = all_k.shape[1]
    key_rows = all_k.reshape(batch_size, piece_rows, head_count, HD)
    value_rows = all_v.reshape(batch_size, piece_rows, head_count, HD)
    allowed = jnp.arange(piece_rows) < own_limit
    scores = jnp.where(
        allowed,
        jnp.einsum("bthd,buhd->bhtu", queries, key_rows, preferred_element_type=jnp.float32)
        * score_scale,
        -jnp.inf,
    )
    gradients = jnp.einsum(
        "bthd,buhd->bhtu", cotangent, value_rows, preferred_element_type=jnp.float32
    )
    key_rows, scores_mem, grads_mem = (key_rows, scores, gradients)
    peak = jnp.maximum(jnp.max(scores_loc, -1), jnp.max(scores_mem, -1))
    summed = jnp.sum(jnp.exp(scores_loc - peak[..., None]), -1) + jnp.sum(
        jnp.exp(scores_mem - peak[..., None]), -1
    )
    log_mass = peak + jnp.log(summed)
    row_delta = jnp.sum(jnp.exp(scores_loc - log_mass[..., None]) * grads_loc, -1) + jnp.sum(
        jnp.exp(scores_mem - log_mass[..., None]) * grads_mem, -1
    )
    piece_rows = key_rows.shape[1]
    attend = jnp.exp(scores_mem - log_mass[..., None])
    d_scores = (attend * (grads_mem - row_delta[..., None])).astype(jnp.bfloat16)
    grad_q = score_scale * jnp.einsum(
        "bhtu,buhd->bthd", d_scores, key_rows, preferred_element_type=jnp.float32
    )
    grad_k = score_scale * jnp.einsum(
        "bhtu,bthd->buhd", d_scores, queries, preferred_element_type=jnp.float32
    )
    grad_v = jnp.einsum(
        "bhtu,bthd->buhd",
        attend.astype(jnp.bfloat16),
        cotangent,
        preferred_element_type=jnp.float32,
    )
    stacked = jnp.stack(
        (
            grad_k.reshape(batch_size, piece_rows, widths),
            grad_v.reshape(batch_size, piece_rows, widths),
        )
    )
    attend_loc = jnp.exp(scores_loc - log_mass[..., None])
    d_loc = (attend_loc * (grads_loc - row_delta[..., None])).astype(jnp.bfloat16)
    grad_qn = (
        score_scale
        * jnp.einsum("bhtu,buhd->bthd", d_loc, key_loc, preferred_element_type=jnp.float32)
        + grad_q
    ).reshape(batch_size, row_count, widths)
    grad_kn_local = score_scale * jnp.einsum(
        "bhtu,bthd->buhd", d_loc, queries, preferred_element_type=jnp.float32
    )
    grad_v_local = jnp.einsum(
        "bhtu,bthd->buhd",
        attend_loc.astype(jnp.bfloat16),
        cotangent,
        preferred_element_type=jnp.float32,
    )
    mine = lax.psum_scatter(stacked.astype(jnp.bfloat16), "seq", scatter_dimension=2, tiled=True)
    grad_mem_k = mine[0].reshape(batch_size, slot_count, head_count, HD)
    grad_mem_v = mine[1].reshape(batch_size, slot_count, head_count, HD)
    squeeze_k_part = jnp.einsum(
        "bmhc,bmhd->hcd", k_unf, grad_mem_k, preferred_element_type=jnp.float32
    )
    squeeze_v_part = jnp.einsum(
        "bmhc,bmhd->hcd", v_unf, grad_mem_v, preferred_element_type=jnp.float32
    )
    back_k = fold_slots(
        jnp.einsum("bmhd,hcd->bmhc", grad_mem_k, key_squeeze, preferred_element_type=jnp.float32)
    )
    back_v = fold_slots(
        jnp.einsum("bmhd,hcd->bmhc", grad_mem_v, value_squeeze, preferred_element_type=jnp.float32)
    )
    grad_kn = grad_kn_local.reshape(batch_size, row_count, widths) + back_k
    grad_value = (grad_v_local.reshape(batch_size, row_count, widths) + back_v).astype(jnp.bfloat16)
    dot_q, dot_k = lax.psum(
        (jnp.sum(query_gain * grad_qn * q_full, -1), jnp.sum(key_gain * grad_kn * k_full, -1)),
        "head",
    )
    grad_query = (
        inv_q * query_gain * grad_qn - q_full * inv_q**3 * dot_q[..., None] / HH
    ).astype(jnp.bfloat16)
    grad_key = (inv_k * key_gain * grad_kn - k_full * inv_k**3 * dot_k[..., None] / HH).astype(
        jnp.bfloat16
    )
    gain_q_part = jnp.sum(grad_qn * q_full * inv_q, (0, 1))
    gain_k_part = jnp.sum(grad_kn * k_full * inv_k, (0, 1))
    grad_query_gain, grad_key_gain, grad_key_squeeze, grad_value_squeeze = (
        lax.psum(gain_q_part.astype(jnp.bfloat16), ("seq", "dp")).astype(jnp.float32),
        lax.psum(gain_k_part.astype(jnp.bfloat16), ("seq", "dp")).astype(jnp.float32),
        lax.psum(squeeze_k_part.astype(jnp.bfloat16), ("seq", "dp")).astype(jnp.float32),
        lax.psum(squeeze_v_part.astype(jnp.bfloat16), ("seq", "dp")).astype(jnp.float32),
    )
    return (
        grad_query,
        grad_key,
        grad_value,
        grad_query_gain,
        grad_key_gain,
        grad_key_squeeze,
        grad_value_squeeze,
    )


F32 = jnp.float32
BF16 = jnp.bfloat16
NN = (((1,), (0,)), ((), ()))
NT = (((1,), (1,)), ((), ()))
TN = (((0,), (0,)), ((), ()))


def dot(a, b, dims=NN):
    return lax.dot_general(a, b, dims, preferred_element_type=F32)


def sds(shape, dtype):
    return jax.ShapeDtypeStruct(shape, dtype)


def cost_of(micros):
    return pl.CostEstimate(
        flops=int(micros * 1e9), bytes_accessed=int(micros * 3.6e6), transcendentals=0
    )


def whole_call(body, outs, *ins, micros=1.0, after=(), scratch=(), vmem=40):
    n_out = len(jax.tree.leaves(outs))
    skip = len(after)
    space = pl.BlockSpec(memory_space=pltpu.VMEM)
    return pl.pallas_call(
        lambda *refs: body(*refs[: len(ins)], *refs[len(ins) + skip :]),
        out_shape=outs,
        in_specs=[
            pl.BlockSpec(memory_space=pltpu.SMEM) if a.dtype == jnp.int32 else space for a in ins
        ]
        + [pl.BlockSpec(memory_space=pl.ANY)] * skip,
        out_specs=jax.tree.map(lambda _: space, outs),
        scratch_shapes=list(scratch),
        compiler_params=pltpu.CompilerParams(vmem_limit_bytes=vmem * 2**20),
        cost_estimate=cost_of(micros),
    )(*ins, *after)


def row_order(rows):
    slots = rows // KS
    r = lax.broadcasted_iota(jnp.int32, (rows, rows), 0)
    c = lax.broadcasted_iota(jnp.int32, (rows, rows), 1)
    return jnp.where(c == KS * (r % slots) + r // slots, 1.0, 0.0).astype(BF16)


def row_order_back(rows):
    slots = rows // KS
    r = lax.broadcasted_iota(jnp.int32, (rows, rows), 0)
    c = lax.broadcasted_iota(jnp.int32, (rows, rows), 1)
    return jnp.where(r == KS * (c % slots) + c // slots, 1.0, 0.0).astype(BF16)


def causal_t(rows):
    slots = rows // KS
    u = lax.broadcasted_iota(jnp.int32, (rows, rows), 0)
    t = lax.broadcasted_iota(jnp.int32, (rows, rows), 1)
    return KS * (u % slots) + u // slots <= t


def fold_lanes(x):
    total = x[:, :HD]
    for i in range(1, x.shape[1] // HD):
        total = total + x[:, i * HD : (i + 1) * HD]
    return total


def lane_sum_row(x):
    return jnp.sum(x.T, axis=0, keepdims=True)


def as_columns(rows):
    pad = jnp.zeros((8 - rows.shape[0], rows.shape[1]), F32)
    return jnp.concatenate([rows, pad], axis=0).T


def on_device(
    query_heads, key_heads, value_heads, query_gain, key_gain, key_squeeze, value_squeeze, grad_out
):
    n_seq, n_head = lax.axis_size("seq"), lax.axis_size("head")
    batch_size, rows, cols = query_heads.shape
    heads = cols // HD
    if batch_size != 1 or n_seq & (n_seq - 1) or heads % n_seq or lax.axis_size("dp") != 2:
        return on_device_any(
            query_heads,
            key_heads,
            value_heads,
            query_gain,
            key_gain,
            key_squeeze,
            value_squeeze,
            grad_out,
        )
    slots = rows // KS
    hp = heads // n_seq
    wide = hp * HD
    mem_rows = n_seq * slots
    peers = range(1, n_seq)
    n_mem = (n_seq - 1) * slots
    scale = HD ** (-0.5)
    full_width = cols * n_head
    me = lax.axis_index("seq")
    core = lax.axis_index("dp")
    ids = jnp.stack([me, core]).astype(jnp.int32)

    def to_peers(axis, arrays):
        n = lax.axis_size(axis)
        return [
            lax.ppermute(a, axis, [(i, i ^ k) for i in range(n)])
            for k, a in zip(range(1, n), arrays)
        ]

    def sum_body(a_ref, b_ref, out_ref):
        out_ref[...] = a_ref[...] + b_ref[...]

    def over_heads(a, beside=()):
        step, got = 1, None
        while step < n_head:
            if got is not None:
                a = whole_call(sum_body, sds(a.shape, a.dtype), a, got, micros=0.1, after=beside)
            got = lax.ppermute(a, "head", [(i, i ^ step) for i in range(n_head)])
            step *= 2
        return a, got

    def to_core(a):
        return lax.ppermute(a, "dp", [(0, 1), (1, 0)])

    q = query_heads[0]
    k = key_heads[0]
    v = value_heads[0]
    do = grad_out[0]
    qg = query_gain.reshape(1, cols)
    kg = key_gain.reshape(1, cols)

    def squares_body(q_ref, k_ref, ss_ref):
        qf = q_ref[...].astype(F32)
        ss_ref[0:1, :] = lane_sum_row(fold_lanes(qf * qf))
        kf = k_ref[...].astype(F32)
        ss_ref[1:2, :] = lane_sum_row(fold_lanes(kf * kf))

    two_rows = sds((2, rows), F32)
    ss = whole_call(squares_body, two_rows, q, k, micros=1.5, vmem=62)
    ss_parts = [ss] + to_peers("head", [ss] * (n_head - 1))

    def compress(source, w_ref, out_ref):
        for h in range(heads):
            total = None
            for j in range(KS):
                part = dot(
                    source[j * slots : (j + 1) * slots, h * HD : (h + 1) * HD],
                    w_ref[h, j * HD : (j + 1) * HD, :],
                )
                total = part if total is None else total + part
            block = h // hp
            out_ref[
                block * slots : (block + 1) * slots, (h % hp) * HD : (h % hp + 1) * HD
            ] = total.astype(BF16)

    def values_body(v_ref, w_ref, vp_ref, mem_ref):
        vp_ref[...] = dot(row_order(rows), v_ref[...]).astype(BF16)
        compress(vp_ref, w_ref, mem_ref)

    rows_shape = sds((rows, cols), BF16)
    mem_shape = sds((mem_rows, wide), BF16)
    vp, mem_v = whole_call(
        values_body, (rows_shape, mem_shape), v, value_squeeze, micros=0.8
    )
    mv_recv = to_peers("seq", [mem_v] * (n_seq - 1))

    def keys_body(k_ref, kg_ref, w_ref, *rest):
        ss_refs = rest[:n_head]
        inv_ref, kn_ref, mem_ref = rest[n_head:]
        total = ss_refs[0][...]
        for other in ss_refs[1:]:
            total = total + other[...]
        natural = as_columns(lax.rsqrt(total / full_width + epsilon))
        order = row_order(rows)
        high = natural.astype(BF16)
        rest_1 = natural - high.astype(F32)
        middle = rest_1.astype(BF16)
        low = (rest_1 - middle.astype(F32)).astype(BF16)
        ordered = dot(order, high) + dot(order, middle) + dot(order, low)
        inv_c = jnp.concatenate([natural[:, 0:1], ordered[:, 1:2], natural[:, 2:]], axis=1)
        inv_ref[...] = inv_c.T[:2]
        normed = (k_ref[...].astype(F32) * natural[:, 1:2] * kg_ref[...]).astype(BF16)
        kn_ref[...] = dot(order, normed).astype(BF16)
        compress(kn_ref, w_ref, mem_ref)

    inv, kn, mem = whole_call(
        keys_body,
        (two_rows, rows_shape, mem_shape),
        k, kg, key_squeeze, *ss_parts,
        micros=20.0,
    )
    mk_recv = to_peers("seq", [mem] * (n_seq - 1))

    def local_body(q_ref, qg_ref, inv_ref, kn_ref, vp_ref, do_ref, qn_ref, st_ref):
        allowed = causal_t(rows)
        inv_c = as_columns(inv_ref[...])[:, 0:1]
        for h in range(heads):
            at = slice(h * HD, (h + 1) * HD)
            qn_h = (q_ref[:, at].astype(F32) * inv_c * qg_ref[:, at]).astype(BF16)
            qn_ref[:, at] = qn_h
            s = jnp.where(allowed, dot(kn_ref[:, at], qn_h, NT) * scale, -jnp.inf)
            g = dot(vp_ref[:, at], do_ref[:, at], NT)
            m = jnp.max(s, axis=0, keepdims=True)
            p = jnp.exp(s - m)
            st_ref[h, 0:1, :] = m
            st_ref[h, 1:2, :] = jnp.sum(p, axis=0, keepdims=True)
            st_ref[h, 2:3, :] = jnp.sum(p * g, axis=0, keepdims=True)

    stat_shape = sds((heads, 8, rows), F32)
    qn, stats = whole_call(
        local_body, (rows_shape, stat_shape), q, qg, inv, kn, vp, do,
        micros=0.5,
        after=tuple(mv_recv),
    )

    def rows_body(ids_ref, kn_ref, vp_ref, k_ref, *outs):
        sends, kp_ref = outs[:-1], outs[-1]
        kp_ref[...] = dot(row_order(rows), k_ref[...]).astype(BF16)
        for r, send in zip(peers, sends):
            dest = ids_ref[0] ^ r
            at = pl.ds(pl.multiple_of(dest * wide, wide), wide)
            send[0] = kn_ref[:, at]
            send[1] = vp_ref[:, at]

    row_pair = sds((2, rows, wide), BF16)
    *row_sends, kp = whole_call(
        rows_body,
        (row_pair,) * (n_seq - 1) + (rows_shape,),
        ids, kn, vp, k,
        after=(stats,),
        micros=0.7,
    )
    rows_recv = to_peers("seq", row_sends)

    def memory_body(ids_ref, qn_ref, do_ref, st_ref, *rest):
        mk_refs = rest[: n_seq - 1]
        mv_refs = rest[n_seq - 1 : 2 * n_seq - 2]
        st2_ref, ds_ref = rest[2 * n_seq - 2 : 2 * n_seq]
        parts = rest[2 * n_seq :]
        mine = ids_ref[0]
        for r in range(n_seq):
            block = mine ^ r
            span = pl.ds(pl.multiple_of(block * slots, slots), slots)
            for i in range(hp):
                at = slice(i * HD, (i + 1) * HD)
                h = block * hp + i
                wide_at = pl.ds(pl.multiple_of(h * HD, HD), HD)
                qn_h = qn_ref[:, wide_at]
                do_h = do_ref[:, wide_at]
                mk = jnp.concatenate([ref[span, at] for ref in mk_refs], axis=0)
                mv = jnp.concatenate([ref[span, at] for ref in mv_refs], axis=0)
                raw = dot(mk, qn_h, NT) * scale
                s = jnp.concatenate(
                    [
                        jnp.where((mine ^ src) < mine, raw[(src - 1) * slots : src * slots], -jnp.inf)
                        for src in peers
                    ],
                    axis=0,
                )
                g = dot(mv, do_h, NT)
                stat = st_ref[h]
                m_loc, l_loc, d_loc = stat[0:1], stat[1:2], stat[2:3]
                m = jnp.maximum(m_loc, jnp.max(s, axis=0, keepdims=True))
                p = jnp.exp(s - m)
                shrink = jnp.exp(m_loc - m)
                mass = l_loc * shrink + jnp.sum(p, axis=0, keepdims=True)
                inv_mass = 1.0 / mass
                delta = (d_loc * shrink + jnp.sum(p * g, axis=0, keepdims=True)) * inv_mass
                st2_ref[h] = jnp.concatenate([m, inv_mass, delta, stat[3:]], axis=0)
                attend = p * inv_mass
                ds = (attend * (g - delta)).astype(BF16)
                ds_ref[h] = ds
                parts[r][0, :, at] = (dot(ds, qn_h) * scale).astype(BF16)
                parts[r][1, :, at] = dot(attend.astype(BF16), do_h).astype(BF16)

    part = sds((2, n_mem, wide), BF16)
    stats2, ds_mem, *parts = whole_call(
        memory_body,
        (stat_shape, sds((heads, n_mem, rows), BF16)) + (part,) * n_seq,
        ids, qn, do, stats, *mk_recv, *mv_recv,
        micros=2.0,
    )
    parts_recv = to_peers("seq", parts[1:])

    def grads_body(q_ref, kp_ref, qn_ref, kn_ref, vp_ref, do_ref, st_ref, ds_ref, *rest):
        mk_refs = rest[: n_seq - 1]
        inv_ref, qg_ref, gq_ref, gk_ref, gv_ref, dq_ref, gain_q_ref, gain_k_ref = rest[n_seq - 1 :]
        allowed = causal_t(rows)
        inv_c = as_columns(inv_ref[...])
        total = jnp.zeros((rows, HD), F32)
        for h in range(heads):
            at = slice(h * HD, (h + 1) * HD)
            narrow = slice((h % hp) * HD, (h % hp + 1) * HD)
            span = slice((h // hp) * slots, (h // hp + 1) * slots)
            qn_h, kn_h, do_h = qn_ref[:, at], kn_ref[:, at], do_ref[:, at]
            s = jnp.where(allowed, dot(kn_h, qn_h, NT) * scale, -jnp.inf)
            g = dot(vp_ref[:, at], do_h, NT)
            m, inv_mass, delta = st_ref[h, 0:1, :], st_ref[h, 1:2, :], st_ref[h, 2:3, :]
            attend = jnp.exp(s - m) * inv_mass
            ds = (attend * (g - delta)).astype(BF16)
            mk = jnp.concatenate([ref[span, narrow] for ref in mk_refs], axis=0)
            gq = scale * (dot(ds, kn_h, TN) + dot(ds_ref[h], mk, TN))
            gk = scale * dot(ds, qn_h)
            gq_ref[:, at] = gq
            gk_ref[:, at] = gk
            gv_ref[:, at] = dot(attend.astype(BF16), do_h)
            gq_q = gq * q_ref[:, at].astype(F32)
            gk_k = gk * kp_ref[:, at].astype(F32)
            total = total + gq_q * qg_ref[:, at]
            gain_q_ref[h : h + 1, :] = jnp.sum(gq_q * inv_c[:, 0:1], axis=0, keepdims=True)
            gain_k_ref[h : h + 1, :] = jnp.sum(gk_k * inv_c[:, 1:2], axis=0, keepdims=True)
        dq_ref[...] = lane_sum_row(total)

    gain_rows = sds((heads, HD), F32)
    wide_f32 = sds((rows, cols), F32)
    dot_row = sds((1, rows), F32)
    gq, gk_local, gv_local, dot_q, gain_q, gain_k = whole_call(
        grads_body,
        (wide_f32, wide_f32, wide_f32, dot_row, gain_rows, gain_rows),
        q, kp, qn, kn, vp, do, stats2, ds_mem, *mk_recv, inv, qg,
        micros=0.5,
        after=tuple(rows_recv),
    )

    def slots_body(*refs):
        ins, outs = refs[:n_seq], refs[n_seq:]
        for r in range(n_seq):
            for tensor in range(2):
                total = None
                for src in range(n_seq):
                    if src == r:
                        continue
                    block = (src ^ r) - 1
                    term = ins[src][tensor, block * slots : (block + 1) * slots, :].astype(F32)
                    total = term if total is None else total + term
                outs[r][tensor] = total.astype(BF16)

    slot_grad = sds((2, slots, wide), BF16)
    slot_grads = whole_call(
        slots_body, (slot_grad,) * n_seq, parts[0], *parts_recv, after=(gain_q,), micros=0.3
    )

    slots_recv = to_peers("seq", slot_grads[1:])

    def weights_body(ids_ref, kn_ref, vp_ref, *rest):
        gm = rest[:n_seq]
        row_refs = rest[n_seq : 2 * n_seq - 1]
        same_ref, other_ref = rest[2 * n_seq - 1 :]
        here = pl.ds(pl.multiple_of(ids_ref[0] * wide, wide), wide)
        own = (kn_ref[:, here], vp_ref[:, here])
        first = ids_ref[1] == 0
        for i in range(hp):
            at = slice(i * HD, (i + 1) * HD)
            for j in range(KS):
                span = slice(j * slots, (j + 1) * slots)
                found = []
                for tensor in range(2):
                    lhs = jnp.concatenate(
                        [own[tensor][span, at]] + [ref[tensor, span, at] for ref in row_refs],
                        axis=0,
                    )
                    rhs = jnp.concatenate([ref[tensor, :, at] for ref in gm], axis=0)
                    found.append(dot(lhs, rhs, TN))
                to = slice((i * KS + j) * HD, (i * KS + j + 1) * HD)
                same_ref[to, :] = jnp.where(first, found[0], found[1])
                other_ref[to, :] = jnp.where(first, found[1], found[0]).astype(BF16)

    span_rows = hp * KS * HD
    w_same, w_other = whole_call(
        weights_body,
        (sds((span_rows, HD), F32), sds((span_rows, HD), BF16)),
        ids, kn, vp, *slot_grads, *rows_recv,
        micros=1.1,
    )
    w_recv = to_core(w_other)

    def chunk_body(a_ref, b_ref, gq_ref, gk_ref, out_ref):
        out_ref[:span_rows, :] = (a_ref[...] + b_ref[...].astype(F32)).astype(BF16)
        gains = jnp.concatenate([gq_ref[...], gk_ref[...]], axis=0)
        out_ref[span_rows:, :] = gains.astype(BF16)

    chunk_shape = sds((span_rows + 2 * heads, HD), BF16)
    chunk = whole_call(chunk_body, chunk_shape, w_same, w_recv, gain_q, gain_k, micros=0.3)
    chunks = to_peers("seq", [chunk] * (n_seq - 1))
    chunk_other = to_core(chunk)

    def send_out(buffer, target, sems, index, at):
        copy = pltpu.make_async_copy(buffer.at[:, at], target.at[:, at], sems.at[index])
        copy.start()
        return copy

    def column_out(body, outs, n_out, *ins, micros, after=()):
        skip = len(after)
        inside = pl.BlockSpec(memory_space=pltpu.VMEM)
        small = len(outs) - n_out
        return pl.pallas_call(
            lambda *refs: body(*refs[: len(ins)], *refs[len(ins) + skip :]),
            out_shape=outs,
            in_specs=[
                pl.BlockSpec(memory_space=pltpu.SMEM) if a.dtype == jnp.int32 else inside
                for a in ins
            ]
            + [pl.BlockSpec(memory_space=pl.ANY)] * skip,
            out_specs=(inside,) * small + (pl.BlockSpec(memory_space=pl.ANY),) * n_out,
            scratch_shapes=[pltpu.VMEM((rows, cols), BF16)] * n_out
            + [pltpu.SemaphoreType.DMA((n_out, n_seq))],
            compiler_params=pltpu.CompilerParams(vmem_limit_bytes=40 * 2**20),
            cost_estimate=cost_of(micros),
        )(*ins, *after)

    def spread_back(gm, w):
        wide_rows = dot(gm, w, NT)
        return jnp.concatenate([wide_rows[:, j * HD : (j + 1) * HD] for j in range(KS)], axis=0)

    def head_places(mine):
        for r in range(n_seq):
            for i in range(hp):
                h = (mine ^ r) * hp + i
                narrow = slice(i * HD, (i + 1) * HD)
                yield r, i, h, narrow, pl.ds(pl.multiple_of(h * HD, HD), HD)

    def back_keys_body(ids_ref, gk_ref, kp_ref, wk_ref, kg_ref, dq_ref, *rest):
        gm = rest[:n_seq]
        gkn_ref, dots_ref = rest[n_seq:]
        total = jnp.zeros((rows, HD), F32)
        for r, i, h, narrow, at in head_places(ids_ref[0]):
            gkn = gk_ref[:, at] + spread_back(gm[r][0, :, narrow], wk_ref[h])
            gkn_ref[:, at] = gkn
            total = total + gkn * kp_ref[:, at].astype(F32) * kg_ref[:, at]
        dots_ref[0:1, :] = dq_ref[...]
        dots_ref[1:2, :] = lane_sum_row(total)

    gkn, dots = whole_call(
        back_keys_body,
        (wide_f32, two_rows),
        ids, gk_local, kp, key_squeeze, kg, dot_q, slot_grads[0], *slots_recv,
        micros=2.0,
        after=(chunk,),
    )

    def back_values_body(ids_ref, gv_ref, wv_ref, *rest):
        gm = rest[:n_seq]
        mark_ref, value_ref, buffer, sems = rest[n_seq:]
        mark_ref[...] = jnp.zeros_like(mark_ref)
        unorder = row_order_back(rows)
        copies = []
        for r, i, h, narrow, at in head_places(ids_ref[0]):
            value = gv_ref[:, at] + spread_back(gm[r][1, :, narrow], wv_ref[h])
            buffer[:, at] = dot(unorder, value.astype(BF16)).astype(BF16)
            if i == hp - 1:
                block = ids_ref[0] ^ r
                wide_at = pl.ds(pl.multiple_of(block * wide, wide), wide)
                copies.append(send_out(buffer, value_ref, sems.at[0], r, wide_at))
        for copy in copies:
            copy.wait()

    mark, grad_value = column_out(
        back_values_body,
        (sds((8, HD), F32), rows_shape),
        1,
        ids, gv_local, value_squeeze, slot_grads[0], *slots_recv,
        micros=2.0,
        after=(dots,),
    )
    dots_parts = over_heads(dots, beside=(mark,))

    kernel_out = sds((heads, KS * HD, HD), F32)
    gains_shape = sds((1, cols), F32)

    def write_chunk(mine, r, read, buffer, sem, target):
        start = (mine ^ r) * hp
        for i in range(hp):
            buffer[start + i] = read(slice(i * KS * HD, (i + 1) * KS * HD)).astype(F32)
        at = pl.ds(start, hp)
        copy = pltpu.make_async_copy(buffer.at[at], target.at[at], sem)
        copy.start()
        return copy

    def own_chunk_body(ids_ref, same, other, *rest):
        mark_ref, gks_ref, gvs_ref, buffer_k, buffer_v, sems = rest
        mark_ref[...] = jnp.zeros_like(mark_ref)
        first = ids_ref[1] == 0
        copies = [
            write_chunk(
                ids_ref[0], 0, lambda at: jnp.where(first, same[at, :], other[at, :]),
                buffer_k, sems.at[0], gks_ref,
            ),
            write_chunk(
                ids_ref[0], 0, lambda at: jnp.where(first, other[at, :], same[at, :]),
                buffer_v, sems.at[1], gvs_ref,
            ),
        ]
        for copy in copies:
            copy.wait()

    smem = pl.BlockSpec(memory_space=pltpu.SMEM)
    inside = pl.BlockSpec(memory_space=pltpu.VMEM)
    outside = pl.BlockSpec(memory_space=pl.ANY)
    buffer = pltpu.VMEM(kernel_out.shape, F32)
    params = pltpu.CompilerParams(vmem_limit_bytes=40 * 2**20)
    own_mark, *part_written = pl.pallas_call(
        own_chunk_body,
        out_shape=(sds((8, HD), F32), kernel_out, kernel_out),
        in_specs=[smem, inside, inside],
        out_specs=(inside, outside, outside),
        scratch_shapes=[buffer, buffer, pltpu.SemaphoreType.DMA((2,))],
        compiler_params=params,
        cost_estimate=cost_of(0.01),
    )(ids, chunk, chunk_other)

    def norms_body(q_ref, kp_ref, gq_ref, gkn_ref, qg_ref, kg_ref, inv_ref, *rest):
        dots_a, dots_b, mark_ref, out_q, out_k, buffer_q, buffer_k, sems = rest
        mark_ref[...] = jnp.zeros_like(mark_ref)
        total = dots_a[...] + dots_b[...]
        inv_rows = inv_ref[...]
        inv_c = as_columns(inv_rows)
        pull = as_columns(inv_rows * inv_rows * inv_rows * total / full_width)
        unorder = row_order_back(rows)
        copies = []
        for r in range(n_seq):
            at = slice(r * wide, (r + 1) * wide)
            buffer_q[:, at] = (
                inv_c[:, 0:1] * qg_ref[:, at] * gq_ref[:, at]
                - q_ref[:, at].astype(F32) * pull[:, 0:1]
            ).astype(BF16)
            copies.append(send_out(buffer_q, out_q, sems.at[0], r, at))
            grad_k = (
                inv_c[:, 1:2] * kg_ref[:, at] * gkn_ref[:, at]
                - kp_ref[:, at].astype(F32) * pull[:, 1:2]
            ).astype(BF16)
            buffer_k[:, at] = dot(unorder, grad_k).astype(BF16)
            copies.append(send_out(buffer_k, out_k, sems.at[1], r, at))
        for copy in copies:
            copy.wait()

    norms_mark, grad_query, grad_key = column_out(
        norms_body,
        (sds((8, HD), F32), rows_shape, rows_shape),
        2,
        q, kp, gq, gkn, qg, kg, inv, *dots_parts,
        micros=0.01,
        after=(own_mark,),
    )

    def pack_body(*refs):
        for r in range(n_seq - 1):
            refs[n_seq - 1][r] = refs[r][...]

    packed_shape = sds((n_seq - 1,) + chunk_shape.shape, BF16)
    packed = whole_call(pack_body, packed_shape, *chunks, micros=0.1, after=(norms_mark, own_mark))
    packed_other = to_core(packed)

    def back_gain(mine, chunk_0, chunks_ref, kg_ref, wk_ref, out_ref):
        sums = []
        for r in range(n_seq):
            for i in range(hp):
                h = (mine ^ r) * hp + i
                total = jnp.zeros((HD, HD), F32)
                for j in range(KS):
                    span = slice((i * KS + j) * HD, (i * KS + j + 1) * HD)
                    grad_w = chunk_0[span, :] if r == 0 else chunks_ref[r - 1, span, :]
                    kernel = wk_ref[h, j * HD : (j + 1) * HD, :]
                    total = total + grad_w.astype(F32) * kernel.astype(F32)
                sums.append(total)
        sums = jnp.concatenate(sums, axis=0)
        high = sums.astype(BF16)
        low = (sums - high.astype(F32)).astype(BF16)
        ones = jnp.ones((16, HD), BF16)
        row = (dot(ones, high, NT) + dot(ones, low, NT))[0:1]
        for r in range(n_seq):
            at = pl.ds(pl.multiple_of((mine ^ r) * wide, wide), wide)
            out_ref[:, at] = row[:, r * wide : (r + 1) * wide] / kg_ref[:, at]

    def write_chunks(mine, chunks_ref, buffer, sems, target):
        return [
            write_chunk(
                mine, r, lambda at, r=r: chunks_ref[r - 1, at, :], buffer, sems.at[r], target
            )
            for r in peers
        ]

    def this_core_body(ids_ref, same_0, same, kg_ref, wk_ref, gks_in, gvs_in, *rest):
        back_ref, gks_ref, gvs_ref, buffer, sems = rest

        @pl.when(ids_ref[1] == 0)
        def _():
            copies = write_chunks(ids_ref[0], same, buffer, sems, gks_ref)
            back_gain(ids_ref[0], same_0, same, kg_ref, wk_ref, back_ref)
            for copy in copies:
                copy.wait()

        @pl.when(ids_ref[1] == 1)
        def _():
            copies = write_chunks(ids_ref[0], same, buffer, sems, gvs_ref)
            back_ref[...] = jnp.zeros_like(back_ref)
            for copy in copies:
                copy.wait()

    def other_core_body(ids_ref, same_0, other_0, same, other, back, kg_ref, wk_ref, *rest):
        gks_ref, gvs_ref, gq_out, gk_out, buffer, gq_row, gk_row, sems = rest[2:]

        def finish(copies):
            total = same_0[span_rows:, :].astype(F32) + other_0[span_rows:, :].astype(F32)
            for r in range(n_seq - 1):
                total = total + same[r, span_rows:, :].astype(F32)
                total = total + other[r, span_rows:, :].astype(F32)
            as_row = lambda x: jnp.concatenate([x[h : h + 1] for h in range(heads)], axis=1)
            gq_row[...] = as_row(total[:heads])
            gk_row[...] += as_row(total[heads:])
            copies.append(pltpu.make_async_copy(gq_row, gq_out, sems.at[0]))
            copies[-1].start()
            copies.append(pltpu.make_async_copy(gk_row, gk_out, sems.at[n_seq]))
            copies[-1].start()
            for copy in copies:
                copy.wait()

        @pl.when(ids_ref[1] == 0)
        def _():
            copies = write_chunks(ids_ref[0], other, buffer, sems, gvs_ref)
            gk_row[...] = back[...]
            finish(copies)

        @pl.when(ids_ref[1] == 1)
        def _():
            copies = write_chunks(ids_ref[0], other, buffer, sems, gks_ref)
            back_gain(ids_ref[0], other_0, other, kg_ref, wk_ref, gk_row)
            finish(copies)

    back_row, *part_written = pl.pallas_call(
        this_core_body,
        out_shape=(gains_shape, kernel_out, kernel_out),
        in_specs=[smem] + [inside] * 4 + [outside] * 2,
        out_specs=(inside, outside, outside),
        input_output_aliases={5: 1, 6: 2},
        scratch_shapes=[buffer, pltpu.SemaphoreType.DMA((n_seq,))],
        compiler_params=params,
        cost_estimate=cost_of(1.6),
    )(ids, chunk, packed, kg, key_squeeze, *part_written)
    gks, gvs, gain_q_all, gain_k_all = pl.pallas_call(
        other_core_body,
        out_shape=(kernel_out, kernel_out, gains_shape, gains_shape),
        in_specs=[smem] + [inside] * 7 + [outside] * 2,
        out_specs=(outside,) * 4,
        input_output_aliases={8: 0, 9: 1},
        scratch_shapes=[
            buffer,
            pltpu.VMEM((1, cols), F32),
            pltpu.VMEM((1, cols), F32),
            pltpu.SemaphoreType.DMA((n_seq + 1,)),
        ],
        compiler_params=params,
        cost_estimate=cost_of(2.2),
    )(ids, chunk, chunk_other, packed, packed_other, back_row, kg, key_squeeze, *part_written)
    return (
        grad_query[None],
        grad_key[None],
        grad_value[None],
        gain_q_all.reshape(cols),
        gain_k_all.reshape(cols),
        gks,
        gvs,
    )


def solution(mesh):
    placed = (
        P("dp", "seq", "head"),
        P("dp", "seq", "head"),
        P("dp", "seq", "head"),
        P("head"),
        P("head"),
        P("head", None, None),
        P("head", None, None),
        P("dp", "seq", "head"),
    )
    return jax.shard_map(
        on_device,
        mesh=mesh,
        in_specs=placed,
        out_specs=(
            P("dp", "seq", "head"),
            P("dp", "seq", "head"),
            P("dp", "seq", "head"),
            P("head"),
            P("head"),
            P("head", None, None),
            P("head", None, None),
        ),
        check_vma=False,
    )
```

```python
import jax
import jax.numpy as jnp
from jax import lax
from jax.experimental import pallas as pl
from jax.experimental.pallas import tpu as pltpu
from jax.sharding import PartitionSpec as P

HD = 128
KS = 4
HH = 4096


epsilon = 1e-06


def unfold_slots(source, head_count):
    batch_size, row_count, widths = source.shape
    return (
        source.reshape(batch_size, row_count // KS, KS, head_count, HD)
        .transpose(0, 1, 3, 2, 4)
        .reshape(batch_size, row_count // KS, head_count, KS * HD)
    )


def fold_slots(source):
    batch_size, slot_count, head_count, spans = source.shape
    return (
        source.reshape(batch_size, slot_count, head_count, KS, HD)
        .transpose(0, 1, 3, 2, 4)
        .reshape(batch_size, slot_count * KS, head_count * HD)
    )


def on_device_any(
    query_heads, key_heads, value_heads, query_gain, key_gain, key_squeeze, value_squeeze, grad_out
):
    batch_size, row_count, widths = query_heads.shape
    head_count = widths // HD
    slot_count = row_count // KS
    score_scale = HD ** (-0.5)
    own_limit = lax.axis_index("seq") * slot_count
    q_full = query_heads.astype(jnp.float32)
    k_full = key_heads.astype(jnp.float32)
    sum_q, sum_k = lax.psum((jnp.sum(q_full * q_full, -1), jnp.sum(k_full * k_full, -1)), "head")
    inv_q = lax.rsqrt(sum_q / HH + epsilon)[..., None]
    inv_k = lax.rsqrt(sum_k / HH + epsilon)[..., None]
    q_norm = (q_full * inv_q * query_gain).astype(jnp.bfloat16)
    k_norm = (k_full * inv_k * key_gain).astype(jnp.bfloat16)
    k_unf = unfold_slots(k_norm, head_count)
    v_unf = unfold_slots(value_heads, head_count)
    mem_k = (
        jnp.einsum("bmhc,hcd->bmhd", k_unf, key_squeeze, preferred_element_type=jnp.float32)
        .astype(jnp.bfloat16)
        .reshape(batch_size, slot_count, widths)
    )
    mem_v = (
        jnp.einsum("bmhc,hcd->bmhd", v_unf, value_squeeze, preferred_element_type=jnp.float32)
        .astype(jnp.bfloat16)
        .reshape(batch_size, slot_count, widths)
    )
    queries = q_norm.reshape(batch_size, row_count, head_count, HD)
    key_loc = k_norm.reshape(batch_size, row_count, head_count, HD)
    value_loc = value_heads.reshape(batch_size, row_count, head_count, HD)
    cotangent = grad_out.reshape(batch_size, row_count, head_count, HD)
    positions = jnp.arange(row_count)
    causal = positions[:, None] >= positions[None, :]
    scores_loc = jnp.where(
        causal,
        jnp.einsum("bthd,buhd->bhtu", queries, key_loc, preferred_element_type=jnp.float32)
        * score_scale,
        -jnp.inf,
    )
    grads_loc = jnp.einsum(
        "bthd,buhd->bhtu", cotangent, value_loc, preferred_element_type=jnp.float32
    )
    all_k, all_v = (
        lax.all_gather(mem_k, "seq", axis=1, tiled=True),
        lax.all_gather(mem_v, "seq", axis=1, tiled=True),
    )
    piece_rows = all_k.shape[1]
    key_rows = all_k.reshape(batch_size, piece_rows, head_count, HD)
    value_rows = all_v.reshape(batch_size, piece_rows, head_count, HD)
    allowed = jnp.arange(piece_rows) < own_limit
    scores = jnp.where(
        allowed,
        jnp.einsum("bthd,buhd->bhtu", queries, key_rows, preferred_element_type=jnp.float32)
        * score_scale,
        -jnp.inf,
    )
    gradients = jnp.einsum(
        "bthd,buhd->bhtu", cotangent, value_rows, preferred_element_type=jnp.float32
    )
    key_rows, scores_mem, grads_mem = (key_rows, scores, gradients)
    peak = jnp.maximum(jnp.max(scores_loc, -1), jnp.max(scores_mem, -1))
    summed = jnp.sum(jnp.exp(scores_loc - peak[..., None]), -1) + jnp.sum(
        jnp.exp(scores_mem - peak[..., None]), -1
    )
    log_mass = peak + jnp.log(summed)
    row_delta = jnp.sum(jnp.exp(scores_loc - log_mass[..., None]) * grads_loc, -1) + jnp.sum(
        jnp.exp(scores_mem - log_mass[..., None]) * grads_mem, -1
    )
    piece_rows = key_rows.shape[1]
    attend = jnp.exp(scores_mem - log_mass[..., None])
    d_scores = (attend * (grads_mem - row_delta[..., None])).astype(jnp.bfloat16)
    grad_q = score_scale * jnp.einsum(
        "bhtu,buhd->bthd", d_scores, key_rows, preferred_element_type=jnp.float32
    )
    grad_k = score_scale * jnp.einsum(
        "bhtu,bthd->buhd", d_scores, queries, preferred_element_type=jnp.float32
    )
    grad_v = jnp.einsum(
        "bhtu,bthd->buhd",
        attend.astype(jnp.bfloat16),
        cotangent,
        preferred_element_type=jnp.float32,
    )
    stacked = jnp.stack(
        (
            grad_k.reshape(batch_size, piece_rows, widths),
            grad_v.reshape(batch_size, piece_rows, widths),
        )
    )
    attend_loc = jnp.exp(scores_loc - log_mass[..., None])
    d_loc = (attend_loc * (grads_loc - row_delta[..., None])).astype(jnp.bfloat16)
    grad_qn = (
        score_scale
        * jnp.einsum("bhtu,buhd->bthd", d_loc, key_loc, preferred_element_type=jnp.float32)
        + grad_q
    ).reshape(batch_size, row_count, widths)
    grad_kn_local = score_scale * jnp.einsum(
        "bhtu,bthd->buhd", d_loc, queries, preferred_element_type=jnp.float32
    )
    grad_v_local = jnp.einsum(
        "bhtu,bthd->buhd",
        attend_loc.astype(jnp.bfloat16),
        cotangent,
        preferred_element_type=jnp.float32,
    )
    mine = lax.psum_scatter(stacked.astype(jnp.bfloat16), "seq", scatter_dimension=2, tiled=True)
    grad_mem_k = mine[0].reshape(batch_size, slot_count, head_count, HD)
    grad_mem_v = mine[1].reshape(batch_size, slot_count, head_count, HD)
    squeeze_k_part = jnp.einsum(
        "bmhc,bmhd->hcd", k_unf, grad_mem_k, preferred_element_type=jnp.float32
    )
    squeeze_v_part = jnp.einsum(
        "bmhc,bmhd->hcd", v_unf, grad_mem_v, preferred_element_type=jnp.float32
    )
    back_k = fold_slots(
        jnp.einsum("bmhd,hcd->bmhc", grad_mem_k, key_squeeze, preferred_element_type=jnp.float32)
    )
    back_v = fold_slots(
        jnp.einsum("bmhd,hcd->bmhc", grad_mem_v, value_squeeze, preferred_element_type=jnp.float32)
    )
    grad_kn = grad_kn_local.reshape(batch_size, row_count, widths) + back_k
    grad_value = (grad_v_local.reshape(batch_size, row_count, widths) + back_v).astype(jnp.bfloat16)
    dot_q, dot_k = lax.psum(
        (jnp.sum(query_gain * grad_qn * q_full, -1), jnp.sum(key_gain * grad_kn * k_full, -1)),
        "head",
    )
    grad_query = (
        inv_q * query_gain * grad_qn - q_full * inv_q**3 * dot_q[..., None] / HH
    ).astype(jnp.bfloat16)
    grad_key = (inv_k * key_gain * grad_kn - k_full * inv_k**3 * dot_k[..., None] / HH).astype(
        jnp.bfloat16
    )
    gain_q_part = jnp.sum(grad_qn * q_full * inv_q, (0, 1))
    gain_k_part = jnp.sum(grad_kn * k_full * inv_k, (0, 1))
    grad_query_gain, grad_key_gain, grad_key_squeeze, grad_value_squeeze = (
        lax.psum(gain_q_part.astype(jnp.bfloat16), ("seq", "dp")).astype(jnp.float32),
        lax.psum(gain_k_part.astype(jnp.bfloat16), ("seq", "dp")).astype(jnp.float32),
        lax.psum(squeeze_k_part.astype(jnp.bfloat16), ("seq", "dp")).astype(jnp.float32),
        lax.psum(squeeze_v_part.astype(jnp.bfloat16), ("seq", "dp")).astype(jnp.float32),
    )
    return (
        grad_query,
        grad_key,
        grad_value,
        grad_query_gain,
        grad_key_gain,
        grad_key_squeeze,
        grad_value_squeeze,
    )


F32 = jnp.float32
BF16 = jnp.bfloat16
NN = (((1,), (0,)), ((), ()))
NT = (((1,), (1,)), ((), ()))
TN = (((0,), (0,)), ((), ()))


def dot(a, b, dims=NN):
    return lax.dot_general(a, b, dims, preferred_element_type=F32)


def sds(shape, dtype):
    return jax.ShapeDtypeStruct(shape, dtype)


def place():
    return lax.axis_index("seq"), lax.axis_index("dp")


def cost_of(micros):
    return pl.CostEstimate(
        flops=int(micros * 1e9), bytes_accessed=int(micros * 3.6e6), transcendentals=0
    )


def whole_call(body, outs, *ins, micros=1.0, after=(), scratch=(), vmem=40, aliases=None):
    first = (place,) if ins[0] is place else ()
    ins = ins[len(first) :]
    n_out = len(jax.tree.leaves(outs))
    skip = len(after)
    space = pl.BlockSpec(memory_space=pltpu.VMEM)
    return pl.pallas_call(
        lambda *refs: body(
            *(ask() for ask in first), *refs[: len(ins)], *refs[len(ins) + skip :]
        ),
        out_shape=outs,
        in_specs=[space] * len(ins) + [pl.BlockSpec(memory_space=pl.ANY)] * skip,
        out_specs=jax.tree.map(lambda _: space, outs),
        scratch_shapes=list(scratch),
        input_output_aliases=aliases or {},
        compiler_params=pltpu.CompilerParams(vmem_limit_bytes=vmem * 2**20),
        cost_estimate=cost_of(micros),
    )(*ins, *after)


def row_order(rows):
    slots = rows // KS
    r = lax.broadcasted_iota(jnp.int32, (rows, rows), 0)
    c = lax.broadcasted_iota(jnp.int32, (rows, rows), 1)
    return jnp.where(c == KS * (r % slots) + r // slots, 1.0, 0.0).astype(BF16)


def row_order_back(rows):
    slots = rows // KS
    r = lax.broadcasted_iota(jnp.int32, (rows, rows), 0)
    c = lax.broadcasted_iota(jnp.int32, (rows, rows), 1)
    return jnp.where(r == KS * (c % slots) + c // slots, 1.0, 0.0).astype(BF16)


def causal_t(rows):
    slots = rows // KS
    u = lax.broadcasted_iota(jnp.int32, (rows, rows), 0)
    t = lax.broadcasted_iota(jnp.int32, (rows, rows), 1)
    return KS * (u % slots) + u // slots <= t


def fold_lanes(x):
    total = x[:, :HD]
    for i in range(1, x.shape[1] // HD):
        total = total + x[:, i * HD : (i + 1) * HD]
    return total


def lane_sum_row(x):
    return jnp.sum(x.T, axis=0, keepdims=True)


def as_columns(rows):
    pad = jnp.zeros((8 - rows.shape[0], rows.shape[1]), F32)
    return jnp.concatenate([rows, pad], axis=0).T


def on_device(
    query_heads, key_heads, value_heads, query_gain, key_gain, key_squeeze, value_squeeze, grad_out
):
    n_seq, n_head = lax.axis_size("seq"), lax.axis_size("head")
    batch_size, rows, cols = query_heads.shape
    heads = cols // HD
    if batch_size != 1 or n_seq & (n_seq - 1) or heads % n_seq or lax.axis_size("dp") != 2:
        return on_device_any(
            query_heads,
            key_heads,
            value_heads,
            query_gain,
            key_gain,
            key_squeeze,
            value_squeeze,
            grad_out,
        )
    slots = rows // KS
    hp = heads // n_seq
    wide = hp * HD
    mem_rows = n_seq * slots
    peers = range(1, n_seq)
    n_mem = (n_seq - 1) * slots
    scale = HD ** (-0.5)
    full_width = cols * n_head

    def to_peers(axis, arrays):
        n = lax.axis_size(axis)
        return [
            lax.ppermute(a, axis, [(i, i ^ k) for i in range(n)])
            for k, a in zip(range(1, n), arrays)
        ]

    def sum_body(a_ref, b_ref, out_ref):
        out_ref[...] = a_ref[...] + b_ref[...]

    def over_heads(a, beside=()):
        step, got = 1, None
        while step < n_head:
            if got is not None:
                a = whole_call(sum_body, sds(a.shape, a.dtype), a, got, micros=0.1, after=beside)
            got = lax.ppermute(a, "head", [(i, i ^ step) for i in range(n_head)])
            step *= 2
        return a, got

    def to_core(a):
        return lax.ppermute(a, "dp", [(0, 1), (1, 0)])

    q = query_heads[0]
    k = key_heads[0]
    v = value_heads[0]
    do = grad_out[0]
    qg = query_gain.reshape(1, cols)
    kg = key_gain.reshape(1, cols)

    def squares_body(q_ref, k_ref, ss_ref):
        qf = q_ref[...].astype(F32)
        ss_ref[0:1, :] = lane_sum_row(fold_lanes(qf * qf))
        kf = k_ref[...].astype(F32)
        ss_ref[1:2, :] = lane_sum_row(fold_lanes(kf * kf))

    two_rows = sds((2, rows), F32)
    ss = whole_call(squares_body, two_rows, q, k, micros=1.5, vmem=62)
    ss_parts = [ss] + to_peers("head", [ss] * (n_head - 1))

    def compress(source, w_ref, out_ref):
        for h in range(heads):
            total = None
            for j in range(KS):
                part = dot(
                    source[j * slots : (j + 1) * slots, h * HD : (h + 1) * HD],
                    w_ref[h, j * HD : (j + 1) * HD, :],
                )
                total = part if total is None else total + part
            block = h // hp
            out_ref[
                block * slots : (block + 1) * slots, (h % hp) * HD : (h % hp + 1) * HD
            ] = total.astype(BF16)

    def pack_slots(mine, mem_ref, sends):
        for k, send in zip(peers, sends):
            for r in peers:
                source = pl.ds(pl.multiple_of((mine ^ k ^ r) * slots, slots), slots)
                send[(r - 1) * slots : r * slots, :] = mem_ref[source, :]

    def values_body(ids_ref, v_ref, w_ref, vp_ref, *rest):
        sends, mem_ref = rest[:-1], rest[-1]
        vp_ref[...] = dot(row_order(rows), v_ref[...]).astype(BF16)
        compress(vp_ref, w_ref, mem_ref)
        pack_slots(ids_ref[0], mem_ref, sends)

    rows_shape = sds((rows, cols), BF16)
    mem_shape = sds((mem_rows, wide), BF16)
    slots_packet = sds((n_mem, wide), BF16)
    mem_scratch = [pltpu.VMEM(mem_shape.shape, BF16)]
    vp, *mv_sends = whole_call(
        values_body,
        (rows_shape,) + (slots_packet,) * (n_seq - 1),
        place, v, value_squeeze,
        scratch=mem_scratch,
        micros=0.8,
    )
    mv_recv = to_peers("seq", mv_sends)

    def keys_body(ids_ref, k_ref, kg_ref, w_ref, *rest):
        ss_refs = rest[:n_head]
        inv_ref, kn_ref = rest[n_head : n_head + 2]
        sends, mem_ref = rest[n_head + 2 : -1], rest[-1]
        total = ss_refs[0][...]
        for other in ss_refs[1:]:
            total = total + other[...]
        natural = as_columns(lax.rsqrt(total / full_width + epsilon))
        order = row_order(rows)
        high = natural.astype(BF16)
        rest_1 = natural - high.astype(F32)
        middle = rest_1.astype(BF16)
        low = (rest_1 - middle.astype(F32)).astype(BF16)
        ordered = dot(order, high) + dot(order, middle) + dot(order, low)
        inv_c = jnp.concatenate([natural[:, 0:1], ordered[:, 1:2], natural[:, 2:]], axis=1)
        inv_ref[...] = inv_c.T[:2]
        normed = (k_ref[...].astype(F32) * natural[:, 1:2] * kg_ref[...]).astype(BF16)
        kn_ref[...] = dot(order, normed).astype(BF16)
        compress(kn_ref, w_ref, mem_ref)
        pack_slots(ids_ref[0], mem_ref, sends)

    inv, kn, *mk_sends = whole_call(
        keys_body,
        (two_rows, rows_shape) + (slots_packet,) * (n_seq - 1),
        place, k, kg, key_squeeze, *ss_parts,
        scratch=mem_scratch,
        micros=20.0,
    )
    mk_recv = to_peers("seq", mk_sends)

    def local_body(q_ref, qg_ref, inv_ref, kn_ref, vp_ref, do_ref, qn_ref, st_ref):
        allowed = causal_t(rows)
        inv_c = as_columns(inv_ref[...])[:, 0:1]
        for h in range(heads):
            at = slice(h * HD, (h + 1) * HD)
            qn_h = (q_ref[:, at].astype(F32) * inv_c * qg_ref[:, at]).astype(BF16)
            qn_ref[:, at] = qn_h
            s = jnp.where(allowed, dot(kn_ref[:, at], qn_h, NT) * scale, -jnp.inf)
            g = dot(vp_ref[:, at], do_ref[:, at], NT)
            m = jnp.max(s, axis=0, keepdims=True)
            p = jnp.exp(s - m)
            st_ref[h, 0:1, :] = m
            st_ref[h, 1:2, :] = jnp.sum(p, axis=0, keepdims=True)
            st_ref[h, 2:3, :] = jnp.sum(p * g, axis=0, keepdims=True)

    stat_shape = sds((heads, 8, rows), F32)
    qn, stats = whole_call(
        local_body, (rows_shape, stat_shape), q, qg, inv, kn, vp, do,
        micros=0.5,
        after=tuple(mv_recv),
    )

    def rows_body(ids_ref, kn_ref, vp_ref, k_ref, *outs):
        sends, kp_ref = outs[:-1], outs[-1]
        kp_ref[...] = dot(row_order(rows), k_ref[...]).astype(BF16)
        for r, send in zip(peers, sends):
            dest = ids_ref[0] ^ r
            at = pl.ds(pl.multiple_of(dest * wide, wide), wide)
            send[0] = kn_ref[:, at]
            send[1] = vp_ref[:, at]

    row_pair = sds((2, rows, wide), BF16)
    *row_sends, kp = whole_call(
        rows_body,
        (row_pair,) * (n_seq - 1) + (rows_shape,),
        place, kn, vp, k,
        after=(stats,),
        micros=0.7,
    )
    rows_recv = to_peers("seq", row_sends)

    def memory_head(mine, qn_h, do_h, mk, mv, stat):
        raw = dot(mk, qn_h, NT) * scale
        s = jnp.concatenate(
            [
                jnp.where((mine ^ src) < mine, raw[(src - 1) * slots : src * slots], -jnp.inf)
                for src in peers
            ],
            axis=0,
        )
        g = dot(mv, do_h, NT)
        m_loc, l_loc, d_loc = stat[0:1], stat[1:2], stat[2:3]
        m = jnp.maximum(m_loc, jnp.max(s, axis=0, keepdims=True))
        p = jnp.exp(s - m)
        shrink = jnp.exp(m_loc - m)
        mass = l_loc * shrink + jnp.sum(p, axis=0, keepdims=True)
        inv_mass = 1.0 / mass
        delta = (d_loc * shrink + jnp.sum(p * g, axis=0, keepdims=True)) * inv_mass
        attend = p * inv_mass
        ds = (attend * (g - delta)).astype(BF16)
        gk = (dot(ds, qn_h) * scale).astype(BF16)
        gv = dot(attend.astype(BF16), do_h).astype(BF16)
        return jnp.concatenate([m, inv_mass, delta, stat[3:]], axis=0), ds, gk, gv

    def places(mine, r, i):
        h = (mine ^ r) * hp + i
        return h, pl.ds(pl.multiple_of(h * HD, HD), HD), slice(i * HD, (i + 1) * HD)

    def memory_body(ids_ref, qn_ref, do_ref, st_ref, *rest):
        mk_refs = rest[: n_seq - 1]
        mv_refs = rest[n_seq - 1 : 2 * n_seq - 2]
        st2_ref, ds_ref = rest[2 * n_seq - 2 : 2 * n_seq]
        parts = rest[2 * n_seq :]
        mine = ids_ref[0]
        for r in peers:
            span = slice((r - 1) * slots, r * slots)
            for i in range(hp):
                h, at, narrow = places(mine, r, i)
                mk = jnp.concatenate([ref[span, narrow] for ref in mk_refs], axis=0)
                mv = jnp.concatenate([ref[span, narrow] for ref in mv_refs], axis=0)
                to = (r - 1) * hp + i
                st2_ref[to], ds_ref[to], gk, gv = memory_head(
                    mine, qn_ref[:, at], do_ref[:, at], mk, mv, st_ref[h]
                )
                parts[r - 1][0, :, narrow] = gk
                parts[r - 1][1, :, narrow] = gv

    part = sds((2, n_mem, wide), BF16)
    far_heads = heads - hp
    stats2, ds_mem, *parts = whole_call(
        memory_body,
        (sds((far_heads, 8, rows), F32), sds((far_heads, n_mem, rows), BF16))
        + (part,) * (n_seq - 1),
        place, qn, do, stats, *mk_recv, *mv_recv,
        micros=2.0,
    )
    parts_recv = to_peers("seq", parts)

    def grads_head(refs, h, at, stat, ds_m, mk, allowed, inv_c):
        q_ref, kp_ref, qn_ref, kn_ref, vp_ref, do_ref, qg_ref = refs[:7]
        gq_ref, gk_ref, gv_ref, gain_q_ref, gain_k_ref = refs[7:]
        qn_h, kn_h, do_h = qn_ref[:, at], kn_ref[:, at], do_ref[:, at]
        s = jnp.where(allowed, dot(kn_h, qn_h, NT) * scale, -jnp.inf)
        g = dot(vp_ref[:, at], do_h, NT)
        m, inv_mass, delta = stat[0:1], stat[1:2], stat[2:3]
        attend = jnp.exp(s - m) * inv_mass
        ds = (attend * (g - delta)).astype(BF16)
        gq = scale * (dot(ds, kn_h, TN) + dot(ds_m, mk, TN))
        gk = scale * dot(ds, qn_h)
        gq_ref[:, at] = gq
        gk_ref[:, at] = gk
        gv_ref[:, at] = dot(attend.astype(BF16), do_h)
        gq_q = gq * q_ref[:, at].astype(F32)
        gk_k = gk * kp_ref[:, at].astype(F32)
        to = pl.ds(h, 1)
        gain_q_ref[to, :] = jnp.sum(gq_q * inv_c[:, 0:1], axis=0, keepdims=True)
        gain_k_ref[to, :] = jnp.sum(gk_k * inv_c[:, 1:2], axis=0, keepdims=True)
        return gq_q * qg_ref[:, at]

    def grads_body(ids_ref, q_ref, kp_ref, qn_ref, kn_ref, vp_ref, do_ref, inv_ref, qg_ref, *rest):
        st_ref, ds_ref = rest[:2]
        mk_refs = rest[2 : n_seq + 1]
        outs, dq_ref = rest[n_seq + 1 : -1], rest[-1]
        refs = (q_ref, kp_ref, qn_ref, kn_ref, vp_ref, do_ref, qg_ref) + tuple(outs)
        allowed = causal_t(rows)
        inv_c = as_columns(inv_ref[...])
        total = jnp.zeros((rows, HD), F32)
        for r in peers:
            span = slice((r - 1) * slots, r * slots)
            for i in range(hp):
                h, at, narrow = places(ids_ref[0], r, i)
                mk = jnp.concatenate([ref[span, narrow] for ref in mk_refs], axis=0)
                to = (r - 1) * hp + i
                total = total + grads_head(
                    refs, h, at, st_ref[to], ds_ref[to], mk, allowed, inv_c
                )
        dq_ref[...] = total

    gain_rows = sds((heads, HD), F32)
    wide_f32 = sds((rows, cols), F32)
    narrow_f32 = sds((rows, HD), F32)
    dot_row = sds((1, rows), F32)
    far_grads = whole_call(
        grads_body,
        (wide_f32, wide_f32, wide_f32, gain_rows, gain_rows, narrow_f32),
        place, q, kp, qn, kn, vp, do, inv, qg, stats2, ds_mem, *mk_recv,
        micros=0.5,
    )

    def own_body(ids_ref, q_ref, kp_ref, qn_ref, kn_ref, vp_ref, do_ref, inv_ref, qg_ref, *rest):
        st_ref, wk_ref, wv_ref = rest[:3]
        row_refs = rest[3 : n_seq + 2]
        dq_in = rest[n_seq + 7]
        outs, (dq_ref, part_ref) = rest[n_seq + 8 : n_seq + 13], rest[n_seq + 13 :]
        refs = (q_ref, kp_ref, qn_ref, kn_ref, vp_ref, do_ref, qg_ref) + tuple(outs)
        allowed = causal_t(rows)
        inv_c = as_columns(inv_ref[...])
        mine = ids_ref[0]
        total = dq_in[...]
        for i in range(hp):
            h, at, narrow = places(mine, 0, i)
            found = []
            for tensor, w_ref in ((0, wk_ref), (1, wv_ref)):
                mem = None
                for j in range(KS):
                    span = slice(j * slots, (j + 1) * slots)
                    rows_j = jnp.concatenate([ref[tensor, span, narrow] for ref in row_refs], axis=0)
                    term = dot(rows_j, w_ref[h, j * HD : (j + 1) * HD, :])
                    mem = term if mem is None else mem + term
                found.append(mem.astype(BF16))
            stat, ds_m, gk, gv = memory_head(
                mine, qn_ref[:, at], do_ref[:, at], found[0], found[1], st_ref[h]
            )
            part_ref[0, :, narrow] = gk
            part_ref[1, :, narrow] = gv
            total = total + grads_head(refs, h, at, stat, ds_m, found[0], allowed, inv_c)
        dq_ref[...] = lane_sum_row(total)

    first_alias = 8 + 3 + n_seq - 1
    gq, gk_local, gv_local, gain_q, gain_k, dot_q, own_part = whole_call(
        own_body,
        (wide_f32, wide_f32, wide_f32, gain_rows, gain_rows, dot_row, part),
        place, q, kp, qn, kn, vp, do, inv, qg, stats, key_squeeze, value_squeeze, *rows_recv,
        *far_grads,
        aliases={first_alias + n: n for n in range(5)},
        micros=0.3,
    )

    def slots_body(*refs):
        ins, outs = refs[:n_seq], refs[n_seq:]
        for r in range(n_seq):
            for tensor in range(2):
                total = None
                for src in range(n_seq):
                    if src == r:
                        continue
                    block = (src ^ r) - 1
                    term = ins[src][tensor, block * slots : (block + 1) * slots, :].astype(F32)
                    total = term if total is None else total + term
                outs[r][tensor] = total.astype(BF16)

    slot_grad = sds((2, slots, wide), BF16)
    slot_grads = whole_call(
        slots_body, (slot_grad,) * n_seq, own_part, *parts_recv, after=(gain_q,), micros=0.3
    )

    slots_recv = to_peers("seq", slot_grads[1:])

    def weights_body(ids_ref, kn_ref, vp_ref, *rest):
        gm = rest[:n_seq]
        row_refs = rest[n_seq : 2 * n_seq - 1]
        same_ref, other_ref = rest[2 * n_seq - 1 :]
        here = pl.ds(pl.multiple_of(ids_ref[0] * wide, wide), wide)
        own = (kn_ref[:, here], vp_ref[:, here])
        first = ids_ref[1] == 0
        for i in range(hp):
            at = slice(i * HD, (i + 1) * HD)
            for j in range(KS):
                span = slice(j * slots, (j + 1) * slots)
                found = []
                for tensor in range(2):
                    lhs = jnp.concatenate(
                        [own[tensor][span, at]] + [ref[tensor, span, at] for ref in row_refs],
                        axis=0,
                    )
                    rhs = jnp.concatenate([ref[tensor, :, at] for ref in gm], axis=0)
                    found.append(dot(lhs, rhs, TN))
                to = slice((i * KS + j) * HD, (i * KS + j + 1) * HD)
                same_ref[to, :] = jnp.where(first, found[0], found[1])
                other_ref[to, :] = jnp.where(first, found[1], found[0]).astype(BF16)

    span_rows = hp * KS * HD
    w_same, w_other = whole_call(
        weights_body,
        (sds((span_rows, HD), F32), sds((span_rows, HD), BF16)),
        place, kn, vp, *slot_grads, *rows_recv,
        micros=1.1,
    )
    w_recv = to_core(w_other)

    def chunk_body(a_ref, b_ref, gq_ref, gk_ref, out_ref):
        out_ref[:span_rows, :] = (a_ref[...] + b_ref[...].astype(F32)).astype(BF16)
        gains = jnp.concatenate([gq_ref[...], gk_ref[...]], axis=0)
        out_ref[span_rows:, :] = gains.astype(BF16)

    chunk_shape = sds((span_rows + 2 * heads, HD), BF16)
    chunk = whole_call(chunk_body, chunk_shape, w_same, w_recv, gain_q, gain_k, micros=0.3, after=tuple(slots_recv))
    chunks = to_peers("seq", [chunk] * (n_seq - 1))
    chunk_other = to_core(chunk)

    def send_out(buffer, target, sems, index, at):
        copy = pltpu.make_async_copy(buffer.at[:, at], target.at[:, at], sems.at[index])
        copy.start()
        return copy

    def column_out(body, outs, n_out, *ins, micros, after=()):
        skip = len(after)
        first = (place,) if ins[0] is place else ()
        ins = ins[len(first) :]
        inside = pl.BlockSpec(memory_space=pltpu.VMEM)
        small = len(outs) - n_out
        return pl.pallas_call(
            lambda *refs: body(
                *(ask() for ask in first), *refs[: len(ins)], *refs[len(ins) + skip :]
            ),
            out_shape=outs,
            in_specs=[inside] * len(ins) + [pl.BlockSpec(memory_space=pl.ANY)] * skip,
            out_specs=(inside,) * small + (pl.BlockSpec(memory_space=pl.ANY),) * n_out,
            scratch_shapes=[pltpu.VMEM((rows, cols), BF16)] * n_out
            + [pltpu.SemaphoreType.DMA((n_out, n_seq))],
            compiler_params=pltpu.CompilerParams(vmem_limit_bytes=40 * 2**20),
            cost_estimate=cost_of(micros),
        )(*ins, *after)

    def spread_back(gm, w):
        wide_rows = dot(gm, w, NT)
        return jnp.concatenate([wide_rows[:, j * HD : (j + 1) * HD] for j in range(KS)], axis=0)

    def head_places(mine):
        for r in range(n_seq):
            for i in range(hp):
                h = (mine ^ r) * hp + i
                narrow = slice(i * HD, (i + 1) * HD)
                yield r, i, h, narrow, pl.ds(pl.multiple_of(h * HD, HD), HD)

    def back_keys_body(ids_ref, gk_ref, kp_ref, wk_ref, kg_ref, dq_ref, *rest):
        gm = rest[:n_seq]
        gkn_ref, dots_ref = rest[n_seq:]
        total = jnp.zeros((rows, HD), F32)
        for r, i, h, narrow, at in head_places(ids_ref[0]):
            gkn = gk_ref[:, at] + spread_back(gm[r][0, :, narrow], wk_ref[h])
            gkn_ref[:, at] = gkn
            total = total + gkn * kp_ref[:, at].astype(F32) * kg_ref[:, at]
        dots_ref[0:1, :] = dq_ref[...]
        dots_ref[1:2, :] = lane_sum_row(total)

    gkn, dots = whole_call(
        back_keys_body,
        (wide_f32, two_rows),
        place, gk_local, kp, key_squeeze, kg, dot_q, slot_grads[0], *slots_recv,
        micros=2.0,
        after=(chunk,),
    )

    def back_values_body(ids_ref, gv_ref, wv_ref, *rest):
        gm = rest[:n_seq]
        mark_ref, value_ref, buffer, sems = rest[n_seq:]
        mark_ref[...] = jnp.zeros_like(mark_ref)
        unorder = row_order_back(rows)
        copies = []
        for r, i, h, narrow, at in head_places(ids_ref[0]):
            value = gv_ref[:, at] + spread_back(gm[r][1, :, narrow], wv_ref[h])
            buffer[:, at] = dot(unorder, value.astype(BF16)).astype(BF16)
            if i == hp - 1:
                block = ids_ref[0] ^ r
                wide_at = pl.ds(pl.multiple_of(block * wide, wide), wide)
                copies.append(send_out(buffer, value_ref, sems.at[0], r, wide_at))
        for copy in copies:
            copy.wait()

    mark, grad_value = column_out(
        back_values_body,
        (sds((8, HD), F32), rows_shape),
        1,
        place, gv_local, value_squeeze, slot_grads[0], *slots_recv,
        micros=2.0,
        after=(dots,),
    )
    dots_parts = over_heads(dots, beside=(mark,))

    kernel_out = sds((heads, KS * HD, HD), F32)
    gains_shape = sds((1, cols), F32)

    def write_chunk(mine, r, read, buffer, sem, target):
        start = (mine ^ r) * hp
        for i in range(hp):
            buffer[start + i] = read(slice(i * KS * HD, (i + 1) * KS * HD)).astype(F32)
        at = pl.ds(start, hp)
        copy = pltpu.make_async_copy(buffer.at[at], target.at[at], sem)
        copy.start()
        return copy

    def own_chunk_body(ids_ref, same, other, *rest):
        mark_ref, gks_ref, gvs_ref, buffer_k, buffer_v, sems = rest
        mark_ref[...] = jnp.zeros_like(mark_ref)
        first = ids_ref[1] == 0
        copies = [
            write_chunk(
                ids_ref[0], 0, lambda at: jnp.where(first, same[at, :], other[at, :]),
                buffer_k, sems.at[0], gks_ref,
            ),
            write_chunk(
                ids_ref[0], 0, lambda at: jnp.where(first, other[at, :], same[at, :]),
                buffer_v, sems.at[1], gvs_ref,
            ),
        ]
        for copy in copies:
            copy.wait()

    inside = pl.BlockSpec(memory_space=pltpu.VMEM)
    outside = pl.BlockSpec(memory_space=pl.ANY)
    buffer = pltpu.VMEM(kernel_out.shape, F32)
    params = pltpu.CompilerParams(vmem_limit_bytes=40 * 2**20)
    own_mark, *part_written = pl.pallas_call(
        lambda *refs: own_chunk_body(place(), *refs),
        out_shape=(sds((8, HD), F32), kernel_out, kernel_out),
        in_specs=[inside, inside],
        out_specs=(inside, outside, outside),
        scratch_shapes=[buffer, buffer, pltpu.SemaphoreType.DMA((2,))],
        compiler_params=params,
        cost_estimate=cost_of(0.01),
    )(chunk, chunk_other)

    def norms_body(q_ref, kp_ref, gq_ref, gkn_ref, qg_ref, kg_ref, inv_ref, *rest):
        dots_a, dots_b, mark_ref, out_q, out_k, buffer_q, buffer_k, sems = rest
        mark_ref[...] = jnp.zeros_like(mark_ref)
        total = dots_a[...] + dots_b[...]
        inv_rows = inv_ref[...]
        inv_c = as_columns(inv_rows)
        pull = as_columns(inv_rows * inv_rows * inv_rows * total / full_width)
        unorder = row_order_back(rows)
        copies = []
        for r in range(n_seq):
            at = slice(r * wide, (r + 1) * wide)
            buffer_q[:, at] = (
                inv_c[:, 0:1] * qg_ref[:, at] * gq_ref[:, at]
                - q_ref[:, at].astype(F32) * pull[:, 0:1]
            ).astype(BF16)
            copies.append(send_out(buffer_q, out_q, sems.at[0], r, at))
            grad_k = (
                inv_c[:, 1:2] * kg_ref[:, at] * gkn_ref[:, at]
                - kp_ref[:, at].astype(F32) * pull[:, 1:2]
            ).astype(BF16)
            buffer_k[:, at] = dot(unorder, grad_k).astype(BF16)
            copies.append(send_out(buffer_k, out_k, sems.at[1], r, at))
        for copy in copies:
            copy.wait()

    norms_mark, grad_query, grad_key = column_out(
        norms_body,
        (sds((8, HD), F32), rows_shape, rows_shape),
        2,
        q, kp, gq, gkn, qg, kg, inv, *dots_parts,
        micros=0.01,
        after=(own_mark,),
    )

    def pack_body(*refs):
        for r in range(n_seq - 1):
            refs[n_seq - 1][r] = refs[r][...]

    packed_shape = sds((n_seq - 1,) + chunk_shape.shape, BF16)
    packed = whole_call(pack_body, packed_shape, *chunks, micros=0.1, after=(norms_mark, own_mark))
    packed_other = to_core(packed)

    def back_gain(mine, chunk_0, chunks_ref, kg_ref, wk_ref, out_ref):
        sums = []
        for r in range(n_seq):
            for i in range(hp):
                h = (mine ^ r) * hp + i
                total = jnp.zeros((HD, HD), F32)
                for j in range(KS):
                    span = slice((i * KS + j) * HD, (i * KS + j + 1) * HD)
                    grad_w = chunk_0[span, :] if r == 0 else chunks_ref[r - 1, span, :]
                    kernel = wk_ref[h, j * HD : (j + 1) * HD, :]
                    total = total + grad_w.astype(F32) * kernel.astype(F32)
                sums.append(total)
        sums = jnp.concatenate(sums, axis=0)
        high = sums.astype(BF16)
        low = (sums - high.astype(F32)).astype(BF16)
        ones = jnp.ones((16, HD), BF16)
        row = (dot(ones, high, NT) + dot(ones, low, NT))[0:1]
        for r in range(n_seq):
            at = pl.ds(pl.multiple_of((mine ^ r) * wide, wide), wide)
            out_ref[:, at] = row[:, r * wide : (r + 1) * wide] / kg_ref[:, at]

    def write_chunks(mine, chunks_ref, buffer, sems, target):
        return [
            write_chunk(
                mine, r, lambda at, r=r: chunks_ref[r - 1, at, :], buffer, sems.at[r], target
            )
            for r in peers
        ]

    def this_core_body(ids_ref, same_0, same, kg_ref, wk_ref, gks_in, gvs_in, *rest):
        back_ref, gks_ref, gvs_ref, buffer, sems = rest

        @pl.when(ids_ref[1] == 0)
        def _():
            copies = write_chunks(ids_ref[0], same, buffer, sems, gks_ref)
            back_gain(ids_ref[0], same_0, same, kg_ref, wk_ref, back_ref)
            for copy in copies:
                copy.wait()

        @pl.when(ids_ref[1] == 1)
        def _():
            copies = write_chunks(ids_ref[0], same, buffer, sems, gvs_ref)
            back_ref[...] = jnp.zeros_like(back_ref)
            for copy in copies:
                copy.wait()

    def other_core_body(ids_ref, same_0, other_0, same, other, back, kg_ref, wk_ref, *rest):
        gks_ref, gvs_ref, gq_out, gk_out, buffer, gq_row, gk_row, sems = rest[2:]

        def finish(copies):
            total = same_0[span_rows:, :].astype(F32) + other_0[span_rows:, :].astype(F32)
            for r in range(n_seq - 1):
                total = total + same[r, span_rows:, :].astype(F32)
                total = total + other[r, span_rows:, :].astype(F32)
            as_row = lambda x: jnp.concatenate([x[h : h + 1] for h in range(heads)], axis=1)
            gq_row[...] = as_row(total[:heads])
            gk_row[...] += as_row(total[heads:])
            copies.append(pltpu.make_async_copy(gq_row, gq_out, sems.at[0]))
            copies[-1].start()
            copies.append(pltpu.make_async_copy(gk_row, gk_out, sems.at[n_seq]))
            copies[-1].start()
            for copy in copies:
                copy.wait()

        @pl.when(ids_ref[1] == 0)
        def _():
            copies = write_chunks(ids_ref[0], other, buffer, sems, gvs_ref)
            gk_row[...] = back[...]
            finish(copies)

        @pl.when(ids_ref[1] == 1)
        def _():
            copies = write_chunks(ids_ref[0], other, buffer, sems, gks_ref)
            back_gain(ids_ref[0], other_0, other, kg_ref, wk_ref, gk_row)
            finish(copies)

    back_row, *part_written = pl.pallas_call(
        lambda *refs: this_core_body(place(), *refs),
        out_shape=(gains_shape, kernel_out, kernel_out),
        in_specs=[inside] * 4 + [outside] * 2,
        out_specs=(inside, outside, outside),
        input_output_aliases={4: 1, 5: 2},
        scratch_shapes=[buffer, pltpu.SemaphoreType.DMA((n_seq,))],
        compiler_params=params,
        cost_estimate=cost_of(1.6),
    )(chunk, packed, kg, key_squeeze, *part_written)
    gks, gvs, gain_q_all, gain_k_all = pl.pallas_call(
        lambda *refs: other_core_body(place(), *refs),
        out_shape=(kernel_out, kernel_out, gains_shape, gains_shape),
        in_specs=[inside] * 7 + [outside] * 2,
        out_specs=(outside,) * 4,
        input_output_aliases={7: 0, 8: 1},
        scratch_shapes=[
            buffer,
            pltpu.VMEM((1, cols), F32),
            pltpu.VMEM((1, cols), F32),
            pltpu.SemaphoreType.DMA((n_seq + 1,)),
        ],
        compiler_params=params,
        cost_estimate=cost_of(2.2),
    )(chunk, chunk_other, packed, packed_other, back_row, kg, key_squeeze, *part_written)
    return (
        grad_query[None],
        grad_key[None],
        grad_value[None],
        gain_q_all.reshape(cols),
        gain_k_all.reshape(cols),
        gks,
        gvs,
    )


def solution(mesh):
    placed = (
        P("dp", "seq", "head"),
        P("dp", "seq", "head"),
        P("dp", "seq", "head"),
        P("head"),
        P("head"),
        P("head", None, None),
        P("head", None, None),
        P("dp", "seq", "head"),
    )
    return jax.shard_map(
        on_device,
        mesh=mesh,
        in_specs=placed,
        out_specs=(
            P("dp", "seq", "head"),
            P("dp", "seq", "head"),
            P("dp", "seq", "head"),
            P("head"),
            P("head"),
            P("head", None, None),
            P("head", None, None),
        ),
        check_vma=False,
    )
```

```python
import jax
import jax.numpy as jnp
from jax import lax
from jax.experimental import pallas as pl
from jax.experimental.pallas import tpu as pltpu
from jax.sharding import PartitionSpec as P

HD = 128
KS = 4
HH = 4096


epsilon = 1e-06


def unfold_slots(source, head_count):
    batch_size, row_count, widths = source.shape
    return (
        source.reshape(batch_size, row_count // KS, KS, head_count, HD)
        .transpose(0, 1, 3, 2, 4)
        .reshape(batch_size, row_count // KS, head_count, KS * HD)
    )


def fold_slots(source):
    batch_size, slot_count, head_count, spans = source.shape
    return (
        source.reshape(batch_size, slot_count, head_count, KS, HD)
        .transpose(0, 1, 3, 2, 4)
        .reshape(batch_size, slot_count * KS, head_count * HD)
    )


def on_device_any(
    query_heads, key_heads, value_heads, query_gain, key_gain, key_squeeze, value_squeeze, grad_out
):
    batch_size, row_count, widths = query_heads.shape
    head_count = widths // HD
    slot_count = row_count // KS
    score_scale = HD ** (-0.5)
    own_limit = lax.axis_index("seq") * slot_count
    q_full = query_heads.astype(jnp.float32)
    k_full = key_heads.astype(jnp.float32)
    sum_q, sum_k = lax.psum((jnp.sum(q_full * q_full, -1), jnp.sum(k_full * k_full, -1)), "head")
    inv_q = lax.rsqrt(sum_q / HH + epsilon)[..., None]
    inv_k = lax.rsqrt(sum_k / HH + epsilon)[..., None]
    q_norm = (q_full * inv_q * query_gain).astype(jnp.bfloat16)
    k_norm = (k_full * inv_k * key_gain).astype(jnp.bfloat16)
    k_unf = unfold_slots(k_norm, head_count)
    v_unf = unfold_slots(value_heads, head_count)
    mem_k = (
        jnp.einsum("bmhc,hcd->bmhd", k_unf, key_squeeze, preferred_element_type=jnp.float32)
        .astype(jnp.bfloat16)
        .reshape(batch_size, slot_count, widths)
    )
    mem_v = (
        jnp.einsum("bmhc,hcd->bmhd", v_unf, value_squeeze, preferred_element_type=jnp.float32)
        .astype(jnp.bfloat16)
        .reshape(batch_size, slot_count, widths)
    )
    queries = q_norm.reshape(batch_size, row_count, head_count, HD)
    key_loc = k_norm.reshape(batch_size, row_count, head_count, HD)
    value_loc = value_heads.reshape(batch_size, row_count, head_count, HD)
    cotangent = grad_out.reshape(batch_size, row_count, head_count, HD)
    positions = jnp.arange(row_count)
    causal = positions[:, None] >= positions[None, :]
    scores_loc = jnp.where(
        causal,
        jnp.einsum("bthd,buhd->bhtu", queries, key_loc, preferred_element_type=jnp.float32)
        * score_scale,
        -jnp.inf,
    )
    grads_loc = jnp.einsum(
        "bthd,buhd->bhtu", cotangent, value_loc, preferred_element_type=jnp.float32
    )
    all_k, all_v = (
        lax.all_gather(mem_k, "seq", axis=1, tiled=True),
        lax.all_gather(mem_v, "seq", axis=1, tiled=True),
    )
    piece_rows = all_k.shape[1]
    key_rows = all_k.reshape(batch_size, piece_rows, head_count, HD)
    value_rows = all_v.reshape(batch_size, piece_rows, head_count, HD)
    allowed = jnp.arange(piece_rows) < own_limit
    scores = jnp.where(
        allowed,
        jnp.einsum("bthd,buhd->bhtu", queries, key_rows, preferred_element_type=jnp.float32)
        * score_scale,
        -jnp.inf,
    )
    gradients = jnp.einsum(
        "bthd,buhd->bhtu", cotangent, value_rows, preferred_element_type=jnp.float32
    )
    key_rows, scores_mem, grads_mem = (key_rows, scores, gradients)
    peak = jnp.maximum(jnp.max(scores_loc, -1), jnp.max(scores_mem, -1))
    summed = jnp.sum(jnp.exp(scores_loc - peak[..., None]), -1) + jnp.sum(
        jnp.exp(scores_mem - peak[..., None]), -1
    )
    log_mass = peak + jnp.log(summed)
    row_delta = jnp.sum(jnp.exp(scores_loc - log_mass[..., None]) * grads_loc, -1) + jnp.sum(
        jnp.exp(scores_mem - log_mass[..., None]) * grads_mem, -1
    )
    piece_rows = key_rows.shape[1]
    attend = jnp.exp(scores_mem - log_mass[..., None])
    d_scores = (attend * (grads_mem - row_delta[..., None])).astype(jnp.bfloat16)
    grad_q = score_scale * jnp.einsum(
        "bhtu,buhd->bthd", d_scores, key_rows, preferred_element_type=jnp.float32
    )
    grad_k = score_scale * jnp.einsum(
        "bhtu,bthd->buhd", d_scores, queries, preferred_element_type=jnp.float32
    )
    grad_v = jnp.einsum(
        "bhtu,bthd->buhd",
        attend.astype(jnp.bfloat16),
        cotangent,
        preferred_element_type=jnp.float32,
    )
    stacked = jnp.stack(
        (
            grad_k.reshape(batch_size, piece_rows, widths),
            grad_v.reshape(batch_size, piece_rows, widths),
        )
    )
    attend_loc = jnp.exp(scores_loc - log_mass[..., None])
    d_loc = (attend_loc * (grads_loc - row_delta[..., None])).astype(jnp.bfloat16)
    grad_qn = (
        score_scale
        * jnp.einsum("bhtu,buhd->bthd", d_loc, key_loc, preferred_element_type=jnp.float32)
        + grad_q
    ).reshape(batch_size, row_count, widths)
    grad_kn_local = score_scale * jnp.einsum(
        "bhtu,bthd->buhd", d_loc, queries, preferred_element_type=jnp.float32
    )
    grad_v_local = jnp.einsum(
        "bhtu,bthd->buhd",
        attend_loc.astype(jnp.bfloat16),
        cotangent,
        preferred_element_type=jnp.float32,
    )
    mine = lax.psum_scatter(stacked.astype(jnp.bfloat16), "seq", scatter_dimension=2, tiled=True)
    grad_mem_k = mine[0].reshape(batch_size, slot_count, head_count, HD)
    grad_mem_v = mine[1].reshape(batch_size, slot_count, head_count, HD)
    squeeze_k_part = jnp.einsum(
        "bmhc,bmhd->hcd", k_unf, grad_mem_k, preferred_element_type=jnp.float32
    )
    squeeze_v_part = jnp.einsum(
        "bmhc,bmhd->hcd", v_unf, grad_mem_v, preferred_element_type=jnp.float32
    )
    back_k = fold_slots(
        jnp.einsum("bmhd,hcd->bmhc", grad_mem_k, key_squeeze, preferred_element_type=jnp.float32)
    )
    back_v = fold_slots(
        jnp.einsum("bmhd,hcd->bmhc", grad_mem_v, value_squeeze, preferred_element_type=jnp.float32)
    )
    grad_kn = grad_kn_local.reshape(batch_size, row_count, widths) + back_k
    grad_value = (grad_v_local.reshape(batch_size, row_count, widths) + back_v).astype(jnp.bfloat16)
    dot_q, dot_k = lax.psum(
        (jnp.sum(query_gain * grad_qn * q_full, -1), jnp.sum(key_gain * grad_kn * k_full, -1)),
        "head",
    )
    grad_query = (
        inv_q * query_gain * grad_qn - q_full * inv_q**3 * dot_q[..., None] / HH
    ).astype(jnp.bfloat16)
    grad_key = (inv_k * key_gain * grad_kn - k_full * inv_k**3 * dot_k[..., None] / HH).astype(
        jnp.bfloat16
    )
    gain_q_part = jnp.sum(grad_qn * q_full * inv_q, (0, 1))
    gain_k_part = jnp.sum(grad_kn * k_full * inv_k, (0, 1))
    grad_query_gain, grad_key_gain, grad_key_squeeze, grad_value_squeeze = (
        lax.psum(gain_q_part.astype(jnp.bfloat16), ("seq", "dp")).astype(jnp.float32),
        lax.psum(gain_k_part.astype(jnp.bfloat16), ("seq", "dp")).astype(jnp.float32),
        lax.psum(squeeze_k_part.astype(jnp.bfloat16), ("seq", "dp")).astype(jnp.float32),
        lax.psum(squeeze_v_part.astype(jnp.bfloat16), ("seq", "dp")).astype(jnp.float32),
    )
    return (
        grad_query,
        grad_key,
        grad_value,
        grad_query_gain,
        grad_key_gain,
        grad_key_squeeze,
        grad_value_squeeze,
    )


F32 = jnp.float32
BF16 = jnp.bfloat16
NN = (((1,), (0,)), ((), ()))
NT = (((1,), (1,)), ((), ()))
TN = (((0,), (0,)), ((), ()))


def dot(a, b, dims=NN):
    return lax.dot_general(a, b, dims, preferred_element_type=F32)


def sds(shape, dtype):
    return jax.ShapeDtypeStruct(shape, dtype)


def place():
    return lax.axis_index("seq"), lax.axis_index("dp")


def cost_of(micros):
    return pl.CostEstimate(
        flops=int(micros * 1e9), bytes_accessed=int(micros * 3.6e6), transcendentals=0
    )


def whole_call(body, outs, *ins, micros=1.0, after=(), scratch=(), vmem=40, aliases=None):
    first = (place,) if ins[0] is place else ()
    ins = ins[len(first) :]
    n_out = len(jax.tree.leaves(outs))
    skip = len(after)
    space = pl.BlockSpec(memory_space=pltpu.VMEM)
    return pl.pallas_call(
        lambda *refs: body(
            *(ask() for ask in first), *refs[: len(ins)], *refs[len(ins) + skip :]
        ),
        out_shape=outs,
        in_specs=[space] * len(ins) + [pl.BlockSpec(memory_space=pl.ANY)] * skip,
        out_specs=jax.tree.map(lambda _: space, outs),
        scratch_shapes=list(scratch),
        input_output_aliases=aliases or {},
        compiler_params=pltpu.CompilerParams(vmem_limit_bytes=vmem * 2**20),
        cost_estimate=cost_of(micros),
    )(*ins, *after)


def row_order(rows):
    slots = rows // KS
    r = lax.broadcasted_iota(jnp.int32, (rows, rows), 0)
    c = lax.broadcasted_iota(jnp.int32, (rows, rows), 1)
    return jnp.where(c == KS * (r % slots) + r // slots, 1.0, 0.0).astype(BF16)


def row_order_back(rows):
    slots = rows // KS
    r = lax.broadcasted_iota(jnp.int32, (rows, rows), 0)
    c = lax.broadcasted_iota(jnp.int32, (rows, rows), 1)
    return jnp.where(r == KS * (c % slots) + c // slots, 1.0, 0.0).astype(BF16)


def causal_t(rows):
    slots = rows // KS
    u = lax.broadcasted_iota(jnp.int32, (rows, rows), 0)
    t = lax.broadcasted_iota(jnp.int32, (rows, rows), 1)
    return KS * (u % slots) + u // slots <= t


def fold_lanes(x):
    total = x[:, :HD]
    for i in range(1, x.shape[1] // HD):
        total = total + x[:, i * HD : (i + 1) * HD]
    return total


def lane_sum_row(x):
    return jnp.sum(x.T, axis=0, keepdims=True)


def as_columns(rows):
    pad = jnp.zeros((8 - rows.shape[0], rows.shape[1]), F32)
    return jnp.concatenate([rows, pad], axis=0).T


def on_device(
    query_heads, key_heads, value_heads, query_gain, key_gain, key_squeeze, value_squeeze, grad_out
):
    n_seq, n_head = lax.axis_size("seq"), lax.axis_size("head")
    batch_size, rows, cols = query_heads.shape
    heads = cols // HD
    if batch_size != 1 or n_seq & (n_seq - 1) or heads % n_seq or lax.axis_size("dp") != 2:
        return on_device_any(
            query_heads,
            key_heads,
            value_heads,
            query_gain,
            key_gain,
            key_squeeze,
            value_squeeze,
            grad_out,
        )
    slots = rows // KS
    hp = heads // n_seq
    wide = hp * HD
    mem_rows = n_seq * slots
    peers = range(1, n_seq)
    n_mem = (n_seq - 1) * slots
    scale = HD ** (-0.5)
    full_width = cols * n_head

    def to_peers(axis, arrays):
        n = lax.axis_size(axis)
        return [
            lax.ppermute(a, axis, [(i, i ^ k) for i in range(n)])
            for k, a in zip(range(1, n), arrays)
        ]

    def sum_body(a_ref, b_ref, out_ref):
        out_ref[...] = a_ref[...] + b_ref[...]

    def over_heads(a, beside=()):
        step, got = 1, None
        while step < n_head:
            if got is not None:
                a = whole_call(sum_body, sds(a.shape, a.dtype), a, got, micros=0.1, after=beside)
            got = lax.ppermute(a, "head", [(i, i ^ step) for i in range(n_head)])
            step *= 2
        return a, got

    def to_core(a):
        return lax.ppermute(a, "dp", [(0, 1), (1, 0)])

    q = query_heads[0]
    k = key_heads[0]
    v = value_heads[0]
    do = grad_out[0]
    qg = query_gain.reshape(1, cols)
    kg = key_gain.reshape(1, cols)

    def squares_body(q_ref, k_ref, ss_ref):
        qf = q_ref[...].astype(F32)
        ss_ref[0:1, :] = lane_sum_row(fold_lanes(qf * qf))
        kf = k_ref[...].astype(F32)
        ss_ref[1:2, :] = lane_sum_row(fold_lanes(kf * kf))

    two_rows = sds((2, rows), F32)
    ss = whole_call(squares_body, two_rows, q, k, micros=1.5, vmem=62)
    ss_parts = [ss] + to_peers("head", [ss] * (n_head - 1))

    def compress(source, w_ref, out_ref):
        for h in range(heads):
            total = None
            for j in range(KS):
                part = dot(
                    source[j * slots : (j + 1) * slots, h * HD : (h + 1) * HD],
                    w_ref[h, j * HD : (j + 1) * HD, :],
                )
                total = part if total is None else total + part
            block = h // hp
            out_ref[
                block * slots : (block + 1) * slots, (h % hp) * HD : (h % hp + 1) * HD
            ] = total.astype(BF16)

    def pack_slots(mine, mem_ref, sends):
        for k, send in zip(peers, sends):
            for r in peers:
                source = pl.ds(pl.multiple_of((mine ^ k ^ r) * slots, slots), slots)
                send[(r - 1) * slots : r * slots, :] = mem_ref[source, :]

    def values_body(ids_ref, v_ref, w_ref, vp_ref, *rest):
        sends, mem_ref = rest[:-1], rest[-1]
        vp_ref[...] = dot(row_order(rows), v_ref[...]).astype(BF16)
        compress(vp_ref, w_ref, mem_ref)
        pack_slots(ids_ref[0], mem_ref, sends)

    rows_shape = sds((rows, cols), BF16)
    mem_shape = sds((mem_rows, wide), BF16)
    slots_packet = sds((n_mem, wide), BF16)
    mem_scratch = [pltpu.VMEM(mem_shape.shape, BF16)]
    vp, *mv_sends = whole_call(
        values_body,
        (rows_shape,) + (slots_packet,) * (n_seq - 1),
        place, v, value_squeeze,
        scratch=mem_scratch,
        micros=0.8,
    )
    mv_recv = to_peers("seq", mv_sends)

    def keys_body(ids_ref, k_ref, kg_ref, w_ref, *rest):
        ss_refs = rest[:n_head]
        inv_ref, kn_ref = rest[n_head : n_head + 2]
        sends, mem_ref = rest[n_head + 2 : -1], rest[-1]
        total = ss_refs[0][...]
        for other in ss_refs[1:]:
            total = total + other[...]
        natural = as_columns(lax.rsqrt(total / full_width + epsilon))
        order = row_order(rows)
        high = natural.astype(BF16)
        rest_1 = natural - high.astype(F32)
        middle = rest_1.astype(BF16)
        low = (rest_1 - middle.astype(F32)).astype(BF16)
        ordered = dot(order, high) + dot(order, middle) + dot(order, low)
        inv_c = jnp.concatenate([natural[:, 0:1], ordered[:, 1:2], natural[:, 2:]], axis=1)
        inv_ref[...] = inv_c.T[:2]
        normed = (k_ref[...].astype(F32) * natural[:, 1:2] * kg_ref[...]).astype(BF16)
        kn_ref[...] = dot(order, normed).astype(BF16)
        compress(kn_ref, w_ref, mem_ref)
        pack_slots(ids_ref[0], mem_ref, sends)

    inv, kn, *mk_sends = whole_call(
        keys_body,
        (two_rows, rows_shape) + (slots_packet,) * (n_seq - 1),
        place, k, kg, key_squeeze, *ss_parts,
        scratch=mem_scratch,
        micros=20.0,
    )
    mk_recv = to_peers("seq", mk_sends)

    def local_body(q_ref, qg_ref, inv_ref, kn_ref, vp_ref, do_ref, qn_ref, st_ref):
        allowed = causal_t(rows)
        inv_c = as_columns(inv_ref[...])[:, 0:1]
        for h in range(heads):
            at = slice(h * HD, (h + 1) * HD)
            qn_h = (q_ref[:, at].astype(F32) * inv_c * qg_ref[:, at]).astype(BF16)
            qn_ref[:, at] = qn_h
            s = jnp.where(allowed, dot(kn_ref[:, at], qn_h, NT) * scale, -jnp.inf)
            g = dot(vp_ref[:, at], do_ref[:, at], NT)
            m = jnp.max(s, axis=0, keepdims=True)
            p = jnp.exp(s - m)
            st_ref[h, 0:1, :] = m
            st_ref[h, 1:2, :] = jnp.sum(p, axis=0, keepdims=True)
            st_ref[h, 2:3, :] = jnp.sum(p * g, axis=0, keepdims=True)

    stat_shape = sds((heads, 8, rows), F32)
    qn, stats = whole_call(
        local_body, (rows_shape, stat_shape), q, qg, inv, kn, vp, do,
        micros=0.5,
        after=tuple(mv_recv),
    )

    def rows_body(ids_ref, kn_ref, vp_ref, k_ref, *outs):
        sends, kp_ref = outs[:-1], outs[-1]
        kp_ref[...] = dot(row_order(rows), k_ref[...]).astype(BF16)
        for r, send in zip(peers, sends):
            dest = ids_ref[0] ^ r
            at = pl.ds(pl.multiple_of(dest * wide, wide), wide)
            send[0] = kn_ref[:, at]
            send[1] = vp_ref[:, at]

    row_pair = sds((2, rows, wide), BF16)
    *row_sends, kp = whole_call(
        rows_body,
        (row_pair,) * (n_seq - 1) + (rows_shape,),
        place, kn, vp, k,
        after=(stats,),
        micros=0.7,
    )
    rows_recv = to_peers("seq", row_sends)

    def memory_head(mine, qn_h, do_h, mk, mv, stat):
        raw = dot(mk, qn_h, NT) * scale
        s = jnp.concatenate(
            [
                jnp.where((mine ^ src) < mine, raw[(src - 1) * slots : src * slots], -jnp.inf)
                for src in peers
            ],
            axis=0,
        )
        g = dot(mv, do_h, NT)
        m_loc, l_loc, d_loc = stat[0:1], stat[1:2], stat[2:3]
        m = jnp.maximum(m_loc, jnp.max(s, axis=0, keepdims=True))
        p = jnp.exp(s - m)
        shrink = jnp.exp(m_loc - m)
        mass = l_loc * shrink + jnp.sum(p, axis=0, keepdims=True)
        inv_mass = 1.0 / mass
        delta = (d_loc * shrink + jnp.sum(p * g, axis=0, keepdims=True)) * inv_mass
        attend = p * inv_mass
        ds = (attend * (g - delta)).astype(BF16)
        gk = (dot(ds, qn_h) * scale).astype(BF16)
        gv = dot(attend.astype(BF16), do_h).astype(BF16)
        return jnp.concatenate([m, inv_mass, delta, stat[3:]], axis=0), ds, gk, gv

    def places(mine, r, i):
        h = (mine ^ r) * hp + i
        return h, pl.ds(pl.multiple_of(h * HD, HD), HD), slice(i * HD, (i + 1) * HD)

    def memory_body(ids_ref, qn_ref, do_ref, st_ref, *rest):
        mk_refs = rest[: n_seq - 1]
        mv_refs = rest[n_seq - 1 : 2 * n_seq - 2]
        st2_ref, ds_ref = rest[2 * n_seq - 2 : 2 * n_seq]
        parts = rest[2 * n_seq :]
        mine = ids_ref[0]
        for r in peers:
            span = slice((r - 1) * slots, r * slots)
            for i in range(hp):
                h, at, narrow = places(mine, r, i)
                mk = jnp.concatenate([ref[span, narrow] for ref in mk_refs], axis=0)
                mv = jnp.concatenate([ref[span, narrow] for ref in mv_refs], axis=0)
                to = (r - 1) * hp + i
                st2_ref[to], ds_ref[to], gk, gv = memory_head(
                    mine, qn_ref[:, at], do_ref[:, at], mk, mv, st_ref[h]
                )
                parts[r - 1][0, :, narrow] = gk
                parts[r - 1][1, :, narrow] = gv

    part = sds((2, n_mem, wide), BF16)
    far_heads = heads - hp
    stats2, ds_mem, *parts = whole_call(
        memory_body,
        (sds((far_heads, 8, rows), F32), sds((far_heads, n_mem, rows), BF16))
        + (part,) * (n_seq - 1),
        place, qn, do, stats, *mk_recv, *mv_recv,
        micros=2.0,
    )
    parts_recv = to_peers("seq", parts)

    def grads_head(refs, h, at, stat, ds_m, mk, allowed, inv_c):
        q_ref, kp_ref, qn_ref, kn_ref, vp_ref, do_ref, qg_ref = refs[:7]
        gq_ref, gk_ref, gv_ref, gain_q_ref, gain_k_ref = refs[7:]
        qn_h, kn_h, do_h = qn_ref[:, at], kn_ref[:, at], do_ref[:, at]
        s = jnp.where(allowed, dot(kn_h, qn_h, NT) * scale, -jnp.inf)
        g = dot(vp_ref[:, at], do_h, NT)
        m, inv_mass, delta = stat[0:1], stat[1:2], stat[2:3]
        attend = jnp.exp(s - m) * inv_mass
        ds = (attend * (g - delta)).astype(BF16)
        gq = scale * (dot(ds, kn_h, TN) + dot(ds_m, mk, TN))
        gk = scale * dot(ds, qn_h)
        gq_ref[:, at] = gq
        gk_ref[:, at] = gk
        gv_ref[:, at] = dot(attend.astype(BF16), do_h)
        gq_q = gq * q_ref[:, at].astype(F32)
        gk_k = gk * kp_ref[:, at].astype(F32)
        to = pl.ds(h, 1)
        gain_q_ref[to, :] = jnp.sum(gq_q * inv_c[:, 0:1], axis=0, keepdims=True)
        gain_k_ref[to, :] = jnp.sum(gk_k * inv_c[:, 1:2], axis=0, keepdims=True)
        return gq_q * qg_ref[:, at]

    def grads_body(ids_ref, q_ref, kp_ref, qn_ref, kn_ref, vp_ref, do_ref, inv_ref, qg_ref, *rest):
        st_ref, ds_ref = rest[:2]
        mk_refs = rest[2 : n_seq + 1]
        outs, dq_ref = rest[n_seq + 1 : -1], rest[-1]
        refs = (q_ref, kp_ref, qn_ref, kn_ref, vp_ref, do_ref, qg_ref) + tuple(outs)
        allowed = causal_t(rows)
        inv_c = as_columns(inv_ref[...])
        total = jnp.zeros((rows, HD), F32)
        for r in peers:
            span = slice((r - 1) * slots, r * slots)
            for i in range(hp):
                h, at, narrow = places(ids_ref[0], r, i)
                mk = jnp.concatenate([ref[span, narrow] for ref in mk_refs], axis=0)
                to = (r - 1) * hp + i
                total = total + grads_head(
                    refs, h, at, st_ref[to], ds_ref[to], mk, allowed, inv_c
                )
        dq_ref[...] = total

    gain_rows = sds((heads, HD), F32)
    wide_f32 = sds((rows, cols), F32)
    narrow_f32 = sds((rows, HD), F32)
    dot_row = sds((1, rows), F32)
    far_grads = whole_call(
        grads_body,
        (wide_f32, wide_f32, wide_f32, gain_rows, gain_rows, narrow_f32),
        place, q, kp, qn, kn, vp, do, inv, qg, stats2, ds_mem, *mk_recv,
        micros=0.5,
    )

    def own_body(ids_ref, q_ref, kp_ref, qn_ref, kn_ref, vp_ref, do_ref, inv_ref, qg_ref, *rest):
        st_ref, wk_ref, wv_ref = rest[:3]
        row_refs = rest[3 : n_seq + 2]
        dq_in = rest[n_seq + 7]
        outs, (dq_ref, part_ref) = rest[n_seq + 8 : n_seq + 13], rest[n_seq + 13 :]
        refs = (q_ref, kp_ref, qn_ref, kn_ref, vp_ref, do_ref, qg_ref) + tuple(outs)
        allowed = causal_t(rows)
        inv_c = as_columns(inv_ref[...])
        mine = ids_ref[0]
        total = dq_in[...]
        for i in range(hp):
            h, at, narrow = places(mine, 0, i)
            found = []
            for tensor, w_ref in ((0, wk_ref), (1, wv_ref)):
                mem = None
                for j in range(KS):
                    span = slice(j * slots, (j + 1) * slots)
                    rows_j = jnp.concatenate([ref[tensor, span, narrow] for ref in row_refs], axis=0)
                    term = dot(rows_j, w_ref[h, j * HD : (j + 1) * HD, :])
                    mem = term if mem is None else mem + term
                found.append(mem.astype(BF16))
            stat, ds_m, gk, gv = memory_head(
                mine, qn_ref[:, at], do_ref[:, at], found[0], found[1], st_ref[h]
            )
            part_ref[0, :, narrow] = gk
            part_ref[1, :, narrow] = gv
            total = total + grads_head(refs, h, at, stat, ds_m, found[0], allowed, inv_c)
        dq_ref[...] = lane_sum_row(total)

    first_alias = 8 + 3 + n_seq - 1
    gq, gk_local, gv_local, gain_q, gain_k, dot_q, own_part = whole_call(
        own_body,
        (wide_f32, wide_f32, wide_f32, gain_rows, gain_rows, dot_row, part),
        place, q, kp, qn, kn, vp, do, inv, qg, stats, key_squeeze, value_squeeze, *rows_recv,
        *far_grads,
        aliases={first_alias + n: n for n in range(5)},
        micros=0.3,
    )

    def slots_body(*refs):
        ins, outs = refs[:n_seq], refs[n_seq:]
        for r in range(n_seq):
            for tensor in range(2):
                total = None
                for src in range(n_seq):
                    if src == r:
                        continue
                    block = (src ^ r) - 1
                    term = ins[src][tensor, block * slots : (block + 1) * slots, :].astype(F32)
                    total = term if total is None else total + term
                outs[r][tensor] = total.astype(BF16)

    slot_grad = sds((2, slots, wide), BF16)
    slot_grads = whole_call(
        slots_body, (slot_grad,) * n_seq, own_part, *parts_recv, after=(gain_q,), micros=0.3
    )

    slots_recv = to_peers("seq", slot_grads[1:])

    def weights_body(ids_ref, kn_ref, vp_ref, *rest):
        gm = rest[:n_seq]
        row_refs = rest[n_seq : 2 * n_seq - 1]
        same_ref, other_ref = rest[2 * n_seq - 1 :]
        here = pl.ds(pl.multiple_of(ids_ref[0] * wide, wide), wide)
        own = (kn_ref[:, here], vp_ref[:, here])
        first = ids_ref[1] == 0
        for i in range(hp):
            at = slice(i * HD, (i + 1) * HD)
            for j in range(KS):
                span = slice(j * slots, (j + 1) * slots)
                found = []
                for tensor in range(2):
                    lhs = jnp.concatenate(
                        [own[tensor][span, at]] + [ref[tensor, span, at] for ref in row_refs],
                        axis=0,
                    )
                    rhs = jnp.concatenate([ref[tensor, :, at] for ref in gm], axis=0)
                    found.append(dot(lhs, rhs, TN))
                to = slice((i * KS + j) * HD, (i * KS + j + 1) * HD)
                same_ref[to, :] = jnp.where(first, found[0], found[1])
                other_ref[to, :] = jnp.where(first, found[1], found[0]).astype(BF16)

    span_rows = hp * KS * HD
    w_same, w_other = whole_call(
        weights_body,
        (sds((span_rows, HD), F32), sds((span_rows, HD), BF16)),
        place, kn, vp, *slot_grads, *rows_recv,
        micros=1.1,
    )
    w_recv = to_core(w_other)

    def chunk_body(a_ref, b_ref, gq_ref, gk_ref, out_ref):
        out_ref[:span_rows, :] = (a_ref[...] + b_ref[...].astype(F32)).astype(BF16)
        gains = jnp.concatenate([gq_ref[...], gk_ref[...]], axis=0)
        out_ref[span_rows:, :] = gains.astype(BF16)

    chunk_shape = sds((span_rows + 2 * heads, HD), BF16)
    chunk = whole_call(chunk_body, chunk_shape, w_same, w_recv, gain_q, gain_k, micros=0.3, after=(slots_recv[1],))
    chunks = to_peers("seq", [chunk] * (n_seq - 1))
    chunk_other = to_core(chunk)

    def send_out(buffer, target, sems, index, at):
        copy = pltpu.make_async_copy(buffer.at[:, at], target.at[:, at], sems.at[index])
        copy.start()
        return copy

    def column_out(body, outs, n_out, *ins, micros, after=()):
        skip = len(after)
        first = (place,) if ins[0] is place else ()
        ins = ins[len(first) :]
        inside = pl.BlockSpec(memory_space=pltpu.VMEM)
        small = len(outs) - n_out
        return pl.pallas_call(
            lambda *refs: body(
                *(ask() for ask in first), *refs[: len(ins)], *refs[len(ins) + skip :]
            ),
            out_shape=outs,
            in_specs=[inside] * len(ins) + [pl.BlockSpec(memory_space=pl.ANY)] * skip,
            out_specs=(inside,) * small + (pl.BlockSpec(memory_space=pl.ANY),) * n_out,
            scratch_shapes=[pltpu.VMEM((rows, cols), BF16)] * n_out
            + [pltpu.SemaphoreType.DMA((n_out, n_seq))],
            compiler_params=pltpu.CompilerParams(vmem_limit_bytes=40 * 2**20),
            cost_estimate=cost_of(micros),
        )(*ins, *after)

    def spread_back(gm, w):
        wide_rows = dot(gm, w, NT)
        return jnp.concatenate([wide_rows[:, j * HD : (j + 1) * HD] for j in range(KS)], axis=0)

    def head_places(mine):
        for r in range(n_seq):
            for i in range(hp):
                h = (mine ^ r) * hp + i
                narrow = slice(i * HD, (i + 1) * HD)
                yield r, i, h, narrow, pl.ds(pl.multiple_of(h * HD, HD), HD)

    def back_keys_body(ids_ref, gk_ref, kp_ref, wk_ref, kg_ref, dq_ref, *rest):
        gm = rest[:n_seq]
        gkn_ref, dots_ref = rest[n_seq:]
        total = jnp.zeros((rows, HD), F32)
        for r, i, h, narrow, at in head_places(ids_ref[0]):
            gkn = gk_ref[:, at] + spread_back(gm[r][0, :, narrow], wk_ref[h])
            gkn_ref[:, at] = gkn
            total = total + gkn * kp_ref[:, at].astype(F32) * kg_ref[:, at]
        dots_ref[0:1, :] = dq_ref[...]
        dots_ref[1:2, :] = lane_sum_row(total)

    gkn, dots = whole_call(
        back_keys_body,
        (wide_f32, two_rows),
        place, gk_local, kp, key_squeeze, kg, dot_q, slot_grads[0], *slots_recv,
        micros=2.0,
        after=(chunk,),
    )

    def back_values_body(ids_ref, gv_ref, wv_ref, *rest):
        gm = rest[:n_seq]
        mark_ref, value_ref, buffer, sems = rest[n_seq:]
        mark_ref[...] = jnp.zeros_like(mark_ref)
        unorder = row_order_back(rows)
        copies = []
        for r, i, h, narrow, at in head_places(ids_ref[0]):
            value = gv_ref[:, at] + spread_back(gm[r][1, :, narrow], wv_ref[h])
            buffer[:, at] = dot(unorder, value.astype(BF16)).astype(BF16)
            if i == hp - 1:
                block = ids_ref[0] ^ r
                wide_at = pl.ds(pl.multiple_of(block * wide, wide), wide)
                copies.append(send_out(buffer, value_ref, sems.at[0], r, wide_at))
        for copy in copies:
            copy.wait()

    mark, grad_value = column_out(
        back_values_body,
        (sds((8, HD), F32), rows_shape),
        1,
        place, gv_local, value_squeeze, slot_grads[0], *slots_recv,
        micros=2.0,
        after=(dots,),
    )
    dots_parts = over_heads(dots, beside=(mark,))

    kernel_out = sds((heads, KS * HD, HD), F32)
    gains_shape = sds((1, cols), F32)

    def write_chunk(mine, r, read, buffer, sem, target):
        start = (mine ^ r) * hp
        for i in range(hp):
            buffer[start + i] = read(slice(i * KS * HD, (i + 1) * KS * HD)).astype(F32)
        at = pl.ds(start, hp)
        copy = pltpu.make_async_copy(buffer.at[at], target.at[at], sem)
        copy.start()
        return copy

    def own_chunk_body(ids_ref, same, other, *rest):
        mark_ref, gks_ref, gvs_ref, buffer_k, buffer_v, sems = rest
        mark_ref[...] = jnp.zeros_like(mark_ref)
        first = ids_ref[1] == 0
        copies = [
            write_chunk(
                ids_ref[0], 0, lambda at: jnp.where(first, same[at, :], other[at, :]),
                buffer_k, sems.at[0], gks_ref,
            ),
            write_chunk(
                ids_ref[0], 0, lambda at: jnp.where(first, other[at, :], same[at, :]),
                buffer_v, sems.at[1], gvs_ref,
            ),
        ]
        for copy in copies:
            copy.wait()

    inside = pl.BlockSpec(memory_space=pltpu.VMEM)
    outside = pl.BlockSpec(memory_space=pl.ANY)
    buffer = pltpu.VMEM(kernel_out.shape, F32)
    params = pltpu.CompilerParams(vmem_limit_bytes=40 * 2**20)
    own_mark, *part_written = pl.pallas_call(
        lambda *refs: own_chunk_body(place(), *refs),
        out_shape=(sds((8, HD), F32), kernel_out, kernel_out),
        in_specs=[inside, inside],
        out_specs=(inside, outside, outside),
        scratch_shapes=[buffer, buffer, pltpu.SemaphoreType.DMA((2,))],
        compiler_params=params,
        cost_estimate=cost_of(0.01),
    )(chunk, chunk_other)

    def norms_body(q_ref, kp_ref, gq_ref, gkn_ref, qg_ref, kg_ref, inv_ref, *rest):
        dots_a, dots_b, mark_ref, out_q, out_k, buffer_q, buffer_k, sems = rest
        mark_ref[...] = jnp.zeros_like(mark_ref)
        total = dots_a[...] + dots_b[...]
        inv_rows = inv_ref[...]
        inv_c = as_columns(inv_rows)
        pull = as_columns(inv_rows * inv_rows * inv_rows * total / full_width)
        unorder = row_order_back(rows)
        copies = []
        for r in range(n_seq):
            at = slice(r * wide, (r + 1) * wide)
            buffer_q[:, at] = (
                inv_c[:, 0:1] * qg_ref[:, at] * gq_ref[:, at]
                - q_ref[:, at].astype(F32) * pull[:, 0:1]
            ).astype(BF16)
            copies.append(send_out(buffer_q, out_q, sems.at[0], r, at))
            grad_k = (
                inv_c[:, 1:2] * kg_ref[:, at] * gkn_ref[:, at]
                - kp_ref[:, at].astype(F32) * pull[:, 1:2]
            ).astype(BF16)
            buffer_k[:, at] = dot(unorder, grad_k).astype(BF16)
            copies.append(send_out(buffer_k, out_k, sems.at[1], r, at))
        for copy in copies:
            copy.wait()

    norms_mark, grad_query, grad_key = column_out(
        norms_body,
        (sds((8, HD), F32), rows_shape, rows_shape),
        2,
        q, kp, gq, gkn, qg, kg, inv, *dots_parts,
        micros=0.01,
        after=(own_mark,),
    )

    def pack_body(*refs):
        for r in range(n_seq - 1):
            refs[n_seq - 1][r] = refs[r][...]

    packed_shape = sds((n_seq - 1,) + chunk_shape.shape, BF16)
    packed = whole_call(pack_body, packed_shape, *chunks, micros=0.1, after=(norms_mark, own_mark))
    packed_other = to_core(packed)

    def back_gain(mine, chunk_0, chunks_ref, kg_ref, wk_ref, out_ref):
        sums = []
        for r in range(n_seq):
            for i in range(hp):
                h = (mine ^ r) * hp + i
                total = jnp.zeros((HD, HD), F32)
                for j in range(KS):
                    span = slice((i * KS + j) * HD, (i * KS + j + 1) * HD)
                    grad_w = chunk_0[span, :] if r == 0 else chunks_ref[r - 1, span, :]
                    kernel = wk_ref[h, j * HD : (j + 1) * HD, :]
                    total = total + grad_w.astype(F32) * kernel.astype(F32)
                sums.append(total)
        sums = jnp.concatenate(sums, axis=0)
        high = sums.astype(BF16)
        low = (sums - high.astype(F32)).astype(BF16)
        ones = jnp.ones((16, HD), BF16)
        row = (dot(ones, high, NT) + dot(ones, low, NT))[0:1]
        for r in range(n_seq):
            at = pl.ds(pl.multiple_of((mine ^ r) * wide, wide), wide)
            out_ref[:, at] = row[:, r * wide : (r + 1) * wide] / kg_ref[:, at]

    def write_chunks(mine, chunks_ref, buffer, sems, target):
        return [
            write_chunk(
                mine, r, lambda at, r=r: chunks_ref[r - 1, at, :], buffer, sems.at[r], target
            )
            for r in peers
        ]

    def this_core_body(ids_ref, same_0, same, kg_ref, wk_ref, gks_in, gvs_in, *rest):
        back_ref, gks_ref, gvs_ref, buffer, sems = rest

        @pl.when(ids_ref[1] == 0)
        def _():
            copies = write_chunks(ids_ref[0], same, buffer, sems, gks_ref)
            back_gain(ids_ref[0], same_0, same, kg_ref, wk_ref, back_ref)
            for copy in copies:
                copy.wait()

        @pl.when(ids_ref[1] == 1)
        def _():
            copies = write_chunks(ids_ref[0], same, buffer, sems, gvs_ref)
            back_ref[...] = jnp.zeros_like(back_ref)
            for copy in copies:
                copy.wait()

    def other_core_body(ids_ref, same_0, other_0, same, other, back, kg_ref, wk_ref, *rest):
        gks_ref, gvs_ref, gq_out, gk_out, buffer, gq_row, gk_row, sems = rest[2:]

        def finish(copies):
            total = same_0[span_rows:, :].astype(F32) + other_0[span_rows:, :].astype(F32)
            for r in range(n_seq - 1):
                total = total + same[r, span_rows:, :].astype(F32)
                total = total + other[r, span_rows:, :].astype(F32)
            as_row = lambda x: jnp.concatenate([x[h : h + 1] for h in range(heads)], axis=1)
            gq_row[...] = as_row(total[:heads])
            gk_row[...] += as_row(total[heads:])
            copies.append(pltpu.make_async_copy(gq_row, gq_out, sems.at[0]))
            copies[-1].start()
            copies.append(pltpu.make_async_copy(gk_row, gk_out, sems.at[n_seq]))
            copies[-1].start()
            for copy in copies:
                copy.wait()

        @pl.when(ids_ref[1] == 0)
        def _():
            copies = write_chunks(ids_ref[0], other, buffer, sems, gvs_ref)
            gk_row[...] = back[...]
            finish(copies)

        @pl.when(ids_ref[1] == 1)
        def _():
            copies = write_chunks(ids_ref[0], other, buffer, sems, gks_ref)
            back_gain(ids_ref[0], other_0, other, kg_ref, wk_ref, gk_row)
            finish(copies)

    back_row, *part_written = pl.pallas_call(
        lambda *refs: this_core_body(place(), *refs),
        out_shape=(gains_shape, kernel_out, kernel_out),
        in_specs=[inside] * 4 + [outside] * 2,
        out_specs=(inside, outside, outside),
        input_output_aliases={4: 1, 5: 2},
        scratch_shapes=[buffer, pltpu.SemaphoreType.DMA((n_seq,))],
        compiler_params=params,
        cost_estimate=cost_of(1.6),
    )(chunk, packed, kg, key_squeeze, *part_written)
    gks, gvs, gain_q_all, gain_k_all = pl.pallas_call(
        lambda *refs: other_core_body(place(), *refs),
        out_shape=(kernel_out, kernel_out, gains_shape, gains_shape),
        in_specs=[inside] * 7 + [outside] * 2,
        out_specs=(outside,) * 4,
        input_output_aliases={7: 0, 8: 1},
        scratch_shapes=[
            buffer,
            pltpu.VMEM((1, cols), F32),
            pltpu.VMEM((1, cols), F32),
            pltpu.SemaphoreType.DMA((n_seq + 1,)),
        ],
        compiler_params=params,
        cost_estimate=cost_of(2.2),
    )(chunk, chunk_other, packed, packed_other, back_row, kg, key_squeeze, *part_written)
    return (
        grad_query[None],
        grad_key[None],
        grad_value[None],
        gain_q_all.reshape(cols),
        gain_k_all.reshape(cols),
        gks,
        gvs,
    )


def solution(mesh):
    placed = (
        P("dp", "seq", "head"),
        P("dp", "seq", "head"),
        P("dp", "seq", "head"),
        P("head"),
        P("head"),
        P("head", None, None),
        P("head", None, None),
        P("dp", "seq", "head"),
    )
    return jax.shard_map(
        on_device,
        mesh=mesh,
        in_specs=placed,
        out_specs=(
            P("dp", "seq", "head"),
            P("dp", "seq", "head"),
            P("dp", "seq", "head"),
            P("head"),
            P("head"),
            P("head", None, None),
            P("head", None, None),
        ),
        check_vma=False,
    )
```

```python
import jax
import jax.numpy as jnp
from jax import lax
from jax.experimental import pallas as pl
from jax.experimental.pallas import tpu as pltpu
from jax.sharding import PartitionSpec as P

HD = 128
KS = 4
HH = 4096


epsilon = 1e-06


def unfold_slots(source, head_count):
    batch_size, row_count, widths = source.shape
    return (
        source.reshape(batch_size, row_count // KS, KS, head_count, HD)
        .transpose(0, 1, 3, 2, 4)
        .reshape(batch_size, row_count // KS, head_count, KS * HD)
    )


def fold_slots(source):
    batch_size, slot_count, head_count, spans = source.shape
    return (
        source.reshape(batch_size, slot_count, head_count, KS, HD)
        .transpose(0, 1, 3, 2, 4)
        .reshape(batch_size, slot_count * KS, head_count * HD)
    )


def on_device_any(
    query_heads, key_heads, value_heads, query_gain, key_gain, key_squeeze, value_squeeze, grad_out
):
    batch_size, row_count, widths = query_heads.shape
    head_count = widths // HD
    slot_count = row_count // KS
    score_scale = HD ** (-0.5)
    own_limit = lax.axis_index("seq") * slot_count
    q_full = query_heads.astype(jnp.float32)
    k_full = key_heads.astype(jnp.float32)
    sum_q, sum_k = lax.psum((jnp.sum(q_full * q_full, -1), jnp.sum(k_full * k_full, -1)), "head")
    inv_q = lax.rsqrt(sum_q / HH + epsilon)[..., None]
    inv_k = lax.rsqrt(sum_k / HH + epsilon)[..., None]
    q_norm = (q_full * inv_q * query_gain).astype(jnp.bfloat16)
    k_norm = (k_full * inv_k * key_gain).astype(jnp.bfloat16)
    k_unf = unfold_slots(k_norm, head_count)
    v_unf = unfold_slots(value_heads, head_count)
    mem_k = (
        jnp.einsum("bmhc,hcd->bmhd", k_unf, key_squeeze, preferred_element_type=jnp.float32)
        .astype(jnp.bfloat16)
        .reshape(batch_size, slot_count, widths)
    )
    mem_v = (
        jnp.einsum("bmhc,hcd->bmhd", v_unf, value_squeeze, preferred_element_type=jnp.float32)
        .astype(jnp.bfloat16)
        .reshape(batch_size, slot_count, widths)
    )
    queries = q_norm.reshape(batch_size, row_count, head_count, HD)
    key_loc = k_norm.reshape(batch_size, row_count, head_count, HD)
    value_loc = value_heads.reshape(batch_size, row_count, head_count, HD)
    cotangent = grad_out.reshape(batch_size, row_count, head_count, HD)
    positions = jnp.arange(row_count)
    causal = positions[:, None] >= positions[None, :]
    scores_loc = jnp.where(
        causal,
        jnp.einsum("bthd,buhd->bhtu", queries, key_loc, preferred_element_type=jnp.float32)
        * score_scale,
        -jnp.inf,
    )
    grads_loc = jnp.einsum(
        "bthd,buhd->bhtu", cotangent, value_loc, preferred_element_type=jnp.float32
    )
    all_k, all_v = (
        lax.all_gather(mem_k, "seq", axis=1, tiled=True),
        lax.all_gather(mem_v, "seq", axis=1, tiled=True),
    )
    piece_rows = all_k.shape[1]
    key_rows = all_k.reshape(batch_size, piece_rows, head_count, HD)
    value_rows = all_v.reshape(batch_size, piece_rows, head_count, HD)
    allowed = jnp.arange(piece_rows) < own_limit
    scores = jnp.where(
        allowed,
        jnp.einsum("bthd,buhd->bhtu", queries, key_rows, preferred_element_type=jnp.float32)
        * score_scale,
        -jnp.inf,
    )
    gradients = jnp.einsum(
        "bthd,buhd->bhtu", cotangent, value_rows, preferred_element_type=jnp.float32
    )
    key_rows, scores_mem, grads_mem = (key_rows, scores, gradients)
    peak = jnp.maximum(jnp.max(scores_loc, -1), jnp.max(scores_mem, -1))
    summed = jnp.sum(jnp.exp(scores_loc - peak[..., None]), -1) + jnp.sum(
        jnp.exp(scores_mem - peak[..., None]), -1
    )
    log_mass = peak + jnp.log(summed)
    row_delta = jnp.sum(jnp.exp(scores_loc - log_mass[..., None]) * grads_loc, -1) + jnp.sum(
        jnp.exp(scores_mem - log_mass[..., None]) * grads_mem, -1
    )
    piece_rows = key_rows.shape[1]
    attend = jnp.exp(scores_mem - log_mass[..., None])
    d_scores = (attend * (grads_mem - row_delta[..., None])).astype(jnp.bfloat16)
    grad_q = score_scale * jnp.einsum(
        "bhtu,buhd->bthd", d_scores, key_rows, preferred_element_type=jnp.float32
    )
    grad_k = score_scale * jnp.einsum(
        "bhtu,bthd->buhd", d_scores, queries, preferred_element_type=jnp.float32
    )
    grad_v = jnp.einsum(
        "bhtu,bthd->buhd",
        attend.astype(jnp.bfloat16),
        cotangent,
        preferred_element_type=jnp.float32,
    )
    stacked = jnp.stack(
        (
            grad_k.reshape(batch_size, piece_rows, widths),
            grad_v.reshape(batch_size, piece_rows, widths),
        )
    )
    attend_loc = jnp.exp(scores_loc - log_mass[..., None])
    d_loc = (attend_loc * (grads_loc - row_delta[..., None])).astype(jnp.bfloat16)
    grad_qn = (
        score_scale
        * jnp.einsum("bhtu,buhd->bthd", d_loc, key_loc, preferred_element_type=jnp.float32)
        + grad_q
    ).reshape(batch_size, row_count, widths)
    grad_kn_local = score_scale * jnp.einsum(
        "bhtu,bthd->buhd", d_loc, queries, preferred_element_type=jnp.float32
    )
    grad_v_local = jnp.einsum(
        "bhtu,bthd->buhd",
        attend_loc.astype(jnp.bfloat16),
        cotangent,
        preferred_element_type=jnp.float32,
    )
    mine = lax.psum_scatter(stacked.astype(jnp.bfloat16), "seq", scatter_dimension=2, tiled=True)
    grad_mem_k = mine[0].reshape(batch_size, slot_count, head_count, HD)
    grad_mem_v = mine[1].reshape(batch_size, slot_count, head_count, HD)
    squeeze_k_part = jnp.einsum(
        "bmhc,bmhd->hcd", k_unf, grad_mem_k, preferred_element_type=jnp.float32
    )
    squeeze_v_part = jnp.einsum(
        "bmhc,bmhd->hcd", v_unf, grad_mem_v, preferred_element_type=jnp.float32
    )
    back_k = fold_slots(
        jnp.einsum("bmhd,hcd->bmhc", grad_mem_k, key_squeeze, preferred_element_type=jnp.float32)
    )
    back_v = fold_slots(
        jnp.einsum("bmhd,hcd->bmhc", grad_mem_v, value_squeeze, preferred_element_type=jnp.float32)
    )
    grad_kn = grad_kn_local.reshape(batch_size, row_count, widths) + back_k
    grad_value = (grad_v_local.reshape(batch_size, row_count, widths) + back_v).astype(jnp.bfloat16)
    dot_q, dot_k = lax.psum(
        (jnp.sum(query_gain * grad_qn * q_full, -1), jnp.sum(key_gain * grad_kn * k_full, -1)),
        "head",
    )
    grad_query = (
        inv_q * query_gain * grad_qn - q_full * inv_q**3 * dot_q[..., None] / HH
    ).astype(jnp.bfloat16)
    grad_key = (inv_k * key_gain * grad_kn - k_full * inv_k**3 * dot_k[..., None] / HH).astype(
        jnp.bfloat16
    )
    gain_q_part = jnp.sum(grad_qn * q_full * inv_q, (0, 1))
    gain_k_part = jnp.sum(grad_kn * k_full * inv_k, (0, 1))
    grad_query_gain, grad_key_gain, grad_key_squeeze, grad_value_squeeze = (
        lax.psum(gain_q_part.astype(jnp.bfloat16), ("seq", "dp")).astype(jnp.float32),
        lax.psum(gain_k_part.astype(jnp.bfloat16), ("seq", "dp")).astype(jnp.float32),
        lax.psum(squeeze_k_part.astype(jnp.bfloat16), ("seq", "dp")).astype(jnp.float32),
        lax.psum(squeeze_v_part.astype(jnp.bfloat16), ("seq", "dp")).astype(jnp.float32),
    )
    return (
        grad_query,
        grad_key,
        grad_value,
        grad_query_gain,
        grad_key_gain,
        grad_key_squeeze,
        grad_value_squeeze,
    )


F32 = jnp.float32
BF16 = jnp.bfloat16
NN = (((1,), (0,)), ((), ()))
NT = (((1,), (1,)), ((), ()))
TN = (((0,), (0,)), ((), ()))


def dot(a, b, dims=NN):
    return lax.dot_general(a, b, dims, preferred_element_type=F32)


def sds(shape, dtype):
    return jax.ShapeDtypeStruct(shape, dtype)


def place():
    return lax.axis_index("seq"), lax.axis_index("dp")


def cost_of(micros):
    return pl.CostEstimate(
        flops=int(micros * 1e9), bytes_accessed=int(micros * 3.6e6), transcendentals=0
    )


def whole_call(body, outs, *ins, micros=1.0, after=(), scratch=(), vmem=40, aliases=None):
    first = (place,) if ins[0] is place else ()
    ins = ins[len(first) :]
    n_out = len(jax.tree.leaves(outs))
    skip = len(after)
    space = pl.BlockSpec(memory_space=pltpu.VMEM)
    return pl.pallas_call(
        lambda *refs: body(
            *(ask() for ask in first), *refs[: len(ins)], *refs[len(ins) + skip :]
        ),
        out_shape=outs,
        in_specs=[space] * len(ins) + [pl.BlockSpec(memory_space=pl.ANY)] * skip,
        out_specs=jax.tree.map(lambda _: space, outs),
        scratch_shapes=list(scratch),
        input_output_aliases=aliases or {},
        compiler_params=pltpu.CompilerParams(vmem_limit_bytes=vmem * 2**20),
        cost_estimate=cost_of(micros),
    )(*ins, *after)


def row_order(rows):
    slots = rows // KS
    r = lax.broadcasted_iota(jnp.int32, (rows, rows), 0)
    c = lax.broadcasted_iota(jnp.int32, (rows, rows), 1)
    return jnp.where(c == KS * (r % slots) + r // slots, 1.0, 0.0).astype(BF16)


def row_order_back(rows):
    slots = rows // KS
    r = lax.broadcasted_iota(jnp.int32, (rows, rows), 0)
    c = lax.broadcasted_iota(jnp.int32, (rows, rows), 1)
    return jnp.where(r == KS * (c % slots) + c // slots, 1.0, 0.0).astype(BF16)


def causal_t(rows):
    slots = rows // KS
    u = lax.broadcasted_iota(jnp.int32, (rows, rows), 0)
    t = lax.broadcasted_iota(jnp.int32, (rows, rows), 1)
    return KS * (u % slots) + u // slots <= t


def fold_lanes(x):
    total = x[:, :HD]
    for i in range(1, x.shape[1] // HD):
        total = total + x[:, i * HD : (i + 1) * HD]
    return total


def lane_sum_row(x):
    return jnp.sum(x.T, axis=0, keepdims=True)


def as_columns(rows):
    pad = jnp.zeros((8 - rows.shape[0], rows.shape[1]), F32)
    return jnp.concatenate([rows, pad], axis=0).T


def on_device(
    query_heads, key_heads, value_heads, query_gain, key_gain, key_squeeze, value_squeeze, grad_out
):
    n_seq, n_head = lax.axis_size("seq"), lax.axis_size("head")
    batch_size, rows, cols = query_heads.shape
    heads = cols // HD
    if batch_size != 1 or n_seq & (n_seq - 1) or heads % n_seq or lax.axis_size("dp") != 2:
        return on_device_any(
            query_heads,
            key_heads,
            value_heads,
            query_gain,
            key_gain,
            key_squeeze,
            value_squeeze,
            grad_out,
        )
    slots = rows // KS
    hp = heads // n_seq
    wide = hp * HD
    mem_rows = n_seq * slots
    peers = range(1, n_seq)
    n_mem = (n_seq - 1) * slots
    scale = HD ** (-0.5)
    full_width = cols * n_head

    def to_peers(axis, arrays):
        n = lax.axis_size(axis)
        return [
            lax.ppermute(a, axis, [(i, i ^ k) for i in range(n)])
            for k, a in zip(range(1, n), arrays)
        ]

    def sum_body(a_ref, b_ref, out_ref):
        out_ref[...] = a_ref[...] + b_ref[...]

    def over_heads(a, beside=()):
        step, got = 1, None
        while step < n_head:
            if got is not None:
                a = whole_call(sum_body, sds(a.shape, a.dtype), a, got, micros=0.1, after=beside)
            got = lax.ppermute(a, "head", [(i, i ^ step) for i in range(n_head)])
            step *= 2
        return a, got

    def to_core(a):
        return lax.ppermute(a, "dp", [(0, 1), (1, 0)])

    q = query_heads[0]
    k = key_heads[0]
    v = value_heads[0]
    do = grad_out[0]
    qg = query_gain.reshape(1, cols)
    kg = key_gain.reshape(1, cols)

    def squares_body(q_ref, k_ref, ss_ref):
        qf = q_ref[...].astype(F32)
        ss_ref[0:1, :] = lane_sum_row(fold_lanes(qf * qf))
        kf = k_ref[...].astype(F32)
        ss_ref[1:2, :] = lane_sum_row(fold_lanes(kf * kf))

    two_rows = sds((2, rows), F32)
    ss = whole_call(squares_body, two_rows, q, k, micros=1.5, vmem=62)
    ss_parts = [ss] + to_peers("head", [ss] * (n_head - 1))

    def compress(source, w_ref, out_ref):
        for h in range(heads):
            total = None
            for j in range(KS):
                part = dot(
                    source[j * slots : (j + 1) * slots, h * HD : (h + 1) * HD],
                    w_ref[h, j * HD : (j + 1) * HD, :],
                )
                total = part if total is None else total + part
            block = h // hp
            out_ref[
                block * slots : (block + 1) * slots, (h % hp) * HD : (h % hp + 1) * HD
            ] = total.astype(BF16)

    def pack_slots(mine, mem_ref, sends):
        for k, send in zip(peers, sends):
            for r in peers:
                source = pl.ds(pl.multiple_of((mine ^ k ^ r) * slots, slots), slots)
                send[(r - 1) * slots : r * slots, :] = mem_ref[source, :]

    def values_body(ids_ref, v_ref, w_ref, vp_ref, *rest):
        sends, mem_ref = rest[:-1], rest[-1]
        vp_ref[...] = dot(row_order(rows), v_ref[...]).astype(BF16)
        compress(vp_ref, w_ref, mem_ref)
        pack_slots(ids_ref[0], mem_ref, sends)

    rows_shape = sds((rows, cols), BF16)
    mem_shape = sds((mem_rows, wide), BF16)
    slots_packet = sds((n_mem, wide), BF16)
    mem_scratch = [pltpu.VMEM(mem_shape.shape, BF16)]
    vp, *mv_sends = whole_call(
        values_body,
        (rows_shape,) + (slots_packet,) * (n_seq - 1),
        place, v, value_squeeze,
        scratch=mem_scratch,
        micros=0.8,
    )
    mv_recv = to_peers("seq", mv_sends)

    def keys_body(ids_ref, k_ref, kg_ref, w_ref, *rest):
        ss_refs = rest[:n_head]
        inv_ref, kn_ref = rest[n_head : n_head + 2]
        sends, mem_ref = rest[n_head + 2 : -1], rest[-1]
        total = ss_refs[0][...]
        for other in ss_refs[1:]:
            total = total + other[...]
        natural = as_columns(lax.rsqrt(total / full_width + epsilon))
        order = row_order(rows)
        inv_ref[...] = natural.T[:2]
        normed = (k_ref[...].astype(F32) * natural[:, 1:2] * kg_ref[...]).astype(BF16)
        kn_ref[...] = dot(order, normed).astype(BF16)
        compress(kn_ref, w_ref, mem_ref)
        pack_slots(ids_ref[0], mem_ref, sends)

    scales, kn, *mk_sends = whole_call(
        keys_body,
        (two_rows, rows_shape) + (slots_packet,) * (n_seq - 1),
        place, k, kg, key_squeeze, *ss_parts,
        scratch=mem_scratch,
        micros=20.0,
    )
    mk_recv = to_peers("seq", mk_sends)

    def local_body(q_ref, qg_ref, scale_ref, kn_ref, vp_ref, do_ref, inv_ref, qn_ref, st_ref):
        natural = as_columns(scale_ref[...])
        order = row_order(rows)
        high = natural.astype(BF16)
        rest_1 = natural - high.astype(F32)
        middle = rest_1.astype(BF16)
        low = (rest_1 - middle.astype(F32)).astype(BF16)
        ordered = dot(order, high) + dot(order, middle) + dot(order, low)
        inv_c = jnp.concatenate([natural[:, 0:1], ordered[:, 1:2], natural[:, 2:]], axis=1)
        inv_ref[...] = inv_c.T[:2]
        allowed = causal_t(rows)
        inv_c = inv_c[:, 0:1]
        for h in range(heads):
            at = slice(h * HD, (h + 1) * HD)
            qn_h = (q_ref[:, at].astype(F32) * inv_c * qg_ref[:, at]).astype(BF16)
            qn_ref[:, at] = qn_h
            s = jnp.where(allowed, dot(kn_ref[:, at], qn_h, NT) * scale, -jnp.inf)
            g = dot(vp_ref[:, at], do_ref[:, at], NT)
            m = jnp.max(s, axis=0, keepdims=True)
            p = jnp.exp(s - m)
            st_ref[h, 0:1, :] = m
            st_ref[h, 1:2, :] = jnp.sum(p, axis=0, keepdims=True)
            st_ref[h, 2:3, :] = jnp.sum(p * g, axis=0, keepdims=True)

    stat_shape = sds((heads, 8, rows), F32)
    inv, qn, stats = whole_call(
        local_body, (two_rows, rows_shape, stat_shape), q, qg, scales, kn, vp, do,
        micros=0.5,
        after=tuple(mv_recv),
    )

    def rows_body(ids_ref, kn_ref, vp_ref, k_ref, *outs):
        sends, kp_ref = outs[:-1], outs[-1]
        kp_ref[...] = dot(row_order(rows), k_ref[...]).astype(BF16)
        for r, send in zip(peers, sends):
            dest = ids_ref[0] ^ r
            at = pl.ds(pl.multiple_of(dest * wide, wide), wide)
            send[0] = kn_ref[:, at]
            send[1] = vp_ref[:, at]

    row_pair = sds((2, rows, wide), BF16)
    *row_sends, kp = whole_call(
        rows_body,
        (row_pair,) * (n_seq - 1) + (rows_shape,),
        place, kn, vp, k,
        after=(stats,),
        micros=0.7,
    )
    rows_recv = to_peers("seq", row_sends)

    def memory_head(mine, qn_h, do_h, mk, mv, stat):
        raw = dot(mk, qn_h, NT) * scale
        s = jnp.concatenate(
            [
                jnp.where((mine ^ src) < mine, raw[(src - 1) * slots : src * slots], -jnp.inf)
                for src in peers
            ],
            axis=0,
        )
        g = dot(mv, do_h, NT)
        m_loc, l_loc, d_loc = stat[0:1], stat[1:2], stat[2:3]
        m = jnp.maximum(m_loc, jnp.max(s, axis=0, keepdims=True))
        p = jnp.exp(s - m)
        shrink = jnp.exp(m_loc - m)
        mass = l_loc * shrink + jnp.sum(p, axis=0, keepdims=True)
        inv_mass = 1.0 / mass
        delta = (d_loc * shrink + jnp.sum(p * g, axis=0, keepdims=True)) * inv_mass
        attend = p * inv_mass
        ds = (attend * (g - delta)).astype(BF16)
        gk = (dot(ds, qn_h) * scale).astype(BF16)
        gv = dot(attend.astype(BF16), do_h).astype(BF16)
        return jnp.concatenate([m, inv_mass, delta, stat[3:]], axis=0), ds, gk, gv

    def places(mine, r, i):
        h = (mine ^ r) * hp + i
        return h, pl.ds(pl.multiple_of(h * HD, HD), HD), slice(i * HD, (i + 1) * HD)

    def memory_body(ids_ref, qn_ref, do_ref, st_ref, *rest):
        mk_refs = rest[: n_seq - 1]
        mv_refs = rest[n_seq - 1 : 2 * n_seq - 2]
        st2_ref, ds_ref = rest[2 * n_seq - 2 : 2 * n_seq]
        parts = rest[2 * n_seq :]
        mine = ids_ref[0]
        for r in peers:
            span = slice((r - 1) * slots, r * slots)
            for i in range(hp):
                h, at, narrow = places(mine, r, i)
                mk = jnp.concatenate([ref[span, narrow] for ref in mk_refs], axis=0)
                mv = jnp.concatenate([ref[span, narrow] for ref in mv_refs], axis=0)
                to = (r - 1) * hp + i
                st2_ref[to], ds_ref[to], gk, gv = memory_head(
                    mine, qn_ref[:, at], do_ref[:, at], mk, mv, st_ref[h]
                )
                parts[r - 1][0, :, narrow] = gk
                parts[r - 1][1, :, narrow] = gv

    part = sds((2, n_mem, wide), BF16)
    far_heads = heads - hp
    stats2, ds_mem, *parts = whole_call(
        memory_body,
        (sds((far_heads, 8, rows), F32), sds((far_heads, n_mem, rows), BF16))
        + (part,) * (n_seq - 1),
        place, qn, do, stats, *mk_recv, *mv_recv,
        micros=2.0,
    )
    parts_recv = to_peers("seq", parts)

    def grads_head(refs, h, at, stat, ds_m, mk, allowed, inv_c):
        q_ref, kp_ref, qn_ref, kn_ref, vp_ref, do_ref, qg_ref = refs[:7]
        gq_ref, gk_ref, gv_ref, gain_q_ref, gain_k_ref = refs[7:]
        qn_h, kn_h, do_h = qn_ref[:, at], kn_ref[:, at], do_ref[:, at]
        s = jnp.where(allowed, dot(kn_h, qn_h, NT) * scale, -jnp.inf)
        g = dot(vp_ref[:, at], do_h, NT)
        m, inv_mass, delta = stat[0:1], stat[1:2], stat[2:3]
        attend = jnp.exp(s - m) * inv_mass
        ds = (attend * (g - delta)).astype(BF16)
        gq = scale * (dot(ds, kn_h, TN) + dot(ds_m, mk, TN))
        gk = scale * dot(ds, qn_h)
        gq_ref[:, at] = gq
        gk_ref[:, at] = gk
        gv_ref[:, at] = dot(attend.astype(BF16), do_h)
        gq_q = gq * q_ref[:, at].astype(F32)
        gk_k = gk * kp_ref[:, at].astype(F32)
        to = pl.ds(h, 1)
        gain_q_ref[to, :] = jnp.sum(gq_q * inv_c[:, 0:1], axis=0, keepdims=True)
        gain_k_ref[to, :] = jnp.sum(gk_k * inv_c[:, 1:2], axis=0, keepdims=True)
        return gq_q * qg_ref[:, at]

    def grads_body(ids_ref, q_ref, kp_ref, qn_ref, kn_ref, vp_ref, do_ref, inv_ref, qg_ref, *rest):
        st_ref, ds_ref = rest[:2]
        mk_refs = rest[2 : n_seq + 1]
        outs, dq_ref = rest[n_seq + 1 : -1], rest[-1]
        refs = (q_ref, kp_ref, qn_ref, kn_ref, vp_ref, do_ref, qg_ref) + tuple(outs)
        allowed = causal_t(rows)
        inv_c = as_columns(inv_ref[...])
        total = jnp.zeros((rows, HD), F32)
        for r in peers:
            span = slice((r - 1) * slots, r * slots)
            for i in range(hp):
                h, at, narrow = places(ids_ref[0], r, i)
                mk = jnp.concatenate([ref[span, narrow] for ref in mk_refs], axis=0)
                to = (r - 1) * hp + i
                total = total + grads_head(
                    refs, h, at, st_ref[to], ds_ref[to], mk, allowed, inv_c
                )
        dq_ref[...] = total

    gain_rows = sds((heads, HD), F32)
    wide_f32 = sds((rows, cols), F32)
    narrow_f32 = sds((rows, HD), F32)
    dot_row = sds((1, rows), F32)
    far_grads = whole_call(
        grads_body,
        (wide_f32, wide_f32, wide_f32, gain_rows, gain_rows, narrow_f32),
        place, q, kp, qn, kn, vp, do, inv, qg, stats2, ds_mem, *mk_recv,
        micros=0.5,
    )

    def own_body(ids_ref, q_ref, kp_ref, qn_ref, kn_ref, vp_ref, do_ref, inv_ref, qg_ref, *rest):
        st_ref, wk_ref, wv_ref = rest[:3]
        row_refs = rest[3 : n_seq + 2]
        dq_in = rest[n_seq + 7]
        outs, (dq_ref, part_ref) = rest[n_seq + 8 : n_seq + 13], rest[n_seq + 13 :]
        refs = (q_ref, kp_ref, qn_ref, kn_ref, vp_ref, do_ref, qg_ref) + tuple(outs)
        allowed = causal_t(rows)
        inv_c = as_columns(inv_ref[...])
        mine = ids_ref[0]
        total = dq_in[...]
        for i in range(hp):
            h, at, narrow = places(mine, 0, i)
            found = []
            for tensor, w_ref in ((0, wk_ref), (1, wv_ref)):
                mem = None
                for j in range(KS):
                    span = slice(j * slots, (j + 1) * slots)
                    rows_j = jnp.concatenate([ref[tensor, span, narrow] for ref in row_refs], axis=0)
                    term = dot(rows_j, w_ref[h, j * HD : (j + 1) * HD, :])
                    mem = term if mem is None else mem + term
                found.append(mem.astype(BF16))
            stat, ds_m, gk, gv = memory_head(
                mine, qn_ref[:, at], do_ref[:, at], found[0], found[1], st_ref[h]
            )
            part_ref[0, :, narrow] = gk
            part_ref[1, :, narrow] = gv
            total = total + grads_head(refs, h, at, stat, ds_m, found[0], allowed, inv_c)
        dq_ref[...] = lane_sum_row(total)

    first_alias = 8 + 3 + n_seq - 1
    gq, gk_local, gv_local, gain_q, gain_k, dot_q, own_part = whole_call(
        own_body,
        (wide_f32, wide_f32, wide_f32, gain_rows, gain_rows, dot_row, part),
        place, q, kp, qn, kn, vp, do, inv, qg, stats, key_squeeze, value_squeeze, *rows_recv,
        *far_grads,
        aliases={first_alias + n: n for n in range(5)},
        micros=0.3,
    )

    def slots_body(*refs):
        ins, outs = refs[:n_seq], refs[n_seq:]
        for r in range(n_seq):
            for tensor in range(2):
                total = None
                for src in range(n_seq):
                    if src == r:
                        continue
                    block = (src ^ r) - 1
                    term = ins[src][tensor, block * slots : (block + 1) * slots, :].astype(F32)
                    total = term if total is None else total + term
                outs[r][tensor] = total.astype(BF16)

    slot_grad = sds((2, slots, wide), BF16)
    slot_grads = whole_call(
        slots_body, (slot_grad,) * n_seq, own_part, *parts_recv, after=(gain_q,), micros=0.3
    )

    slots_recv = to_peers("seq", slot_grads[1:])

    def weights_body(ids_ref, kn_ref, vp_ref, *rest):
        gm = rest[:n_seq]
        row_refs = rest[n_seq : 2 * n_seq - 1]
        same_ref, other_ref = rest[2 * n_seq - 1 :]
        here = pl.ds(pl.multiple_of(ids_ref[0] * wide, wide), wide)
        own = (kn_ref[:, here], vp_ref[:, here])
        first = ids_ref[1] == 0
        for i in range(hp):
            at = slice(i * HD, (i + 1) * HD)
            for j in range(KS):
                span = slice(j * slots, (j + 1) * slots)
                found = []
                for tensor in range(2):
                    lhs = jnp.concatenate(
                        [own[tensor][span, at]] + [ref[tensor, span, at] for ref in row_refs],
                        axis=0,
                    )
                    rhs = jnp.concatenate([ref[tensor, :, at] for ref in gm], axis=0)
                    found.append(dot(lhs, rhs, TN))
                to = slice((i * KS + j) * HD, (i * KS + j + 1) * HD)
                same_ref[to, :] = jnp.where(first, found[0], found[1])
                other_ref[to, :] = jnp.where(first, found[1], found[0]).astype(BF16)

    span_rows = hp * KS * HD
    w_same, w_other = whole_call(
        weights_body,
        (sds((span_rows, HD), F32), sds((span_rows, HD), BF16)),
        place, kn, vp, *slot_grads, *rows_recv,
        micros=1.1,
    )
    w_recv = to_core(w_other)

    def chunk_body(a_ref, b_ref, gq_ref, gk_ref, out_ref):
        out_ref[:span_rows, :] = (a_ref[...] + b_ref[...].astype(F32)).astype(BF16)
        gains = jnp.concatenate([gq_ref[...], gk_ref[...]], axis=0)
        out_ref[span_rows:, :] = gains.astype(BF16)

    chunk_shape = sds((span_rows + 2 * heads, HD), BF16)
    chunk = whole_call(chunk_body, chunk_shape, w_same, w_recv, gain_q, gain_k, micros=0.3, after=(slots_recv[1],))
    chunks = to_peers("seq", [chunk] * (n_seq - 1))
    chunk_other = to_core(chunk)

    def send_out(buffer, target, sems, index, at):
        copy = pltpu.make_async_copy(buffer.at[:, at], target.at[:, at], sems.at[index])
        copy.start()
        return copy

    def column_out(body, outs, n_out, *ins, micros, after=()):
        skip = len(after)
        first = (place,) if ins[0] is place else ()
        ins = ins[len(first) :]
        inside = pl.BlockSpec(memory_space=pltpu.VMEM)
        small = len(outs) - n_out
        return pl.pallas_call(
            lambda *refs: body(
                *(ask() for ask in first), *refs[: len(ins)], *refs[len(ins) + skip :]
            ),
            out_shape=outs,
            in_specs=[inside] * len(ins) + [pl.BlockSpec(memory_space=pl.ANY)] * skip,
            out_specs=(inside,) * small + (pl.BlockSpec(memory_space=pl.ANY),) * n_out,
            scratch_shapes=[pltpu.VMEM((rows, cols), BF16)] * n_out
            + [pltpu.SemaphoreType.DMA((n_out, n_seq))],
            compiler_params=pltpu.CompilerParams(vmem_limit_bytes=40 * 2**20),
            cost_estimate=cost_of(micros),
        )(*ins, *after)

    def spread_back(gm, w):
        wide_rows = dot(gm, w, NT)
        return jnp.concatenate([wide_rows[:, j * HD : (j + 1) * HD] for j in range(KS)], axis=0)

    def head_places(mine):
        for r in range(n_seq):
            for i in range(hp):
                h = (mine ^ r) * hp + i
                narrow = slice(i * HD, (i + 1) * HD)
                yield r, i, h, narrow, pl.ds(pl.multiple_of(h * HD, HD), HD)

    def back_keys_body(ids_ref, gk_ref, kp_ref, wk_ref, kg_ref, dq_ref, *rest):
        gm = rest[:n_seq]
        gkn_ref, dots_ref = rest[n_seq:]
        total = jnp.zeros((rows, HD), F32)
        for r, i, h, narrow, at in head_places(ids_ref[0]):
            gkn = gk_ref[:, at] + spread_back(gm[r][0, :, narrow], wk_ref[h])
            gkn_ref[:, at] = gkn
            total = total + gkn * kp_ref[:, at].astype(F32) * kg_ref[:, at]
        dots_ref[0:1, :] = dq_ref[...]
        dots_ref[1:2, :] = lane_sum_row(total)

    gkn, dots = whole_call(
        back_keys_body,
        (wide_f32, two_rows),
        place, gk_local, kp, key_squeeze, kg, dot_q, slot_grads[0], *slots_recv,
        micros=2.0,
        after=(chunk,),
    )

    def back_values_body(ids_ref, gv_ref, wv_ref, *rest):
        gm = rest[:n_seq]
        mark_ref, value_ref, buffer, sems = rest[n_seq:]
        mark_ref[...] = jnp.zeros_like(mark_ref)
        unorder = row_order_back(rows)
        copies = []
        for r, i, h, narrow, at in head_places(ids_ref[0]):
            value = gv_ref[:, at] + spread_back(gm[r][1, :, narrow], wv_ref[h])
            buffer[:, at] = dot(unorder, value.astype(BF16)).astype(BF16)
            if i == hp - 1:
                block = ids_ref[0] ^ r
                wide_at = pl.ds(pl.multiple_of(block * wide, wide), wide)
                copies.append(send_out(buffer, value_ref, sems.at[0], r, wide_at))
        for copy in copies:
            copy.wait()

    mark, grad_value = column_out(
        back_values_body,
        (sds((8, HD), F32), rows_shape),
        1,
        place, gv_local, value_squeeze, slot_grads[0], *slots_recv,
        micros=2.0,
        after=(dots,),
    )
    dots_parts = over_heads(dots, beside=(mark,))

    kernel_out = sds((heads, KS * HD, HD), F32)
    gains_shape = sds((1, cols), F32)

    def write_chunk(mine, r, read, buffer, sem, target):
        start = (mine ^ r) * hp
        for i in range(hp):
            buffer[start + i] = read(slice(i * KS * HD, (i + 1) * KS * HD)).astype(F32)
        at = pl.ds(start, hp)
        copy = pltpu.make_async_copy(buffer.at[at], target.at[at], sem)
        copy.start()
        return copy

    def own_chunk_body(ids_ref, same, other, *rest):
        mark_ref, gks_ref, gvs_ref, buffer_k, buffer_v, sems = rest
        mark_ref[...] = jnp.zeros_like(mark_ref)
        first = ids_ref[1] == 0
        copies = [
            write_chunk(
                ids_ref[0], 0, lambda at: jnp.where(first, same[at, :], other[at, :]),
                buffer_k, sems.at[0], gks_ref,
            ),
            write_chunk(
                ids_ref[0], 0, lambda at: jnp.where(first, other[at, :], same[at, :]),
                buffer_v, sems.at[1], gvs_ref,
            ),
        ]
        for copy in copies:
            copy.wait()

    inside = pl.BlockSpec(memory_space=pltpu.VMEM)
    outside = pl.BlockSpec(memory_space=pl.ANY)
    buffer = pltpu.VMEM(kernel_out.shape, F32)
    params = pltpu.CompilerParams(vmem_limit_bytes=40 * 2**20)
    own_mark, *part_written = pl.pallas_call(
        lambda *refs: own_chunk_body(place(), *refs),
        out_shape=(sds((8, HD), F32), kernel_out, kernel_out),
        in_specs=[inside, inside],
        out_specs=(inside, outside, outside),
        scratch_shapes=[buffer, buffer, pltpu.SemaphoreType.DMA((2,))],
        compiler_params=params,
        cost_estimate=cost_of(0.01),
    )(chunk, chunk_other)

    def norms_body(q_ref, kp_ref, gq_ref, gkn_ref, qg_ref, kg_ref, inv_ref, *rest):
        dots_a, dots_b, mark_ref, out_q, out_k, buffer_q, buffer_k, sems = rest
        mark_ref[...] = jnp.zeros_like(mark_ref)
        total = dots_a[...] + dots_b[...]
        inv_rows = inv_ref[...]
        inv_c = as_columns(inv_rows)
        pull = as_columns(inv_rows * inv_rows * inv_rows * total / full_width)
        unorder = row_order_back(rows)
        copies = []
        for r in range(n_seq):
            at = slice(r * wide, (r + 1) * wide)
            buffer_q[:, at] = (
                inv_c[:, 0:1] * qg_ref[:, at] * gq_ref[:, at]
                - q_ref[:, at].astype(F32) * pull[:, 0:1]
            ).astype(BF16)
            copies.append(send_out(buffer_q, out_q, sems.at[0], r, at))
            grad_k = (
                inv_c[:, 1:2] * kg_ref[:, at] * gkn_ref[:, at]
                - kp_ref[:, at].astype(F32) * pull[:, 1:2]
            ).astype(BF16)
            buffer_k[:, at] = dot(unorder, grad_k).astype(BF16)
            copies.append(send_out(buffer_k, out_k, sems.at[1], r, at))
        for copy in copies:
            copy.wait()

    norms_mark, grad_query, grad_key = column_out(
        norms_body,
        (sds((8, HD), F32), rows_shape, rows_shape),
        2,
        q, kp, gq, gkn, qg, kg, inv, *dots_parts,
        micros=0.01,
        after=(own_mark,),
    )

    def pack_body(*refs):
        for r in range(n_seq - 1):
            refs[n_seq - 1][r] = refs[r][...]

    packed_shape = sds((n_seq - 1,) + chunk_shape.shape, BF16)
    packed = whole_call(pack_body, packed_shape, *chunks, micros=0.1, after=(norms_mark, own_mark))
    packed_other = to_core(packed)

    def back_gain(mine, chunk_0, chunks_ref, kg_ref, wk_ref, out_ref):
        sums = []
        for r in range(n_seq):
            for i in range(hp):
                h = (mine ^ r) * hp + i
                total = jnp.zeros((HD, HD), F32)
                for j in range(KS):
                    span = slice((i * KS + j) * HD, (i * KS + j + 1) * HD)
                    grad_w = chunk_0[span, :] if r == 0 else chunks_ref[r - 1, span, :]
                    kernel = wk_ref[h, j * HD : (j + 1) * HD, :]
                    total = total + grad_w.astype(F32) * kernel.astype(F32)
                sums.append(total)
        sums = jnp.concatenate(sums, axis=0)
        high = sums.astype(BF16)
        low = (sums - high.astype(F32)).astype(BF16)
        ones = jnp.ones((16, HD), BF16)
        row = (dot(ones, high, NT) + dot(ones, low, NT))[0:1]
        for r in range(n_seq):
            at = pl.ds(pl.multiple_of((mine ^ r) * wide, wide), wide)
            out_ref[:, at] = row[:, r * wide : (r + 1) * wide] / kg_ref[:, at]

    def write_chunks(mine, chunks_ref, buffer, sems, target):
        return [
            write_chunk(
                mine, r, lambda at, r=r: chunks_ref[r - 1, at, :], buffer, sems.at[r], target
            )
            for r in peers
        ]

    def this_core_body(ids_ref, same_0, same, kg_ref, wk_ref, gks_in, gvs_in, *rest):
        back_ref, gks_ref, gvs_ref, buffer, sems = rest

        @pl.when(ids_ref[1] == 0)
        def _():
            copies = write_chunks(ids_ref[0], same, buffer, sems, gks_ref)
            back_gain(ids_ref[0], same_0, same, kg_ref, wk_ref, back_ref)
            for copy in copies:
                copy.wait()

        @pl.when(ids_ref[1] == 1)
        def _():
            copies = write_chunks(ids_ref[0], same, buffer, sems, gvs_ref)
            back_ref[...] = jnp.zeros_like(back_ref)
            for copy in copies:
                copy.wait()

    def other_core_body(ids_ref, same_0, other_0, same, other, back, kg_ref, wk_ref, *rest):
        gks_ref, gvs_ref, gq_out, gk_out, buffer, gq_row, gk_row, sems = rest[2:]

        def finish(copies):
            total = same_0[span_rows:, :].astype(F32) + other_0[span_rows:, :].astype(F32)
            for r in range(n_seq - 1):
                total = total + same[r, span_rows:, :].astype(F32)
                total = total + other[r, span_rows:, :].astype(F32)
            as_row = lambda x: jnp.concatenate([x[h : h + 1] for h in range(heads)], axis=1)
            gq_row[...] = as_row(total[:heads])
            gk_row[...] += as_row(total[heads:])
            copies.append(pltpu.make_async_copy(gq_row, gq_out, sems.at[0]))
            copies[-1].start()
            copies.append(pltpu.make_async_copy(gk_row, gk_out, sems.at[n_seq]))
            copies[-1].start()
            for copy in copies:
                copy.wait()

        @pl.when(ids_ref[1] == 0)
        def _():
            copies = write_chunks(ids_ref[0], other, buffer, sems, gvs_ref)
            gk_row[...] = back[...]
            finish(copies)

        @pl.when(ids_ref[1] == 1)
        def _():
            copies = write_chunks(ids_ref[0], other, buffer, sems, gks_ref)
            back_gain(ids_ref[0], other_0, other, kg_ref, wk_ref, gk_row)
            finish(copies)

    back_row, *part_written = pl.pallas_call(
        lambda *refs: this_core_body(place(), *refs),
        out_shape=(gains_shape, kernel_out, kernel_out),
        in_specs=[inside] * 4 + [outside] * 2,
        out_specs=(inside, outside, outside),
        input_output_aliases={4: 1, 5: 2},
        scratch_shapes=[buffer, pltpu.SemaphoreType.DMA((n_seq,))],
        compiler_params=params,
        cost_estimate=cost_of(1.6),
    )(chunk, packed, kg, key_squeeze, *part_written)
    gks, gvs, gain_q_all, gain_k_all = pl.pallas_call(
        lambda *refs: other_core_body(place(), *refs),
        out_shape=(kernel_out, kernel_out, gains_shape, gains_shape),
        in_specs=[inside] * 7 + [outside] * 2,
        out_specs=(outside,) * 4,
        input_output_aliases={7: 0, 8: 1},
        scratch_shapes=[
            buffer,
            pltpu.VMEM((1, cols), F32),
            pltpu.VMEM((1, cols), F32),
            pltpu.SemaphoreType.DMA((n_seq + 1,)),
        ],
        compiler_params=params,
        cost_estimate=cost_of(2.2),
    )(chunk, chunk_other, packed, packed_other, back_row, kg, key_squeeze, *part_written)
    return (
        grad_query[None],
        grad_key[None],
        grad_value[None],
        gain_q_all.reshape(cols),
        gain_k_all.reshape(cols),
        gks,
        gvs,
    )


def solution(mesh):
    placed = (
        P("dp", "seq", "head"),
        P("dp", "seq", "head"),
        P("dp", "seq", "head"),
        P("head"),
        P("head"),
        P("head", None, None),
        P("head", None, None),
        P("dp", "seq", "head"),
    )
    return jax.shard_map(
        on_device,
        mesh=mesh,
        in_specs=placed,
        out_specs=(
            P("dp", "seq", "head"),
            P("dp", "seq", "head"),
            P("dp", "seq", "head"),
            P("head"),
            P("head"),
            P("head", None, None),
            P("head", None, None),
        ),
        check_vma=False,
    )
```
